32 devices in a mesh: seq: 8 (over z, core), dp: 4 (over y, x).
Axes of the slice: x: 2, y: 2, z: 4, core: 2. Of those that a mesh axis runs over, the one named last changes fastest.
Arguments:
- queries: bfloat16 [4, 1024, 1280], P('dp', 'seq'), may hold values from -43 to 43
- key_rows: bfloat16 [4, 1024, 1280], P('dp', 'seq'), may hold values from -7 to 7
- value_rows: bfloat16 [4, 1024, 1280], P('dp', 'seq'), may hold values from -6 to 6
- resid_in: bfloat16 [4, 1024, 1280], P('dp', 'seq'), may hold values from -6 to 6
- llm_grad: bfloat16 [4, 1536, 1280], P('dp', 'seq'), may hold values from -6 to 6
- vision_slot: int32 [4, 1536], P('dp', 'seq'), may hold values from -1 to 1023, as said below
- window_mask: int32 [4, 16, 2], P('dp', 'seq'), may hold values from 0 to 1, as said below
- w_up: bfloat16 [1280, 2560], P('dp'), may hold values from -0.15625 to 0.15625
- w_down: bfloat16 [2560, 1280], P('dp'), may hold values from -0.125 to 0.125
- norm_gain: bfloat16 [1280], P('dp'), may hold values from 0.25 to 1.75
Outputs:
- grad_query: bfloat16 [4, 1024, 1280], P('dp', 'seq')
- grad_key: bfloat16 [4, 1024, 1280], P('dp', 'seq')
- grad_value: bfloat16 [4, 1024, 1280], P('dp', 'seq')
- grad_resid: bfloat16 [4, 1024, 1280], P('dp', 'seq')
- grad_up: bfloat16 [1280, 2560], P('seq', 'dp')
- grad_down: bfloat16 [2560, 1280], P('seq', 'dp')
- grad_gain: float32 [1280], replicated
The draws below stay inside these ranges and needn't reach their ends.
Inputs may be any that keep to these rules, and one draw needn't show every extreme that they name: `vision_slot`: -1 marks a text position; every vision token of a batch stands at exactly one position. Positions come in aligned runs of 16: each run is text or the 16 consecutive vision tokens of one tile, in order. Each language-model shard holds exactly 8 tiles, and at most 32 vision tokens of one owner; in every batch, for every owner, some shard holds exactly 32 of that owner's vision tokens. `window_mask`: each owner's 2 blocks are split into images of one or more consecutive blocks; a block attends to exactly the blocks of its own image, itself included (entry i % 2 of row i is 1).
All inputs are finite; a program needn't handle non-finite values.
Results may differ from the reference program's by a relative error of at most 0.023.
Values may be sent and summed in bfloat16 or wider, within the bound.
No kernel may reach another device: no remote copies, remote signals or barrier semaphores. Data moves between devices by JAX's collectives and lax.ppermute only.
A program may use at most 128 MiB of HBM per device.

```python
import math
import jax
import jax.numpy as jnp
from jax import lax

HEADS = 16
HDIM = 80
D = 1280
FF = 2560
BLK = 64
PIECE = 16
TOK_DEV = 128
NBD = 2
NPIECE = 8
L_DEV = 192
VISION = 1024
LLM_LEN = 1536
BATCHES = 4
N_SEQ = 8


def query_key_pair(key):
    base = jax.random.fold_in(key, 11)
    query_key, other_key = jax.random.split(base)
    shape = (BATCHES, VISION, D)
    query_out = jnp.clip(jax.random.normal(query_key, shape, jnp.float32), -6.0, 6.0)
    key_out = jnp.clip(jax.random.normal(other_key, shape, jnp.float32), -6.0, 6.0)
    return (query_out, key_out)


def draw_queries(key, part):
    return query_key_pair(key)[0].astype(jnp.bfloat16)


def draw_key_rows(key, part):
    return query_key_pair(key)[1].astype(jnp.bfloat16)


def draw_vision_slot(key, part):
    slot_count = L_DEV // PIECE

    def one_batch(batch_key):
        order_key, place_key = jax.random.split(batch_key)
        order = jax.random.permutation(order_key, N_SEQ)
        tile_index = jnp.arange(NPIECE)
        shifts = jnp.where(tile_index == 0, order[0], order[(tile_index - 1) % N_SEQ])
        sender = jnp.arange(N_SEQ)[:, None]
        owner = (sender - shifts[None, :]) % N_SEQ
        first = owner * TOK_DEV + tile_index[None, :] * PIECE
        layout = jax.vmap(lambda one_key: jax.random.permutation(one_key, slot_count))(jax.random.split(place_key, N_SEQ))
        clipped = jnp.minimum(layout, NPIECE - 1)
        starts = jnp.where(layout < NPIECE, jnp.take_along_axis(first, clipped, axis=1), -1)
        offsets = jnp.arange(PIECE)
        values = jnp.where(starts[:, :, None] >= 0, starts[:, :, None] + offsets[None, None, :], -1)
        return values.reshape(N_SEQ * L_DEV).astype(jnp.int32)
    return jax.vmap(one_batch)(jax.random.split(jax.random.fold_in(key, 23), BATCHES))


def draw_window_mask(key, part):
    cut_key = jax.random.fold_in(key, 37)
    cuts = jax.random.randint(cut_key, (BATCHES, N_SEQ, NBD), 0, 2)
    cuts = jnp.where(jnp.arange(NBD)[None, None, :] == 0, 0, cuts)
    image = jnp.cumsum(cuts, axis=2)
    allowed = image[:, :, :, None] == image[:, :, None, :]
    return allowed.astype(jnp.int32).reshape(BATCHES, N_SEQ * NBD, NBD)


def spiked(values, stream_key, source, target, shards_of, factor):
    owner, partner = [(jnp.arange(values.shape[axis_at]) // (values.shape[axis_at] // shards_of)).reshape([-1 if axis == axis_at else 1 for axis in range(values.ndim)]) for axis_at in (source, target)]
    chosen = jax.random.permutation(stream_key, shards_of)[partner]
    strong = (owner == chosen) | (owner == (partner + shards_of // 2) % shards_of)
    return jnp.where(strong, factor * values, values)


def level_of(own_key, dims, shards, least, largest):
    loudness = 1.0
    for dim, shards_of in shards:
        heights = jax.random.uniform(jax.random.fold_in(jax.random.fold_in(own_key, 6), dim), (shards_of,), jnp.float32, least / len(shards), largest / len(shards))
        loudness = loudness * jnp.repeat(jnp.exp(heights), dims[dim] // shards_of).reshape((-1,) + (1,) * (len(dims) - 1 - dim))
    return loudness


def bell_draw(key, dims, spread, limit, shards=(), held_as=jnp.bfloat16):
    values = spread * jax.random.normal(key, dims, jnp.float32)
    if shards:
        values = values * level_of(key, dims, shards, -0.22, 0.18)
    return jnp.clip(values, -limit, limit).astype(held_as)


def gaussian_with(stream_key, extent, width, limit, shards, heavy, kind=jnp.bfloat16):
    result = width * jax.random.normal(stream_key, extent, jnp.float32)
    if shards:
        result = result * level_of(stream_key, extent, shards, -0.22, 0.18)
    return jnp.clip(spiked(result, jax.random.fold_in(stream_key, 3), *heavy), -limit, limit).astype(kind)


def setup_inputs(seed: int = 0) -> dict:
    splits = jax.random.split(jax.random.key(seed), 11)
    return {
        "queries": draw_queries(jax.random.fold_in(splits[10], 71), 0),
        "key_rows": draw_key_rows(jax.random.fold_in(splits[10], 71), 0),
        "value_rows": bell_draw(splits[2], (BATCHES, VISION, D), 1.0, 6.0, ((0, 4), (1, 8))),
        "resid_in": bell_draw(splits[3], (BATCHES, VISION, D), 1.0, 6.0, ((0, 4), (1, 8))),
        "llm_grad": gaussian_with(splits[4], (BATCHES, LLM_LEN, D), 1.0, 6.0, ((0, 4), (1, 8)), (1, 2, 8, 2.0)),
        "vision_slot": draw_vision_slot(jax.random.fold_in(splits[10], 71), 0),
        "window_mask": draw_window_mask(jax.random.fold_in(splits[10], 71), 0),
        "w_up": bell_draw(splits[7], (D, FF), D ** -0.5, 0.15625, ((0, 4),)),
        "w_down": bell_draw(splits[8], (FF, D), FF ** -0.5, 0.125, ((0, 4),)),
        "norm_gain": jnp.clip(1.0 + 0.15 * jax.random.normal(splits[9], (D,), jnp.float32), 0.25, 1.75).astype(jnp.bfloat16),
    }


def rounded(value):
    return lax.optimization_barrier(value.astype(jnp.bfloat16))

def contract(left, right, left_dim, right_dim):
    return lax.dot_general(left, right, (((left_dim,), (right_dim,)), ((), ())), preferred_element_type=jnp.float32)

def owner_pass(query, key_block, value_block, resid, grad_rows, window_mask, up_full, down_full, gain_full):
    tokens = query.shape[0]
    att_scale = 1.0 / math.sqrt(HDIM)
    best = lax.Precision.HIGHEST
    allowed = jnp.repeat(jnp.repeat(window_mask > 0, BLK, axis=0), BLK, axis=1)
    q_heads = query.astype(jnp.float32).reshape(tokens, HEADS, HDIM)
    k_heads = key_block.astype(jnp.float32).reshape(tokens, HEADS, HDIM)
    v_heads = value_block.astype(jnp.float32).reshape(tokens, HEADS, HDIM)
    scores = jnp.einsum('qhd,khd->hqk', q_heads, k_heads, precision=best) * att_scale
    masked = jnp.where(allowed[None], scores, -jnp.inf)
    highest = lax.optimization_barrier(jnp.max(masked, axis=2, keepdims=True))
    exp_terms = jnp.where(allowed[None], jnp.exp(masked - highest), 0.0)
    attn_probs = exp_terms / lax.optimization_barrier(jnp.sum(exp_terms, axis=2, keepdims=True))
    probs_low = rounded(attn_probs)
    attn_heads = rounded(jnp.einsum('hqk,khd->qhd', probs_low.astype(jnp.float32), v_heads, precision=best))
    attn_out = attn_heads.reshape(tokens, HEADS * HDIM)
    hidden = resid.astype(jnp.float32) + attn_out.astype(jnp.float32)
    center = lax.optimization_barrier(jnp.mean(hidden, axis=1, keepdims=True))
    variance = lax.optimization_barrier(jnp.mean(jnp.square(hidden - center), axis=1, keepdims=True))
    inverse = lax.rsqrt(variance + 1e-06)
    normal_unit = (hidden - center) * inverse
    gain_wide = gain_full.astype(jnp.float32)
    normed = rounded(normal_unit * gain_wide)
    pre_act = jnp.dot(normed, up_full, preferred_element_type=jnp.float32)
    sig_gate = jax.nn.sigmoid(1.702 * pre_act)
    act_low = rounded(pre_act * sig_gate)
    d_act = contract(grad_rows, down_full, 1, 1)
    d_pre = rounded(d_act * (sig_gate + 1.702 * pre_act * sig_gate * (1.0 - sig_gate)))
    d_normed = contract(d_pre, up_full, 1, 1)
    gain_term = lax.optimization_barrier(jnp.sum(d_normed * normal_unit, axis=0))
    d_unit = d_normed * gain_wide
    d_hidden = inverse * (d_unit - lax.optimization_barrier(jnp.mean(d_unit, axis=1, keepdims=True)) - normal_unit * lax.optimization_barrier(jnp.mean(d_unit * normal_unit, axis=1, keepdims=True)))
    grad_resid = rounded(grad_rows.astype(jnp.float32) + d_hidden)
    grad_heads = grad_resid.astype(jnp.float32).reshape(tokens, HEADS, HDIM)
    grad_value = rounded(jnp.einsum('hqk,qhd->khd', probs_low.astype(jnp.float32), grad_heads, precision=best))
    d_probs = jnp.einsum('qhd,khd->hqk', grad_heads, v_heads, precision=best)
    delta = jnp.einsum('qhd,qhd->hq', grad_heads, attn_heads.astype(jnp.float32), precision=best)
    d_scores = rounded(attn_probs * (d_probs - delta[:, :, None]) * att_scale)
    grad_query = rounded(jnp.einsum('hqk,khd->qhd', d_scores.astype(jnp.float32), k_heads, precision=best))
    grad_key = rounded(jnp.einsum('hqk,qhd->khd', d_scores.astype(jnp.float32), q_heads, precision=best))
    down_term = contract(act_low, grad_rows, 0, 0)
    up_term = contract(normed, d_pre, 0, 0)
    flat = (tokens, HEADS * HDIM)
    return (grad_query.reshape(flat), grad_key.reshape(flat), grad_value.reshape(flat), grad_resid, up_term, down_term, gain_term)

def reference(queries, key_rows, value_rows, resid_in, llm_grad, vision_slot, window_mask, w_up, w_down, norm_gain):

    def batch_step(totals, batch):
        query, key_block, value_block, resid, llm_rows, slot_ids, mask_rows = batch
        target = jnp.where(slot_ids >= 0, slot_ids, VISION).astype(jnp.int32)
        grad_rows = jnp.zeros((VISION, D), jnp.bfloat16).at[target].set(llm_rows, mode='drop')
        per_owner = (query.reshape(N_SEQ, TOK_DEV, D), key_block.reshape(N_SEQ, TOK_DEV, D), value_block.reshape(N_SEQ, TOK_DEV, D), resid.reshape(N_SEQ, TOK_DEV, D), grad_rows.reshape(N_SEQ, TOK_DEV, D), mask_rows.reshape(N_SEQ, NBD, NBD))

        def owner_step(sums, owner):
            results = owner_pass(owner[0], owner[1], owner[2], owner[3], owner[4], owner[5], w_up, w_down, norm_gain)
            up_sum = sums[0] + rounded(results[4]).astype(jnp.float32)
            down_sum = sums[1] + rounded(results[5]).astype(jnp.float32)
            gain_sum = sums[2] + results[6]
            return ((up_sum, down_sum, gain_sum), (results[0], results[1], results[2], results[3]))
        start = (jnp.zeros((D, FF), jnp.float32), jnp.zeros((FF, D), jnp.float32), jnp.zeros((D,), jnp.float32))
        inner, grads = lax.scan(owner_step, start, per_owner)
        up_total = totals[0] + rounded(inner[0]).astype(jnp.float32)
        down_total = totals[1] + rounded(inner[1]).astype(jnp.float32)
        gain_total = totals[2] + inner[2]
        shaped = (grads[0].reshape(VISION, D), grads[1].reshape(VISION, D), grads[2].reshape(VISION, D), grads[3].reshape(VISION, D))
        return ((up_total, down_total, gain_total), shaped)
    start = (jnp.zeros((D, FF), jnp.float32), jnp.zeros((FF, D), jnp.float32), jnp.zeros((D,), jnp.float32))
    final, grads = lax.scan(batch_step, start, (queries, key_rows, value_rows, resid_in, llm_grad, vision_slot, window_mask))
    factor = 1.0 / math.sqrt(BATCHES * VISION)
    return (grads[0], grads[1], grads[2], grads[3], (final[0] * factor).astype(jnp.bfloat16), (final[1] * factor).astype(jnp.bfloat16), final[2] * factor)
```

```python
import math

import jax
import jax.numpy as jnp
from jax import lax
from jax.sharding import PartitionSpec as P

HEADS = 16
HDIM = 80
BLK = 64
PIECE = 16
CORES = 2


def contract(left, right, left_dim, right_dim):
    return lax.dot_general(
        left, right, (((left_dim,), (right_dim,)), ((), ())), preferred_element_type=jnp.float32
    )


def pick(blocks, index):
    return lax.dynamic_index_in_dim(blocks, index, 0, keepdims=False)


def swap_dp(block, count, step):
    return lax.ppermute(block, "dp", [(i, i ^ step) for i in range(count)])


def swap_seq(block, count, step):
    return lax.ppermute(block, "seq", [(i, i ^ step) for i in range(count)])


def gather_up(w_up, n_dp, n_seq, dp, core):
    rows, ff = w_up.shape
    cols, half = ff // n_dp, rows // CORES
    own = lax.dynamic_slice(w_up, (0, dp * cols), (rows, cols))
    got = []
    for k in range(1, n_dp):
        piece = lax.dynamic_slice(w_up, (core * half, (dp ^ k) * cols), (half, cols))
        got.append(swap_dp(piece, n_dp, k))
    mine = jnp.stack(got)
    mate = swap_seq(mine, n_seq, 1)
    low = jnp.where(core == 0, mine, mate)
    high = jnp.where(core == 0, mate, mine)
    pairs = jnp.concatenate([low, high], axis=1)
    full = jnp.concatenate([own[None], pairs], axis=0)
    order = dp ^ jnp.arange(n_dp)
    return full[order].reshape(n_dp * rows, cols)


def gather_gain(norm_gain, n_dp, dp):
    parts = jnp.stack(
        [norm_gain] + [swap_dp(norm_gain, n_dp, k) for k in range(1, n_dp)]
    )
    return parts[dp ^ jnp.arange(n_dp)].reshape(-1)


def owner_rows(llm_rows, slot_ids, n_seq, tokens):
    length, feat = llm_rows.shape
    per_owner = tokens // PIECE
    capacity = 1 + (per_owner + n_seq - 2) // n_seq
    first = slot_ids.reshape(length // PIECE, PIECE)[:, 0]
    tile = jnp.where(first >= 0, first // PIECE, n_seq * per_owner)
    owner = tile // per_owner
    place = tile % per_owner
    onehot = (owner[:, None] == jnp.arange(n_seq)[None, :]).astype(jnp.int32)
    rank = jnp.sum((jnp.cumsum(onehot, axis=0) - 1) * onehot, axis=1)
    target = jnp.where(first >= 0, owner * capacity + rank, -1)
    row_in = jnp.arange(length) % PIECE
    target_row = jnp.repeat(target * PIECE, PIECE) + row_in
    place_row = jnp.repeat(place * PIECE, PIECE) + row_in
    slots = n_seq * capacity * PIECE
    select = (target_row[None, :] == jnp.arange(slots)[:, None]).astype(jnp.bfloat16)
    tag = jnp.where(jnp.arange(128)[None, :] == 0, jnp.repeat(place + 1, PIECE)[:, None], 0)
    wide = jnp.concatenate([llm_rows, tag.astype(jnp.bfloat16)], axis=1)
    send = contract(select, wide, 1, 0).astype(jnp.bfloat16)
    got = lax.all_to_all(
        send.reshape(n_seq, capacity * PIECE, feat + 128),
        "seq",
        split_axis=0,
        concat_axis=0,
        tiled=True,
    ).reshape(slots, feat + 128)
    tile_got = got[:, feat : feat + 1].astype(jnp.int32) - 1
    row_got = tile_got * PIECE + (jnp.arange(slots) % PIECE)[:, None]
    place_got = jnp.where(tile_got >= 0, row_got, -1)
    landing = (place_got == jnp.arange(tokens)[None, :]).astype(jnp.bfloat16)
    return contract(landing, got[:, :feat], 0, 0).astype(jnp.bfloat16)


def gather_tokens(block, n_dp):
    return jnp.concatenate([block] + [swap_dp(block, n_dp, k) for k in range(1, n_dp)], axis=0)


def scatter_up(term, n_seq, seq):
    n_z, core, z = n_seq // CORES, seq % CORES, seq // CORES
    rows, cols = term.shape
    pieces = term.reshape(n_z, CORES, rows // n_seq, cols)
    keep = lax.dynamic_index_in_dim(pieces, core, 1, keepdims=False)
    give = lax.dynamic_index_in_dim(pieces, 1 - core, 1, keepdims=False)
    both = (
        keep.astype(jnp.float32) + swap_seq(give.astype(jnp.bfloat16), n_seq, 1).astype(jnp.float32)
    ).astype(jnp.bfloat16)
    total = pick(both, z).astype(jnp.float32)
    for k in reversed(range(1, n_z)):
        total = total + swap_seq(pick(both, z ^ k), n_seq, CORES * k).astype(jnp.float32)
    return total


def scatter_down(term, n_seq, n_dp, seq, dp):
    n_z, core, z = n_seq // CORES, seq % CORES, seq // CORES
    rows, cols = term.shape
    n_h, width = n_seq // n_dp, cols // n_dp
    if n_h != CORES:
        return scatter_down_direct(term, n_seq, n_dp, seq)
    half = rows // CORES
    keep = lax.dynamic_slice(term, (core * half, 0), (half, cols))
    give = lax.dynamic_slice(term, ((1 - core) * half, 0), (half, cols))
    both = (
        keep.astype(jnp.float32) + swap_seq(give.astype(jnp.bfloat16), n_seq, 1).astype(jnp.float32)
    ).astype(jnp.bfloat16)
    pieces = both.reshape(half, n_dp, width).transpose(1, 0, 2)
    planes = jnp.stack(
        [pick(pieces, dp)] + [swap_dp(pick(pieces, dp ^ k), n_dp, k) for k in range(1, n_dp)]
    )
    total = pick(planes, dp ^ z).astype(jnp.float32)
    for k in reversed(range(1, n_z)):
        total = total + swap_seq(pick(planes, dp ^ z ^ k), n_seq, CORES * k).astype(jnp.float32)
    return total


def scatter_down_direct(term, n_seq, n_dp, seq):
    n_z, core, z = n_seq // CORES, seq % CORES, seq // CORES
    rows, cols = term.shape
    n_h, n_e = n_seq // n_dp, n_dp // CORES
    half = cols // CORES
    keep = lax.dynamic_slice(term, (0, core * half), (rows, half))
    give = lax.dynamic_slice(term, (0, (1 - core) * half), (rows, half))
    both = keep + swap_seq(give.astype(jnp.bfloat16), n_seq, 1).astype(jnp.float32)
    pieces = (
        both.reshape(n_h, rows // n_h, n_e, half // n_e)
        .transpose(0, 2, 1, 3)
        .reshape(n_z, rows // n_h, half // n_e)
        .astype(jnp.bfloat16)
    )
    total = 0.0
    for j in range(n_z):
        pairs = []
        for a in range(n_z):
            m = (a + j) % n_z
            for c in range(CORES):
                for d in range(n_dp):
                    source = (a * CORES + c) * n_dp + d
                    goal = (d * n_h + m // n_e) * n_dp + c * n_e + m % n_e
                    pairs.append((source, goal))
        block = lax.ppermute(pick(pieces, (z + j) % n_z), ("seq", "dp"), pairs)
        total = total + block.astype(jnp.float32)
    return total


def sum_all(term, n_seq, n_dp):
    total = term + swap_seq(term, n_seq, 1)
    term = total
    for k in range(1, n_seq // CORES):
        total = total + swap_seq(term, n_seq, CORES * k)
    term = total
    for k in range(1, n_dp):
        total = total + swap_dp(term, n_dp, k)
    return total


def per_device(
    queries,
    key_rows,
    value_rows,
    resid_in,
    llm_grad,
    vision_slot,
    window_mask,
    w_up,
    w_down,
    norm_gain,
):
    n_seq = lax.axis_size("seq")
    n_dp = lax.axis_size("dp")
    seq = lax.axis_index("seq")
    dp = lax.axis_index("dp")
    core = seq % CORES
    query = queries[0]
    key_block = key_rows[0]
    value_block = value_rows[0]
    tokens, feat_dim = query.shape
    att_scale = 1.0 / math.sqrt(HDIM)

    grad_rows = owner_rows(llm_grad[0], vision_slot[0], n_seq, tokens)
    gain_full = gather_gain(norm_gain, n_dp, dp)
    up_cols = gather_up(w_up, n_dp, n_seq, dp, core)

    allowed = jnp.repeat(jnp.repeat(window_mask[0] > 0, BLK, axis=0), BLK, axis=1)
    q_heads = query.reshape(tokens, HEADS, HDIM)
    k_heads = key_block.reshape(tokens, HEADS, HDIM)
    v_heads = value_block.reshape(tokens, HEADS, HDIM)
    scores = (
        jnp.einsum("qhd,khd->hqk", q_heads, k_heads, preferred_element_type=jnp.float32) * att_scale
    )
    masked = jnp.where(allowed[None], scores, -jnp.inf)
    highest = jnp.max(masked, axis=2, keepdims=True)
    exp_terms = jnp.where(allowed[None], jnp.exp(masked - highest), 0.0)
    attn_probs = exp_terms / jnp.sum(exp_terms, axis=2, keepdims=True)
    probs_low = attn_probs.astype(jnp.bfloat16)
    attn_heads = jnp.einsum(
        "hqk,khd->qhd", probs_low, v_heads, preferred_element_type=jnp.float32
    ).astype(jnp.bfloat16)
    attn_out = attn_heads.reshape(tokens, feat_dim)
    hidden = resid_in[0].astype(jnp.float32) + attn_out.astype(jnp.float32)
    center = jnp.mean(hidden, axis=1, keepdims=True)
    variance = jnp.mean(jnp.square(hidden - center), axis=1, keepdims=True)
    inverse = lax.rsqrt(variance + 1e-06)
    normal_unit = (hidden - center) * inverse
    gain_wide = gain_full.astype(jnp.float32)
    normed = (normal_unit * gain_wide).astype(jnp.bfloat16)

    normed_all = gather_tokens(normed, n_dp)
    rows_all = gather_tokens(grad_rows, n_dp)
    pre_act = contract(normed_all, up_cols, 1, 0)
    sig_gate = jax.nn.sigmoid(1.702 * pre_act)
    act_low = (pre_act * sig_gate).astype(jnp.bfloat16)
    d_act = contract(rows_all, w_down, 1, 1)
    d_pre = (d_act * (sig_gate + 1.702 * pre_act * sig_gate * (1.0 - sig_gate))).astype(
        jnp.bfloat16
    )
    d_part = contract(d_pre, up_cols, 1, 1)
    d_normed = d_part[:tokens]
    for k in range(1, n_dp):
        block = d_part[k * tokens : (k + 1) * tokens].astype(jnp.bfloat16)
        d_normed = d_normed + swap_dp(block, n_dp, k).astype(jnp.float32)

    up_term = contract(normed_all, d_pre, 0, 0)
    down_term = contract(act_low, rows_all, 0, 0)
    up_panel = scatter_up(up_term, n_seq, seq)
    down_panel = scatter_down(down_term, n_seq, n_dp, seq, dp)

    gain_term = jnp.sum(d_normed * normal_unit, axis=0)
    d_unit = d_normed * gain_wide
    d_hidden = inverse * (
        d_unit
        - jnp.mean(d_unit, axis=1, keepdims=True)
        - normal_unit * jnp.mean(d_unit * normal_unit, axis=1, keepdims=True)
    )
    grad_resid = (grad_rows.astype(jnp.float32) + d_hidden).astype(jnp.bfloat16)
    grad_heads = grad_resid.reshape(tokens, HEADS, HDIM)
    grad_value = jnp.einsum(
        "hqk,qhd->khd", probs_low, grad_heads, preferred_element_type=jnp.float32
    ).astype(jnp.bfloat16)
    d_probs = jnp.einsum("qhd,khd->hqk", grad_heads, v_heads, preferred_element_type=jnp.float32)
    delta = jnp.einsum("qhd,qhd->hq", grad_heads, attn_heads, preferred_element_type=jnp.float32)
    d_scores = (attn_probs * (d_probs - delta[:, :, None]) * att_scale).astype(jnp.bfloat16)
    grad_query = jnp.einsum(
        "hqk,khd->qhd", d_scores, k_heads, preferred_element_type=jnp.float32
    ).astype(jnp.bfloat16)
    grad_key = jnp.einsum(
        "hqk,qhd->khd", d_scores, q_heads, preferred_element_type=jnp.float32
    ).astype(jnp.bfloat16)
    factor = 1.0 / math.sqrt(n_dp * n_seq * tokens)
    gain_total = sum_all(gain_term, n_seq, n_dp)
    return (
        grad_query.reshape(1, tokens, feat_dim),
        grad_key.reshape(1, tokens, feat_dim),
        grad_value.reshape(1, tokens, feat_dim),
        grad_resid[None],
        (up_panel * factor).astype(jnp.bfloat16),
        (down_panel * factor).astype(jnp.bfloat16),
        gain_total * factor,
    )


def solution(mesh):
    in_specs = (
        P("dp", "seq", None),
        P("dp", "seq", None),
        P("dp", "seq", None),
        P("dp", "seq", None),
        P("dp", "seq", None),
        P("dp", "seq"),
        P("dp", "seq", None),
        P("dp", None),
        P("dp", None),
        P("dp"),
    )
    out_specs = (
        P("dp", "seq", None),
        P("dp", "seq", None),
        P("dp", "seq", None),
        P("dp", "seq", None),
        P("seq", "dp"),
        P("seq", "dp"),
        P(),
    )
    return jax.shard_map(
        per_device, mesh=mesh, in_specs=in_specs, out_specs=out_specs, check_vma=False
    )
```

```python
import math

import jax
import jax.numpy as jnp
from jax import lax
from jax.experimental import pallas as pl
from jax.experimental.pallas import tpu as pltpu
from jax.sharding import PartitionSpec as P

HEADS = 16
HDIM = 80
BLK = 64
PIECE = 16
CORES = 2
LANES = 128
VMEM_BYTES = 48 * 1024 * 1024


def vmem_call(body, out_shape, in_spaces, flops):
    return pl.pallas_call(
        body,
        out_shape=out_shape,
        in_specs=[pl.BlockSpec(memory_space=space) for space in in_spaces],
        out_specs=jax.tree.map(lambda _: pl.BlockSpec(memory_space=pltpu.VMEM), out_shape),
        compiler_params=pltpu.CompilerParams(vmem_limit_bytes=VMEM_BYTES),
        cost_estimate=pl.CostEstimate(flops=flops, bytes_accessed=4 << 20, transcendentals=0),
    )


def contract(left, right, left_dim, right_dim):
    return lax.dot_general(
        left, right, (((left_dim,), (right_dim,)), ((), ())), preferred_element_type=jnp.float32
    )


def pick(blocks, index):
    return lax.dynamic_index_in_dim(blocks, index, 0, keepdims=False)


def swap_dp(block, count, step):
    return lax.ppermute(block, "dp", [(i, i ^ step) for i in range(count)])


def swap_seq(block, count, step):
    return lax.ppermute(block, "seq", [(i, i ^ step) for i in range(count)])


def gather_up(w_up, n_dp, n_seq, dp, core):
    rows, ff = w_up.shape
    cols, half = ff // n_dp, rows // CORES
    own = lax.dynamic_slice(w_up, (0, dp * cols), (rows, cols))
    got = []
    for k in range(1, n_dp):
        piece = lax.dynamic_slice(w_up, (core * half, (dp ^ k) * cols), (half, cols))
        got.append(swap_dp(piece, n_dp, k))
    mine = jnp.stack(got)
    mate = swap_seq(mine, n_seq, 1)
    low = jnp.where(core == 0, mine, mate)
    high = jnp.where(core == 0, mate, mine)
    pairs = jnp.concatenate([low, high], axis=1)
    full = jnp.concatenate([own[None], pairs], axis=0)
    order = dp ^ jnp.arange(n_dp)
    return full[order].reshape(n_dp * rows, cols)


def gather_gain(norm_gain, n_dp, dp):
    parts = jnp.stack(
        [norm_gain] + [swap_dp(norm_gain, n_dp, k) for k in range(1, n_dp)]
    )
    return parts[dp ^ jnp.arange(n_dp)].reshape(-1)


def send_kernel(n_seq, capacity, per_owner, slot_ref, rows_ref, out_ref):
    length, feat = rows_ref.shape
    out_ref[...] = jnp.zeros(out_ref.shape, jnp.bfloat16)
    row = lax.broadcasted_iota(jnp.int32, (PIECE, LANES), 0)
    firsts = [slot_ref[0, t * PIECE] for t in range(length // PIECE)]
    owners = [jnp.where(f >= 0, f // (per_owner * PIECE), n_seq) for f in firsts]
    for t, first in enumerate(firsts):
        rank = jnp.int32(0)
        for earlier in range(t):
            rank = rank + jnp.where(owners[earlier] == owners[t], 1, 0)

        @pl.when(first >= 0)
        def _(t=t, first=first, rank=rank):
            place = pl.ds(pl.multiple_of(rank * PIECE, PIECE), PIECE)
            out_ref[owners[t], place, :feat] = rows_ref[t * PIECE : (t + 1) * PIECE, :]
            landing = first % (per_owner * PIECE) + row + 1
            out_ref[owners[t], place, feat:] = landing.astype(jnp.float32).astype(jnp.bfloat16)


def land_kernel(got_ref, out_ref):
    tokens, feat = out_ref.shape
    slots = got_ref.shape[0]
    marks = got_ref[:, feat:].astype(jnp.float32)
    goal = lax.broadcasted_iota(jnp.int32, (slots, LANES), 1) + 1
    rows = got_ref[:, :feat]
    for part in range(tokens // LANES):
        select = (marks == (goal + part * LANES).astype(jnp.float32)).astype(jnp.bfloat16)
        out_ref[part * LANES : (part + 1) * LANES, :] = contract(select, rows, 0, 0).astype(
            jnp.bfloat16
        )


def owner_rows(llm_rows, slot_ids, n_seq, tokens):
    length, feat = llm_rows.shape
    per_owner = tokens // PIECE
    capacity = 1 + (per_owner + n_seq - 2) // n_seq
    rows = capacity * PIECE
    send = vmem_call(
        lambda *refs: send_kernel(n_seq, capacity, per_owner, *refs),
        jax.ShapeDtypeStruct((n_seq, rows, feat + LANES), jnp.bfloat16),
        [pltpu.SMEM, pltpu.VMEM],
        1 << 20,
    )(slot_ids, llm_rows)
    got = lax.all_to_all(send, "seq", split_axis=0, concat_axis=0, tiled=True)
    landed = vmem_call(
        land_kernel,
        jax.ShapeDtypeStruct((tokens, feat), jnp.bfloat16),
        [pltpu.VMEM],
        1 << 26,
    )(got.reshape(n_seq * rows, feat + LANES))
    return send, landed


def head_lanes(head, rows, width, start):
    lane = lax.broadcasted_iota(jnp.int32, (rows, width), 1) + start
    return (lane >= head * HDIM) & (lane < (head + 1) * HDIM)


def span_of(head):
    start = head * HDIM // LANES * LANES
    stop = -(-(head + 1) * HDIM // LANES) * LANES
    return start, stop


def masked_head(ref, head):
    start, stop = span_of(head)
    block = ref[:, start:stop]
    return jnp.where(head_lanes(head, block.shape[0], stop - start, start), block, 0).astype(
        block.dtype
    )


def add_span(total, head, part):
    start, stop = span_of(head)
    for at in range(start, stop, LANES):
        piece = part[:, at - start : at - start + LANES]
        total[at] = total[at] + piece if at in total else piece


def forward_kernel(
    mask_ref, q_ref, k_ref, v_ref, resid_ref, probs_ref, out_ref, unit_ref, inverse_ref
):
    tokens, feat = q_ref.shape
    scale = 1.0 / math.sqrt(HDIM)
    row = lax.broadcasted_iota(jnp.int32, (tokens, tokens), 0) // BLK
    col = lax.broadcasted_iota(jnp.int32, (tokens, tokens), 1) // BLK
    allowed = row == col
    for i in range(tokens // BLK):
        for j in range(tokens // BLK):
            if i != j:
                allowed = allowed | ((row == i) & (col == j) & (mask_ref[i, j] > 0))
    total = {}
    for head in range(HEADS):
        start, stop = span_of(head)
        scores = contract(q_ref[:, start:stop], masked_head(k_ref, head), 1, 1) * scale
        scores = jnp.where(allowed, scores, -jnp.inf)
        exp_terms = jnp.exp(scores - jnp.max(scores, axis=1, keepdims=True))
        probs = exp_terms / jnp.sum(exp_terms, axis=1, keepdims=True)
        probs_ref[head] = probs
        add_span(total, head, contract(probs.astype(jnp.bfloat16), masked_head(v_ref, head), 1, 0))
    for at, value in total.items():
        out_ref[:, at : at + LANES] = value.astype(jnp.bfloat16)
    hidden = resid_ref[...].astype(jnp.float32) + out_ref[...].astype(jnp.float32)
    center = jnp.mean(hidden, axis=1, keepdims=True)
    hidden = hidden - center
    variance = jnp.mean(jnp.square(hidden), axis=1, keepdims=True)
    inverse = lax.rsqrt(variance + 1e-06)
    unit_ref[...] = hidden * inverse
    inverse_ref[...] = jnp.broadcast_to(inverse, inverse_ref.shape)


def forward(mask, query, key_block, value_block, resid):
    tokens, feat = query.shape
    return vmem_call(
        forward_kernel,
        (
            jax.ShapeDtypeStruct((HEADS, tokens, tokens), jnp.float32),
            jax.ShapeDtypeStruct((tokens, feat), jnp.bfloat16),
            jax.ShapeDtypeStruct((tokens, feat), jnp.float32),
            jax.ShapeDtypeStruct((tokens, LANES), jnp.float32),
        ),
        [pltpu.SMEM] + [pltpu.VMEM] * 4,
        1 << 31,
    )(mask, query, key_block, value_block, resid)


def backward_kernel(
    own_ref,
    got_ref,
    rows_ref,
    unit_ref,
    inverse_ref,
    gain_ref,
    probs_ref,
    out_ref,
    q_ref,
    k_ref,
    v_ref,
    gq_ref,
    gk_ref,
    gv_ref,
    gr_ref,
    gain_term_ref,
):
    tokens, feat = q_ref.shape
    scale = 1.0 / math.sqrt(HDIM)
    d_normed = own_ref[...]
    for part in range(got_ref.shape[0]):
        d_normed = d_normed + got_ref[part].astype(jnp.float32)
    unit = unit_ref[...]
    gain_term_ref[...] = jnp.sum(d_normed * unit, axis=0, keepdims=True)
    d_unit = d_normed * gain_ref[...].astype(jnp.float32)
    d_hidden = inverse_ref[:, :1] * (
        d_unit
        - jnp.mean(d_unit, axis=1, keepdims=True)
        - unit * jnp.mean(d_unit * unit, axis=1, keepdims=True)
    )
    gr_ref[...] = (rows_ref[...].astype(jnp.float32) + d_hidden).astype(jnp.bfloat16)
    totals = ({}, {}, {})
    for head in range(HEADS):
        start, stop = span_of(head)
        probs = probs_ref[head]
        grad = masked_head(gr_ref, head)
        add_span(totals[0], head, contract(probs.astype(jnp.bfloat16), grad, 0, 0))
        d_probs = contract(grad, v_ref[:, start:stop], 1, 1)
        delta = jnp.sum(
            grad.astype(jnp.float32) * out_ref[:, start:stop].astype(jnp.float32),
            axis=1,
            keepdims=True,
        )
        d_scores = (probs * (d_probs - delta) * scale).astype(jnp.bfloat16)
        add_span(totals[1], head, contract(d_scores, masked_head(k_ref, head), 1, 0))
        add_span(totals[2], head, contract(d_scores, masked_head(q_ref, head), 0, 0))
    for ref, total in zip((gv_ref, gq_ref, gk_ref), totals):
        for at, value in total.items():
            ref[:, at : at + LANES] = value.astype(jnp.bfloat16)


def backward(*operands):
    tokens, feat = operands[0].shape
    return vmem_call(
        backward_kernel,
        tuple(jax.ShapeDtypeStruct((tokens, feat), jnp.bfloat16) for _ in range(4))
        + (jax.ShapeDtypeStruct((1, feat), jnp.float32),),
        [pltpu.VMEM] * 11,
        1 << 32,
    )(*operands)


def gather_tokens(block, n_dp):
    return jnp.concatenate([block] + [swap_dp(block, n_dp, k) for k in range(1, n_dp)], axis=0)


def scatter_up(term, n_seq, seq):
    n_z, core, z = n_seq // CORES, seq % CORES, seq // CORES
    rows, cols = term.shape
    pieces = term.reshape(n_z, CORES, rows // n_seq, cols)
    keep = lax.dynamic_index_in_dim(pieces, core, 1, keepdims=False)
    give = lax.dynamic_index_in_dim(pieces, 1 - core, 1, keepdims=False)
    both = (
        keep.astype(jnp.float32) + swap_seq(give.astype(jnp.bfloat16), n_seq, 1).astype(jnp.float32)
    ).astype(jnp.bfloat16)
    total = pick(both, z).astype(jnp.float32)
    for k in reversed(range(1, n_z)):
        total = total + swap_seq(pick(both, z ^ k), n_seq, CORES * k).astype(jnp.float32)
    return total


def scatter_down(term, n_seq, n_dp, seq, dp):
    n_z, core, z = n_seq // CORES, seq % CORES, seq // CORES
    rows, cols = term.shape
    n_h, width = n_seq // n_dp, cols // n_dp
    if n_h != CORES:
        return scatter_down_direct(term, n_seq, n_dp, seq)
    half = rows // CORES
    keep = lax.dynamic_slice(term, (core * half, 0), (half, cols))
    give = lax.dynamic_slice(term, ((1 - core) * half, 0), (half, cols))
    both = (
        keep.astype(jnp.float32) + swap_seq(give.astype(jnp.bfloat16), n_seq, 1).astype(jnp.float32)
    ).astype(jnp.bfloat16)
    pieces = both.reshape(half, n_dp, width).transpose(1, 0, 2)
    planes = jnp.stack(
        [pick(pieces, dp)] + [swap_dp(pick(pieces, dp ^ k), n_dp, k) for k in range(1, n_dp)]
    )
    total = pick(planes, dp ^ z).astype(jnp.float32)
    for k in reversed(range(1, n_z)):
        total = total + swap_seq(pick(planes, dp ^ z ^ k), n_seq, CORES * k).astype(jnp.float32)
    return total


def scatter_down_direct(term, n_seq, n_dp, seq):
    n_z, core, z = n_seq // CORES, seq % CORES, seq // CORES
    rows, cols = term.shape
    n_h, n_e = n_seq // n_dp, n_dp // CORES
    half = cols // CORES
    keep = lax.dynamic_slice(term, (0, core * half), (rows, half))
    give = lax.dynamic_slice(term, (0, (1 - core) * half), (rows, half))
    both = keep + swap_seq(give.astype(jnp.bfloat16), n_seq, 1).astype(jnp.float32)
    pieces = (
        both.reshape(n_h, rows // n_h, n_e, half // n_e)
        .transpose(0, 2, 1, 3)
        .reshape(n_z, rows // n_h, half // n_e)
        .astype(jnp.bfloat16)
    )
    total = 0.0
    for j in range(n_z):
        pairs = []
        for a in range(n_z):
            m = (a + j) % n_z
            for c in range(CORES):
                for d in range(n_dp):
                    source = (a * CORES + c) * n_dp + d
                    goal = (d * n_h + m // n_e) * n_dp + c * n_e + m % n_e
                    pairs.append((source, goal))
        block = lax.ppermute(pick(pieces, (z + j) % n_z), ("seq", "dp"), pairs)
        total = total + block.astype(jnp.float32)
    return total


def sum_all(term, n_seq, n_dp):
    total = term + swap_seq(term, n_seq, 1)
    term = total
    for k in range(1, n_seq // CORES):
        total = total + swap_seq(term, n_seq, CORES * k)
    term = total
    for k in range(1, n_dp):
        total = total + swap_dp(term, n_dp, k)
    return total


def per_device(
    queries,
    key_rows,
    value_rows,
    resid_in,
    llm_grad,
    vision_slot,
    window_mask,
    w_up,
    w_down,
    norm_gain,
):
    n_seq = lax.axis_size("seq")
    n_dp = lax.axis_size("dp")
    seq = lax.axis_index("seq")
    dp = lax.axis_index("dp")
    core = seq % CORES
    tokens, feat_dim = queries.shape[1:]

    send, grad_rows = owner_rows(llm_grad[0], vision_slot, n_seq, tokens)
    w_up, norm_gain, send = lax.optimization_barrier((w_up, norm_gain, send))
    gain_full = gather_gain(norm_gain, n_dp, dp)
    up_cols = gather_up(w_up, n_dp, n_seq, dp, core)

    attn_probs, attn_out, normal_unit, inverse = forward(
        window_mask[0], queries[0], key_rows[0], value_rows[0], resid_in[0]
    )
    normed = (normal_unit * gain_full.astype(jnp.float32)).astype(jnp.bfloat16)

    normed_all = gather_tokens(normed, n_dp)
    rows_all = gather_tokens(grad_rows, n_dp)
    pre_act = contract(normed_all, up_cols, 1, 0)
    sig_gate = jax.nn.sigmoid(1.702 * pre_act)
    act_low = (pre_act * sig_gate).astype(jnp.bfloat16)
    d_act = contract(rows_all, w_down, 1, 1)
    d_pre = (d_act * (sig_gate + 1.702 * pre_act * sig_gate * (1.0 - sig_gate))).astype(
        jnp.bfloat16
    )
    d_part = contract(d_pre, up_cols, 1, 1)
    d_got = jnp.stack(
        [
            swap_dp(d_part[k * tokens : (k + 1) * tokens].astype(jnp.bfloat16), n_dp, k)
            for k in range(1, n_dp)
        ]
    )

    up_term = contract(normed_all, d_pre, 0, 0)
    down_term = contract(act_low, rows_all, 0, 0)
    up_panel = scatter_up(up_term, n_seq, seq)
    down_panel = scatter_down(down_term, n_seq, n_dp, seq, dp)

    grad_query, grad_key, grad_value, grad_resid, gain_term = backward(
        d_part[:tokens],
        d_got,
        grad_rows,
        normal_unit,
        inverse,
        gain_full[None],
        attn_probs,
        attn_out,
        queries[0],
        key_rows[0],
        value_rows[0],
    )
    factor = 1.0 / math.sqrt(n_dp * n_seq * tokens)
    gain_total = sum_all(gain_term[0], n_seq, n_dp)
    return (
        grad_query[None],
        grad_key[None],
        grad_value[None],
        grad_resid[None],
        (up_panel * factor).astype(jnp.bfloat16),
        (down_panel * factor).astype(jnp.bfloat16),
        gain_total * factor,
    )


def solution(mesh):
    in_specs = (
        P("dp", "seq", None),
        P("dp", "seq", None),
        P("dp", "seq", None),
        P("dp", "seq", None),
        P("dp", "seq", None),
        P("dp", "seq"),
        P("dp", "seq", None),
        P("dp", None),
        P("dp", None),
        P("dp"),
    )
    out_specs = (
        P("dp", "seq", None),
        P("dp", "seq", None),
        P("dp", "seq", None),
        P("dp", "seq", None),
        P("seq", "dp"),
        P("seq", "dp"),
        P(),
    )
    return jax.shard_map(
        per_device, mesh=mesh, in_specs=in_specs, out_specs=out_specs, check_vma=False
    )
```

```python
import math

import jax
import jax.numpy as jnp
from jax import lax
from jax.experimental import pallas as pl
from jax.experimental.pallas import tpu as pltpu
from jax.sharding import PartitionSpec as P

HEADS = 16
HDIM = 80
BLK = 64
PIECE = 16
CORES = 2
LANES = 128
VMEM_BYTES = 32 * 1024 * 1024


def vmem_call(body, out_shape, in_spaces, flops):
    return pl.pallas_call(
        body,
        out_shape=out_shape,
        in_specs=[pl.BlockSpec(memory_space=space) for space in in_spaces],
        out_specs=jax.tree.map(lambda _: pl.BlockSpec(memory_space=pltpu.VMEM), out_shape),
        compiler_params=pltpu.CompilerParams(vmem_limit_bytes=VMEM_BYTES),
        cost_estimate=pl.CostEstimate(flops=flops, bytes_accessed=4 << 20, transcendentals=0),
    )


def contract(left, right, left_dim, right_dim):
    return lax.dot_general(
        left, right, (((left_dim,), (right_dim,)), ((), ())), preferred_element_type=jnp.float32
    )


def pick(blocks, index):
    return lax.dynamic_index_in_dim(blocks, index, 0, keepdims=False)


def swap_dp(block, count, step):
    return lax.ppermute(block, "dp", [(i, i ^ step) for i in range(count)])


def swap_seq(block, count, step):
    return lax.ppermute(block, "seq", [(i, i ^ step) for i in range(count)])


def fetch_up(w_up, n_dp, n_seq, dp, core):
    rows, ff = w_up.shape
    cols, half = ff // n_dp, rows // CORES
    own = lax.dynamic_slice(w_up, (0, dp * cols), (rows, cols))
    got = []
    for k in range(1, n_dp):
        piece = lax.dynamic_slice(w_up, (core * half, (dp ^ k) * cols), (half, cols))
        got.append(swap_dp(piece, n_dp, k))
    mine = jnp.stack(got)
    return own, mine, swap_seq(mine, n_seq, 1)


def join_up(own, mine, mate, n_dp, dp, core):
    low = jnp.where(core == 0, mine, mate)
    high = jnp.where(core == 0, mate, mine)
    pairs = jnp.concatenate([low, high], axis=1)
    full = jnp.concatenate([own[None], pairs], axis=0)
    return full[dp ^ jnp.arange(n_dp)].reshape(-1, own.shape[1])


def gather_gain(norm_gain, n_dp, dp):
    parts = jnp.stack(
        [norm_gain] + [swap_dp(norm_gain, n_dp, k) for k in range(1, n_dp)]
    )
    return parts[dp ^ jnp.arange(n_dp)].reshape(-1)


def send_kernel(n_seq, capacity, per_owner, slot_ref, rows_ref, out_ref):
    length, feat = rows_ref.shape
    out_ref[...] = jnp.zeros(out_ref.shape, jnp.bfloat16)
    row = lax.broadcasted_iota(jnp.int32, (PIECE, LANES), 0)
    firsts = [slot_ref[0, t * PIECE] for t in range(length // PIECE)]
    owners = [jnp.where(f >= 0, f // (per_owner * PIECE), n_seq) for f in firsts]
    for t, first in enumerate(firsts):
        rank = jnp.int32(0)
        for earlier in range(t):
            rank = rank + jnp.where(owners[earlier] == owners[t], 1, 0)

        @pl.when(first >= 0)
        def _(t=t, first=first, rank=rank):
            place = pl.ds(pl.multiple_of(rank * PIECE, PIECE), PIECE)
            out_ref[owners[t], place, :feat] = rows_ref[t * PIECE : (t + 1) * PIECE, :]
            landing = first % (per_owner * PIECE) + row + 1
            out_ref[owners[t], place, feat:] = landing.astype(jnp.float32).astype(jnp.bfloat16)


def land_kernel(got_ref, out_ref):
    tokens, feat = out_ref.shape
    slots = got_ref.shape[0]
    marks = got_ref[:, feat:].astype(jnp.float32)
    goal = lax.broadcasted_iota(jnp.int32, (slots, LANES), 1) + 1
    rows = got_ref[:, :feat]
    for part in range(tokens // LANES):
        select = (marks == (goal + part * LANES).astype(jnp.float32)).astype(jnp.bfloat16)
        out_ref[part * LANES : (part + 1) * LANES, :] = contract(select, rows, 0, 0).astype(
            jnp.bfloat16
        )


def owner_rows(llm_rows, slot_ids, n_seq, tokens):
    length, feat = llm_rows.shape
    per_owner = tokens // PIECE
    capacity = 1 + (per_owner + n_seq - 2) // n_seq
    rows = capacity * PIECE
    send = vmem_call(
        lambda *refs: send_kernel(n_seq, capacity, per_owner, *refs),
        jax.ShapeDtypeStruct((n_seq, rows, feat + LANES), jnp.bfloat16),
        [pltpu.SMEM, pltpu.VMEM],
        1 << 20,
    )(slot_ids, llm_rows)
    got = lax.all_to_all(send, "seq", split_axis=0, concat_axis=0, tiled=True)
    landed = vmem_call(
        land_kernel,
        jax.ShapeDtypeStruct((tokens, feat), jnp.bfloat16),
        [pltpu.VMEM],
        1 << 26,
    )(got.reshape(n_seq * rows, feat + LANES))
    return send, landed


def head_lanes(head, rows, width, start):
    lane = lax.broadcasted_iota(jnp.int32, (rows, width), 1) + start
    return (lane >= head * HDIM) & (lane < (head + 1) * HDIM)


def span_of(head):
    start = head * HDIM // LANES * LANES
    stop = -(-(head + 1) * HDIM // LANES) * LANES
    return start, stop


def masked_head(ref, head):
    start, stop = span_of(head)
    block = ref[:, start:stop]
    return jnp.where(head_lanes(head, block.shape[0], stop - start, start), block, 0).astype(
        block.dtype
    )


def add_span(total, head, part):
    start, stop = span_of(head)
    for at in range(start, stop, LANES):
        piece = part[:, at - start : at - start + LANES]
        total[at] = total[at] + piece if at in total else piece


def forward_kernel(
    mask_ref, q_ref, k_ref, v_ref, resid_ref, probs_ref, out_ref, unit_ref, inverse_ref
):
    tokens, feat = q_ref.shape
    scale = 1.0 / math.sqrt(HDIM)
    row = lax.broadcasted_iota(jnp.int32, (tokens, tokens), 0) // BLK
    col = lax.broadcasted_iota(jnp.int32, (tokens, tokens), 1) // BLK
    allowed = row == col
    for i in range(tokens // BLK):
        for j in range(tokens // BLK):
            if i != j:
                allowed = allowed | ((row == i) & (col == j) & (mask_ref[i, j] > 0))
    total = {}
    for head in range(HEADS):
        start, stop = span_of(head)
        scores = contract(q_ref[:, start:stop], masked_head(k_ref, head), 1, 1) * scale
        scores = jnp.where(allowed, scores, -jnp.inf)
        exp_terms = jnp.exp(scores - jnp.max(scores, axis=1, keepdims=True))
        probs = exp_terms / jnp.sum(exp_terms, axis=1, keepdims=True)
        probs_ref[head] = probs
        add_span(total, head, contract(probs.astype(jnp.bfloat16), masked_head(v_ref, head), 1, 0))
    for at, value in total.items():
        out_ref[:, at : at + LANES] = value.astype(jnp.bfloat16)
    hidden = resid_ref[...].astype(jnp.float32) + out_ref[...].astype(jnp.float32)
    center = jnp.mean(hidden, axis=1, keepdims=True)
    hidden = hidden - center
    variance = jnp.mean(jnp.square(hidden), axis=1, keepdims=True)
    inverse = lax.rsqrt(variance + 1e-06)
    unit_ref[...] = hidden * inverse
    inverse_ref[...] = jnp.broadcast_to(inverse, inverse_ref.shape)


def forward(mask, query, key_block, value_block, resid):
    tokens, feat = query.shape
    return vmem_call(
        forward_kernel,
        (
            jax.ShapeDtypeStruct((HEADS, tokens, tokens), jnp.float32),
            jax.ShapeDtypeStruct((tokens, feat), jnp.bfloat16),
            jax.ShapeDtypeStruct((tokens, feat), jnp.float32),
            jax.ShapeDtypeStruct((tokens, LANES), jnp.float32),
        ),
        [pltpu.SMEM] + [pltpu.VMEM] * 4,
        1 << 31,
    )(mask, query, key_block, value_block, resid)


def backward_kernel(
    own_ref,
    got_ref,
    rows_ref,
    unit_ref,
    inverse_ref,
    gain_ref,
    probs_ref,
    out_ref,
    q_ref,
    k_ref,
    v_ref,
    gq_ref,
    gk_ref,
    gv_ref,
    gr_ref,
):
    tokens, feat = q_ref.shape
    scale = 1.0 / math.sqrt(HDIM)
    d_normed = own_ref[...]
    for part in range(got_ref.shape[0]):
        d_normed = d_normed + got_ref[part].astype(jnp.float32)
    unit = unit_ref[...]
    d_unit = d_normed * gain_ref[...].astype(jnp.float32)
    d_hidden = inverse_ref[:, :1] * (
        d_unit
        - jnp.mean(d_unit, axis=1, keepdims=True)
        - unit * jnp.mean(d_unit * unit, axis=1, keepdims=True)
    )
    gr_ref[...] = (rows_ref[...].astype(jnp.float32) + d_hidden).astype(jnp.bfloat16)
    totals = ({}, {}, {})
    for head in range(HEADS):
        start, stop = span_of(head)
        probs = probs_ref[head]
        grad = masked_head(gr_ref, head)
        add_span(totals[0], head, contract(probs.astype(jnp.bfloat16), grad, 0, 0))
        d_probs = contract(grad, v_ref[:, start:stop], 1, 1)
        delta = jnp.sum(
            grad.astype(jnp.float32) * out_ref[:, start:stop].astype(jnp.float32),
            axis=1,
            keepdims=True,
        )
        d_scores = (probs * (d_probs - delta) * scale).astype(jnp.bfloat16)
        add_span(totals[1], head, contract(d_scores, masked_head(k_ref, head), 1, 0))
        add_span(totals[2], head, contract(d_scores, masked_head(q_ref, head), 0, 0))
    for ref, total in zip((gv_ref, gq_ref, gk_ref), totals):
        for at, value in total.items():
            ref[:, at : at + LANES] = value.astype(jnp.bfloat16)


def backward(*operands):
    tokens, feat = operands[0].shape
    return vmem_call(
        backward_kernel,
        tuple(jax.ShapeDtypeStruct((tokens, feat), jnp.bfloat16) for _ in range(4)),
        [pltpu.VMEM] * 11,
        1 << 32,
    )(*operands)


def gather_tokens(block, n_dp):
    return jnp.concatenate([block] + [swap_dp(block, n_dp, k) for k in range(1, n_dp)], axis=0)


def scatter_up(term, n_seq, seq):
    n_z, core, z = n_seq // CORES, seq % CORES, seq // CORES
    rows, cols = term.shape
    pieces = term.reshape(n_z, CORES, rows // n_seq, cols)
    keep = lax.dynamic_index_in_dim(pieces, core, 1, keepdims=False)
    give = lax.dynamic_index_in_dim(pieces, 1 - core, 1, keepdims=False)
    both = (
        keep.astype(jnp.float32) + swap_seq(give.astype(jnp.bfloat16), n_seq, 1).astype(jnp.float32)
    ).astype(jnp.bfloat16)
    total = pick(both, z).astype(jnp.float32)
    for k in reversed(range(1, n_z)):
        total = total + swap_seq(pick(both, z ^ k), n_seq, CORES * k).astype(jnp.float32)
    return total


def scatter_down(term, n_seq, n_dp, seq):
    n_z, core, z = n_seq // CORES, seq % CORES, seq // CORES
    rows, cols = term.shape
    n_h, n_e = n_seq // n_dp, n_dp // CORES
    half = cols // CORES
    keep = lax.dynamic_slice(term, (0, core * half), (rows, half))
    give = lax.dynamic_slice(term, (0, (1 - core) * half), (rows, half))
    both = keep + swap_seq(give.astype(jnp.bfloat16), n_seq, 1).astype(jnp.float32)
    pieces = (
        both.reshape(n_h, rows // n_h, n_e, half // n_e)
        .transpose(0, 2, 1, 3)
        .reshape(n_z, rows // n_h, half // n_e)
        .astype(jnp.bfloat16)
    )
    total = 0.0
    for j in range(n_z):
        pairs = []
        for a in range(n_z):
            m = (a + j) % n_z
            for c in range(CORES):
                for d in range(n_dp):
                    source = (a * CORES + c) * n_dp + d
                    goal = (d * n_h + m // n_e) * n_dp + c * n_e + m % n_e
                    pairs.append((source, goal))
        block = lax.ppermute(pick(pieces, (z + j) % n_z), ("seq", "dp"), pairs)
        total = total + block.astype(jnp.float32)
    return total


def sum_all(term, n_seq, n_dp):
    total = term + swap_seq(term, n_seq, 1)
    term = total
    for k in range(1, n_seq // CORES):
        total = total + swap_seq(term, n_seq, CORES * k)
    term = total
    for k in range(1, n_dp):
        total = total + swap_dp(term, n_dp, k)
    return total


def assemble_kernel(place_ref, own_ref, mine_ref, mate_ref, normed_ref, up_ref, act_ref, slope_ref):
    rows = own_ref.shape[0]
    half = rows // CORES
    dp, core = place_ref[0], place_ref[1]
    up_ref[pl.ds(pl.multiple_of(dp * rows, PIECE), rows), :] = own_ref[...]
    for k in range(mine_ref.shape[0]):
        base = (dp ^ (k + 1)) * rows
        for ref, which in ((mine_ref, core), (mate_ref, 1 - core)):
            up_ref[pl.ds(pl.multiple_of(base + which * half, PIECE), half), :] = ref[k]
    pre_act = contract(normed_ref[...], up_ref[...], 1, 0)
    sig_gate = jax.nn.sigmoid(1.702 * pre_act)
    act_ref[...] = (pre_act * sig_gate).astype(jnp.bfloat16)
    slope_ref[...] = sig_gate + 1.702 * pre_act * sig_gate * (1.0 - sig_gate)


def assemble(place, own, mine, mate, normed_all):
    tokens, feat = normed_all.shape
    cols = own.shape[1]
    return vmem_call(
        assemble_kernel,
        (
            jax.ShapeDtypeStruct((feat, cols), jnp.bfloat16),
            jax.ShapeDtypeStruct((tokens, cols), jnp.bfloat16),
            jax.ShapeDtypeStruct((tokens, cols), jnp.float32),
        ),
        [pltpu.SMEM] + [pltpu.VMEM] * 4,
        2 * tokens * feat * cols,
    )(place, own, mine, mate, normed_all)


def store_by_core(core, value, which, keep_ref, give_ref, index):
    @pl.when(core == which)
    def _():
        keep_ref[index] = value

    @pl.when(core != which)
    def _():
        give_ref[index] = value


def down_kernel(place_ref, act_ref, rows_ref, keep_ref, give_ref):
    n_dp, half, width = keep_ref.shape
    term = contract(act_ref[...], rows_ref[...], 0, 0).astype(jnp.bfloat16)
    for which in range(CORES):
        for d in range(n_dp):
            piece = term[which * half : (which + 1) * half, d * width : (d + 1) * width]
            store_by_core(place_ref[1], piece, which, keep_ref, give_ref, d)


def down_pieces(place, act_low, rows_all, n_dp):
    tokens, feat = rows_all.shape
    cols = act_low.shape[1]
    piece = jax.ShapeDtypeStruct((n_dp, cols // CORES, feat // n_dp), jnp.bfloat16)
    return vmem_call(
        down_kernel, (piece, piece), [pltpu.SMEM] + [pltpu.VMEM] * 2, 2 * tokens * feat * cols
    )(place, act_low, rows_all)


def hidden_kernel(
    rows_ref, down_ref, slope_ref, up_ref, normed_ref, gain_ref, pre_ref, own_ref, *rest
):
    tokens = own_ref.shape[0]
    d_act = contract(rows_ref[...], down_ref[...], 1, 1)
    d_pre = (d_act * slope_ref[...]).astype(jnp.bfloat16)
    pre_ref[...] = d_pre
    part = contract(d_pre, up_ref[...], 1, 1)
    own_ref[...] = part[:tokens]
    for k, ref in enumerate(rest[:-1]):
        ref[...] = part[(k + 1) * tokens : (k + 2) * tokens].astype(jnp.bfloat16)
    term = jnp.sum(part * normed_ref[...].astype(jnp.float32), axis=0, keepdims=True)
    rest[-1][...] = term / gain_ref[...].astype(jnp.float32)


def hidden_grads(rows_all, w_down, slope, up_cols, normed_all, gain, tokens):
    total, feat = rows_all.shape
    cols = slope.shape[1]
    return vmem_call(
        hidden_kernel,
        (
            jax.ShapeDtypeStruct((total, cols), jnp.bfloat16),
            jax.ShapeDtypeStruct((tokens, feat), jnp.float32),
        )
        + tuple(
            jax.ShapeDtypeStruct((tokens, feat), jnp.bfloat16) for _ in range(total // tokens - 1)
        )
        + (jax.ShapeDtypeStruct((1, feat), jnp.float32),),
        [pltpu.VMEM] * 6,
        4 * total * feat * cols,
    )(rows_all, w_down, slope, up_cols, normed_all, gain)


def up_kernel(place_ref, normed_ref, pre_ref, keep_ref, give_ref):
    n_z, rows, cols = keep_ref.shape
    term = contract(normed_ref[...], pre_ref[...], 0, 0).astype(jnp.bfloat16)
    for z in range(n_z):
        for which in range(CORES):
            start = (z * CORES + which) * rows
            piece = term[start : start + rows]
            store_by_core(place_ref[1], piece, which, keep_ref, give_ref, z)


def up_pieces(place, normed_all, d_pre, n_z):
    tokens, feat = normed_all.shape
    cols = d_pre.shape[1]
    piece = jax.ShapeDtypeStruct((n_z, feat // n_z // CORES, cols), jnp.bfloat16)
    return vmem_call(
        up_kernel, (piece, piece), [pltpu.SMEM] + [pltpu.VMEM] * 2, 2 * tokens * feat * cols
    )(place, normed_all, d_pre)


def wide_sum(*terms):
    return sum(term.astype(jnp.float32) for term in terms)


def as_rows(vector, width):
    high = lax.reduce_precision(vector, 8, 7)
    low = vector - high
    rows = jnp.concatenate([high.reshape(-1, width), low.reshape(-1, width)], axis=0)
    return jnp.pad(rows.astype(jnp.bfloat16), ((0, PIECE - rows.shape[0]), (0, 0)))


def from_rows(rows, length):
    count = length // rows.shape[1]
    return wide_sum(rows[:count], rows[count : 2 * count]).reshape(length)


def weight_sums(up_both, down_both, gain_part, n_seq, n_dp, seq, dp):
    n_z, z = n_seq // CORES, seq // CORES
    up_keep, up_give = up_both
    down_keep, down_give = down_both
    feat = gain_part.shape[0]
    flat = up_give.reshape(-1, up_give.shape[2])
    sent = jnp.concatenate([flat, as_rows(gain_part, flat.shape[1])], axis=0)
    down_mate = swap_seq(down_give, n_seq, 1)
    up_got = swap_seq(sent, n_seq, 1)
    up_mate = up_got[: flat.shape[0]].reshape(up_give.shape)
    gain_part = gain_part + from_rows(up_got[flat.shape[0] :], feat)

    half, width = down_keep.shape[1:]
    gain_rows = as_rows(gain_part, width)

    def down_piece(index):
        piece = wide_sum(pick(down_keep, index), pick(down_mate, index)).astype(jnp.bfloat16)
        return jnp.concatenate([piece, gain_rows], axis=0)

    planes = jnp.stack(
        [down_piece(dp)] + [swap_dp(down_piece(dp ^ k), n_dp, k) for k in range(1, n_dp)]
    )
    gain_part = sum(from_rows(planes[k, half:], feat) for k in range(n_dp))
    gain_rows = as_rows(gain_part, width)

    def up_piece(index):
        return wide_sum(pick(up_keep, index), pick(up_mate, index))

    up_total = up_piece(z)
    for k in reversed(range(1, n_z)):
        block = swap_seq(up_piece(z ^ k).astype(jnp.bfloat16), n_seq, CORES * k)
        up_total = up_total + block.astype(jnp.float32)

    down_total = pick(planes, dp ^ z)[:half].astype(jnp.float32)
    for k in reversed(range(1, n_z)):
        piece = jnp.concatenate([pick(planes, dp ^ z ^ k)[:half], gain_rows], axis=0)
        block = swap_seq(piece, n_seq, CORES * k)
        down_total = down_total + block[:half].astype(jnp.float32)
        gain_part = gain_part + from_rows(block[half:], feat)
    return up_total, down_total, gain_part


def per_device(
    queries,
    key_rows,
    value_rows,
    resid_in,
    llm_grad,
    vision_slot,
    window_mask,
    w_up,
    w_down,
    norm_gain,
):
    n_seq = lax.axis_size("seq")
    n_dp = lax.axis_size("dp")
    seq = lax.axis_index("seq")
    dp = lax.axis_index("dp")
    core = seq % CORES
    tokens, feat_dim = queries.shape[1:]

    send, grad_rows = owner_rows(llm_grad[0], vision_slot, n_seq, tokens)
    w_up, norm_gain, send = lax.optimization_barrier((w_up, norm_gain, send))
    gain_full = gather_gain(norm_gain, n_dp, dp)
    own, mine, mate = fetch_up(w_up, n_dp, n_seq, dp, core)

    attn_probs, attn_out, normal_unit, inverse = forward(
        window_mask[0], queries[0], key_rows[0], value_rows[0], resid_in[0]
    )
    normed = (normal_unit * gain_full.astype(jnp.float32)).astype(jnp.bfloat16)

    normed_all = gather_tokens(normed, n_dp)
    rows_all = gather_tokens(grad_rows, n_dp)
    if n_seq == CORES * n_dp:
        place = jnp.stack([dp, core]).astype(jnp.int32)
        up_cols, act_low, slope = assemble(place, own, mine, mate, normed_all)
        down_both = down_pieces(place, act_low, rows_all, n_dp)
        d_pre, d_own, *d_parts, gain_part = hidden_grads(
            rows_all, w_down, slope, up_cols, normed_all, gain_full[None], tokens
        )
        d_got = [swap_dp(part, n_dp, k + 1) for k, part in enumerate(d_parts)]
        up_both = up_pieces(place, normed_all, d_pre, n_seq // CORES)
        up_panel, down_panel, gain_total = weight_sums(
            up_both, down_both, gain_part[0], n_seq, n_dp, seq, dp
        )
    else:
        up_cols = join_up(own, mine, mate, n_dp, dp, core)
        pre_act = contract(normed_all, up_cols, 1, 0)
        sig_gate = jax.nn.sigmoid(1.702 * pre_act)
        act_low = (pre_act * sig_gate).astype(jnp.bfloat16)
        d_act = contract(rows_all, w_down, 1, 1)
        d_pre = (d_act * (sig_gate + 1.702 * pre_act * sig_gate * (1.0 - sig_gate))).astype(
            jnp.bfloat16
        )
        d_part = contract(d_pre, up_cols, 1, 1)
        d_own = d_part[:tokens]
        d_got = [
            swap_dp(d_part[k * tokens : (k + 1) * tokens].astype(jnp.bfloat16), n_dp, k)
            for k in range(1, n_dp)
        ]
        up_panel = scatter_up(contract(normed_all, d_pre, 0, 0), n_seq, seq)
        down_panel = scatter_down(contract(act_low, rows_all, 0, 0), n_seq, n_dp, seq)
        gain_part = jnp.sum(d_part * normed_all.astype(jnp.float32), axis=0)
        gain_total = sum_all(gain_part / gain_full.astype(jnp.float32), n_seq, n_dp)

    grad_query, grad_key, grad_value, grad_resid = backward(
        d_own,
        jnp.stack(d_got),
        grad_rows,
        normal_unit,
        inverse,
        gain_full[None],
        attn_probs,
        attn_out,
        queries[0],
        key_rows[0],
        value_rows[0],
    )
    factor = 1.0 / math.sqrt(n_dp * n_seq * tokens)
    return (
        grad_query[None],
        grad_key[None],
        grad_value[None],
        grad_resid[None],
        (up_panel * factor).astype(jnp.bfloat16),
        (down_panel * factor).astype(jnp.bfloat16),
        gain_total * factor,
    )


def solution(mesh):
    in_specs = (
        P("dp", "seq", None),
        P("dp", "seq", None),
        P("dp", "seq", None),
        P("dp", "seq", None),
        P("dp", "seq", None),
        P("dp", "seq"),
        P("dp", "seq", None),
        P("dp", None),
        P("dp", None),
        P("dp"),
    )
    out_specs = (
        P("dp", "seq", None),
        P("dp", "seq", None),
        P("dp", "seq", None),
        P("dp", "seq", None),
        P("seq", "dp"),
        P("seq", "dp"),
        P(),
    )
    return jax.shard_map(
        per_device, mesh=mesh, in_specs=in_specs, out_specs=out_specs, check_vma=False
    )
```

```python
import math

import jax
import jax.numpy as jnp
from jax import lax
from jax.experimental import pallas as pl
from jax.experimental.pallas import tpu as pltpu
from jax.sharding import PartitionSpec as P

HEADS = 16
HDIM = 80
BLK = 64
PIECE = 16
CORES = 2
LANES = 128
VMEM_BYTES = 32 * 1024 * 1024


def vmem_call(body, out_shape, in_spaces, flops):
    return pl.pallas_call(
        body,
        out_shape=out_shape,
        in_specs=[pl.BlockSpec(memory_space=space) for space in in_spaces],
        out_specs=jax.tree.map(lambda _: pl.BlockSpec(memory_space=pltpu.VMEM), out_shape),
        compiler_params=pltpu.CompilerParams(vmem_limit_bytes=VMEM_BYTES),
        cost_estimate=pl.CostEstimate(flops=flops, bytes_accessed=4 << 20, transcendentals=0),
    )


def contract(left, right, left_dim, right_dim):
    return lax.dot_general(
        left, right, (((left_dim,), (right_dim,)), ((), ())), preferred_element_type=jnp.float32
    )


def pick(blocks, index):
    return lax.dynamic_index_in_dim(blocks, index, 0, keepdims=False)


def swap_dp(block, count, step):
    return lax.ppermute(block, "dp", [(i, i ^ step) for i in range(count)])


def swap_seq(block, count, step):
    return lax.ppermute(block, "seq", [(i, i ^ step) for i in range(count)])


def fetch_pieces(w_up, n_dp, n_seq, dp, core):
    rows, ff = w_up.shape
    cols, half = ff // n_dp, rows // CORES
    own = lax.dynamic_slice(w_up, (0, dp * cols), (rows, cols))
    got = []
    for k in range(1, n_dp):
        piece = lax.dynamic_slice(w_up, (core * half, (dp ^ k) * cols), (half, cols))
        got.append(swap_dp(piece, n_dp, k))
    mine = jnp.stack(got)
    return own, mine, swap_seq(mine, n_seq, 1)


def join_up(own, mine, mate, n_dp, dp, core):
    low = jnp.where(core == 0, mine, mate)
    high = jnp.where(core == 0, mate, mine)
    pairs = jnp.concatenate([low, high], axis=1)
    full = jnp.concatenate([own[None], pairs], axis=0)
    return full[dp ^ jnp.arange(n_dp)].reshape(-1, own.shape[1])


def gather_gain(norm_gain, n_dp, dp):
    parts = jnp.stack(
        [norm_gain] + [swap_dp(norm_gain, n_dp, k) for k in range(1, n_dp)]
    )
    return parts[dp ^ jnp.arange(n_dp)].reshape(-1)


def send_kernel(n_seq, capacity, per_owner, slot_ref, rows_ref, out_ref):
    length, feat = rows_ref.shape
    out_ref[...] = jnp.zeros(out_ref.shape, jnp.bfloat16)
    row = lax.broadcasted_iota(jnp.int32, (PIECE, LANES), 0)
    firsts = [slot_ref[0, t * PIECE] for t in range(length // PIECE)]
    owners = [jnp.where(f >= 0, f // (per_owner * PIECE), n_seq) for f in firsts]
    for t, first in enumerate(firsts):
        rank = jnp.int32(0)
        for earlier in range(t):
            rank = rank + jnp.where(owners[earlier] == owners[t], 1, 0)

        @pl.when(first >= 0)
        def _(t=t, first=first, rank=rank):
            place = pl.ds(pl.multiple_of(rank * PIECE, PIECE), PIECE)
            out_ref[owners[t], place, :feat] = rows_ref[t * PIECE : (t + 1) * PIECE, :]
            landing = first % (per_owner * PIECE) + row + 1
            out_ref[owners[t], place, feat:] = landing.astype(jnp.float32).astype(jnp.bfloat16)


def land_kernel(got_ref, out_ref):
    tokens, feat = out_ref.shape
    slots = got_ref.shape[0]
    marks = got_ref[:, feat:].astype(jnp.float32)
    goal = lax.broadcasted_iota(jnp.int32, (slots, LANES), 1) + 1
    rows = got_ref[:, :feat]
    for part in range(tokens // LANES):
        select = (marks == (goal + part * LANES).astype(jnp.float32)).astype(jnp.bfloat16)
        out_ref[part * LANES : (part + 1) * LANES, :] = contract(select, rows, 0, 0).astype(
            jnp.bfloat16
        )


def owner_rows(llm_rows, slot_ids, n_seq, tokens):
    length, feat = llm_rows.shape
    per_owner = tokens // PIECE
    capacity = 1 + (per_owner + n_seq - 2) // n_seq
    rows = capacity * PIECE
    send = vmem_call(
        lambda *refs: send_kernel(n_seq, capacity, per_owner, *refs),
        jax.ShapeDtypeStruct((n_seq, rows, feat + LANES), jnp.bfloat16),
        [pltpu.SMEM, pltpu.VMEM],
        1 << 20,
    )(slot_ids, llm_rows)
    got = lax.all_to_all(send, "seq", split_axis=0, concat_axis=0, tiled=True)
    landed = vmem_call(
        land_kernel,
        jax.ShapeDtypeStruct((tokens, feat), jnp.bfloat16),
        [pltpu.VMEM],
        1 << 26,
    )(got.reshape(n_seq * rows, feat + LANES))
    return landed


def head_lanes(head, rows, width, start):
    lane = lax.broadcasted_iota(jnp.int32, (rows, width), 1) + start
    return (lane >= head * HDIM) & (lane < (head + 1) * HDIM)


def span_of(head):
    start = head * HDIM // LANES * LANES
    stop = -(-(head + 1) * HDIM // LANES) * LANES
    return start, stop


def masked_head(ref, head):
    start, stop = span_of(head)
    block = ref[:, start:stop]
    return jnp.where(head_lanes(head, block.shape[0], stop - start, start), block, 0).astype(
        block.dtype
    )


def add_span(total, head, part):
    start, stop = span_of(head)
    for at in range(start, stop, LANES):
        piece = part[:, at - start : at - start + LANES]
        total[at] = total[at] + piece if at in total else piece


def forward_kernel(
    mask_ref, q_ref, k_ref, v_ref, resid_ref, probs_ref, out_ref, unit_ref, inverse_ref
):
    tokens, feat = q_ref.shape
    scale = 1.0 / math.sqrt(HDIM)
    row = lax.broadcasted_iota(jnp.int32, (tokens, tokens), 0) // BLK
    col = lax.broadcasted_iota(jnp.int32, (tokens, tokens), 1) // BLK
    allowed = row == col
    for i in range(tokens // BLK):
        for j in range(tokens // BLK):
            if i != j:
                allowed = allowed | ((row == i) & (col == j) & (mask_ref[i, j] > 0))
    total = {}
    for head in range(HEADS):
        start, stop = span_of(head)
        scores = contract(q_ref[:, start:stop], masked_head(k_ref, head), 1, 1) * scale
        scores = jnp.where(allowed, scores, -jnp.inf)
        exp_terms = jnp.exp(scores - jnp.max(scores, axis=1, keepdims=True))
        probs = exp_terms / jnp.sum(exp_terms, axis=1, keepdims=True)
        probs_ref[head] = probs
        add_span(total, head, contract(probs.astype(jnp.bfloat16), masked_head(v_ref, head), 1, 0))
    for at, value in total.items():
        out_ref[:, at : at + LANES] = value.astype(jnp.bfloat16)
    hidden = resid_ref[...].astype(jnp.float32) + out_ref[...].astype(jnp.float32)
    center = jnp.mean(hidden, axis=1, keepdims=True)
    hidden = hidden - center
    variance = jnp.mean(jnp.square(hidden), axis=1, keepdims=True)
    inverse = lax.rsqrt(variance + 1e-06)
    unit_ref[...] = hidden * inverse
    inverse_ref[...] = jnp.broadcast_to(inverse, inverse_ref.shape)


def forward(mask, query, key_block, value_block, resid):
    tokens, feat = query.shape
    return vmem_call(
        forward_kernel,
        (
            jax.ShapeDtypeStruct((HEADS, tokens, tokens), jnp.float32),
            jax.ShapeDtypeStruct((tokens, feat), jnp.bfloat16),
            jax.ShapeDtypeStruct((tokens, feat), jnp.float32),
            jax.ShapeDtypeStruct((tokens, LANES), jnp.float32),
        ),
        [pltpu.SMEM] + [pltpu.VMEM] * 4,
        1 << 31,
    )(mask, query, key_block, value_block, resid)


def backward_kernel(
    got_ref,
    rows_ref,
    unit_ref,
    inverse_ref,
    gain_ref,
    probs_ref,
    out_ref,
    q_ref,
    k_ref,
    v_ref,
    gq_ref,
    gk_ref,
    gv_ref,
    gr_ref,
):
    tokens, feat = q_ref.shape
    scale = 1.0 / math.sqrt(HDIM)
    d_normed = sum(got_ref[part].astype(jnp.float32) for part in range(got_ref.shape[0]))
    unit = unit_ref[...]
    d_unit = d_normed * gain_ref[...].astype(jnp.float32)
    d_hidden = inverse_ref[:, :1] * (
        d_unit
        - jnp.mean(d_unit, axis=1, keepdims=True)
        - unit * jnp.mean(d_unit * unit, axis=1, keepdims=True)
    )
    gr_ref[...] = (rows_ref[...].astype(jnp.float32) + d_hidden).astype(jnp.bfloat16)
    totals = ({}, {}, {})
    for head in range(HEADS):
        start, stop = span_of(head)
        probs = probs_ref[head]
        grad = masked_head(gr_ref, head)
        add_span(totals[0], head, contract(probs.astype(jnp.bfloat16), grad, 0, 0))
        d_probs = contract(grad, v_ref[:, start:stop], 1, 1)
        delta = jnp.sum(
            grad.astype(jnp.float32) * out_ref[:, start:stop].astype(jnp.float32),
            axis=1,
            keepdims=True,
        )
        d_scores = (probs * (d_probs - delta) * scale).astype(jnp.bfloat16)
        add_span(totals[1], head, contract(d_scores, masked_head(k_ref, head), 1, 0))
        add_span(totals[2], head, contract(d_scores, masked_head(q_ref, head), 0, 0))
    for ref, total in zip((gv_ref, gq_ref, gk_ref), totals):
        for at, value in total.items():
            ref[:, at : at + LANES] = value.astype(jnp.bfloat16)


def backward(*operands):
    tokens, feat = operands[1].shape
    return vmem_call(
        backward_kernel,
        tuple(jax.ShapeDtypeStruct((tokens, feat), jnp.bfloat16) for _ in range(4)),
        [pltpu.VMEM] * 10,
        1 << 32,
    )(*operands)


def gather_tokens(block, n_dp):
    return jnp.concatenate([block] + [swap_dp(block, n_dp, k) for k in range(1, n_dp)], axis=0)


def scatter_up(term, n_seq, seq):
    n_z, core, z = n_seq // CORES, seq % CORES, seq // CORES
    rows, cols = term.shape
    pieces = term.reshape(n_z, CORES, rows // n_seq, cols)
    keep = lax.dynamic_index_in_dim(pieces, core, 1, keepdims=False)
    give = lax.dynamic_index_in_dim(pieces, 1 - core, 1, keepdims=False)
    both = (
        keep.astype(jnp.float32) + swap_seq(give.astype(jnp.bfloat16), n_seq, 1).astype(jnp.float32)
    ).astype(jnp.bfloat16)
    total = pick(both, z).astype(jnp.float32)
    for k in reversed(range(1, n_z)):
        total = total + swap_seq(pick(both, z ^ k), n_seq, CORES * k).astype(jnp.float32)
    return total


def scatter_down(term, n_seq, n_dp, seq):
    n_z, core, z = n_seq // CORES, seq % CORES, seq // CORES
    rows, cols = term.shape
    n_h, n_e = n_seq // n_dp, n_dp // CORES
    half = cols // CORES
    keep = lax.dynamic_slice(term, (0, core * half), (rows, half))
    give = lax.dynamic_slice(term, (0, (1 - core) * half), (rows, half))
    both = keep + swap_seq(give.astype(jnp.bfloat16), n_seq, 1).astype(jnp.float32)
    pieces = (
        both.reshape(n_h, rows // n_h, n_e, half // n_e)
        .transpose(0, 2, 1, 3)
        .reshape(n_z, rows // n_h, half // n_e)
        .astype(jnp.bfloat16)
    )
    total = 0.0
    for j in range(n_z):
        pairs = []
        for a in range(n_z):
            m = (a + j) % n_z
            for c in range(CORES):
                for d in range(n_dp):
                    source = (a * CORES + c) * n_dp + d
                    goal = (d * n_h + m // n_e) * n_dp + c * n_e + m % n_e
                    pairs.append((source, goal))
        block = lax.ppermute(pick(pieces, (z + j) % n_z), ("seq", "dp"), pairs)
        total = total + block.astype(jnp.float32)
    return total


def sum_all(term, n_seq, n_dp):
    total = term + swap_seq(term, n_seq, 1)
    term = total
    for k in range(1, n_seq // CORES):
        total = total + swap_seq(term, n_seq, CORES * k)
    term = total
    for k in range(1, n_dp):
        total = total + swap_dp(term, n_dp, k)
    return total


def fetch_kernel(place_ref, up_ref, gain_ref, out_ref):
    n_dp, _, cols = out_ref.shape
    half = up_ref.shape[0] // CORES
    rows = pl.ds(pl.multiple_of(place_ref[1] * half, PIECE), half)
    gain = gain_ref[...].astype(jnp.float32)
    gain = jnp.concatenate([gain, jnp.zeros((1, cols - gain.shape[1]), jnp.float32)], axis=1)
    gain = jnp.broadcast_to(gain, (PIECE, cols)).astype(jnp.bfloat16)
    for d in range(n_dp):
        out_ref[d, :half, :] = up_ref[rows, d * cols : (d + 1) * cols]
        out_ref[d, half:, :] = gain


def fetch_up(place, w_up, norm_gain, n_dp):
    rows, ff = w_up.shape
    shape = (n_dp, rows // CORES + PIECE, ff // n_dp)
    sent = vmem_call(
        fetch_kernel,
        jax.ShapeDtypeStruct(shape, jnp.bfloat16),
        [pltpu.SMEM, pltpu.VMEM, pltpu.VMEM],
        1 << 20,
    )(place, w_up, norm_gain[None])
    return lax.all_to_all(sent, "dp", split_axis=0, concat_axis=0, tiled=True)


def assemble_kernel(place_ref, mine_ref, mate_ref, *refs):
    *normed_refs, up_ref, act_ref, slope_ref, flip_ref, all_ref = refs
    n_dp, half, cols = mine_ref.shape
    half = half - PIECE
    core = place_ref[1]
    for d in range(n_dp):
        for ref, which in ((mine_ref, core), (mate_ref, 1 - core)):
            base = (d * CORES + which) * half
            up_ref[pl.ds(pl.multiple_of(base, PIECE), half), :] = ref[d, :half, :]
    tokens = normed_refs[0].shape[0]
    for k, ref in enumerate(normed_refs):
        all_ref[k * tokens : (k + 1) * tokens, :] = ref[...]
        flip_ref[:, k * tokens : (k + 1) * tokens] = ref[...].T
    pre_act = contract(all_ref[...], up_ref[...], 1, 0)
    sig_gate = jax.nn.sigmoid(1.702 * pre_act)
    act_ref[...] = (pre_act * sig_gate).astype(jnp.bfloat16).T
    slope_ref[...] = sig_gate + 1.702 * pre_act * sig_gate * (1.0 - sig_gate)


def assemble(place, mine, mate, normed_blocks):
    tokens, feat = normed_blocks[0].shape
    total = tokens * len(normed_blocks)
    cols = mine.shape[2]
    return vmem_call(
        assemble_kernel,
        (
            jax.ShapeDtypeStruct((feat, cols), jnp.bfloat16),
            jax.ShapeDtypeStruct((cols, total), jnp.bfloat16),
            jax.ShapeDtypeStruct((total, cols), jnp.float32),
            jax.ShapeDtypeStruct((feat, total), jnp.bfloat16),
            jax.ShapeDtypeStruct((total, feat), jnp.bfloat16),
        ),
        [pltpu.SMEM] + [pltpu.VMEM] * (2 + len(normed_blocks)),
        2 * total * feat * cols,
    )(place, mine, mate, *normed_blocks)


def store_by_core(core, value, which, keep_ref, give_ref, index):
    @pl.when(core == which)
    def _():
        keep_ref[index] = value

    @pl.when(core != which)
    def _():
        give_ref[index] = value


def up_kernel(
    place_ref, rows_ref, down_ref, slope_ref, flip_ref, pre_ref, keep_ref, give_ref
):
    n_z, rows, cols = keep_ref.shape
    d_act = contract(rows_ref[...], down_ref[...], 1, 1)
    d_pre = (d_act * slope_ref[...]).astype(jnp.bfloat16)
    pre_ref[...] = d_pre
    term = contract(flip_ref[...], d_pre, 1, 0).astype(jnp.bfloat16)
    for z in range(n_z):
        for which in range(CORES):
            start = (z * CORES + which) * rows
            piece = term[start : start + rows]
            store_by_core(place_ref[1], piece, which, keep_ref, give_ref, z)


def up_pieces(place, rows_all, w_down, slope, normed_flip, n_z):
    total, feat = rows_all.shape
    cols = slope.shape[1]
    piece = jax.ShapeDtypeStruct((n_z, feat // n_z // CORES, cols), jnp.bfloat16)
    return vmem_call(
        up_kernel,
        (jax.ShapeDtypeStruct((total, cols), jnp.bfloat16), piece, piece),
        [pltpu.SMEM] + [pltpu.VMEM] * 4,
        4 * total * feat * cols,
    )(place, rows_all, w_down, slope, normed_flip)


def down_kernel(place_ref, act_ref, rows_ref, keep_ref, give_ref):
    n_dp, half, width = keep_ref.shape
    term = contract(act_ref[...], rows_ref[...], 1, 0).astype(jnp.bfloat16)
    for which in range(CORES):
        for d in range(n_dp):
            piece = term[which * half : (which + 1) * half, d * width : (d + 1) * width]
            store_by_core(place_ref[1], piece, which, keep_ref, give_ref, d)


def down_pieces(place, act_flip, rows_all, n_dp):
    tokens, feat = rows_all.shape
    cols = act_flip.shape[0]
    piece = jax.ShapeDtypeStruct((n_dp, cols // CORES, feat // n_dp), jnp.bfloat16)
    return vmem_call(
        down_kernel, (piece, piece), [pltpu.SMEM] + [pltpu.VMEM] * 2, 2 * tokens * feat * cols
    )(place, act_flip, rows_all)


def part_kernel(place_ref, pre_ref, up_ref, normed_ref, gain_ref, parts_ref, term_ref):
    n_dp, tokens, _ = parts_ref.shape
    part = contract(pre_ref[...], up_ref[...], 1, 1)
    for k in range(n_dp):
        rows = part[k * tokens : (k + 1) * tokens]
        parts_ref[place_ref[0] ^ k] = rows.astype(jnp.bfloat16)
    term = jnp.sum(part * normed_ref[...].astype(jnp.float32), axis=0, keepdims=True)
    term_ref[...] = term / gain_ref[...].astype(jnp.float32)


def normed_parts(place, d_pre, up_cols, normed_all, gain, n_dp):
    total, feat = normed_all.shape
    return vmem_call(
        part_kernel,
        (
            jax.ShapeDtypeStruct((n_dp, total // n_dp, feat), jnp.bfloat16),
            jax.ShapeDtypeStruct((1, feat), jnp.float32),
        ),
        [pltpu.SMEM] + [pltpu.VMEM] * 4,
        2 * total * feat * d_pre.shape[1],
    )(place, d_pre, up_cols, normed_all, gain)


def wide_sum(*terms):
    return sum(term.astype(jnp.float32) for term in terms)


def to_rows(vector, width):
    high = vector.astype(jnp.bfloat16).astype(jnp.float32)
    rows = [
        part[:, at : at + width]
        for part in (high, vector - high)
        for at in range(0, vector.shape[1], width)
    ]
    rows.append(jnp.zeros((PIECE - len(rows), width), jnp.float32))
    return jnp.concatenate(rows, axis=0).astype(jnp.bfloat16)


def plane_kernel(keep_ref, mate_ref, term_ref, other_ref, out_ref):
    n_dp, half, width = keep_ref.shape
    rows = to_rows(term_ref[...] + other_ref[...], width)
    for d in range(n_dp):
        out_ref[d, :half, :] = wide_sum(keep_ref[d], mate_ref[d]).astype(jnp.bfloat16)
        out_ref[d, half:, :] = rows


def rise_kernel(place_ref, got_ref, own_ref, *send_refs):
    half = got_ref.shape[1] - PIECE
    z = place_ref[2]
    rows = wide_sum(*(got_ref[d, half:, :] for d in range(got_ref.shape[0])))
    count = got_ref.shape[0]
    total = rows[:count] + rows[count : 2 * count]
    high = total.astype(jnp.bfloat16).astype(jnp.float32)
    pad = jnp.zeros((PIECE - 2 * count, rows.shape[1]), jnp.float32)
    rows = jnp.concatenate([high, total - high, pad], axis=0).astype(jnp.bfloat16)
    for k, ref in enumerate((own_ref,) + send_refs):
        ref[:half, :] = got_ref[z ^ k, :half, :]
        ref[half:, :] = rows


def last_kernel(factor, *refs):
    *in_refs, down_ref, gain_ref = refs
    half = down_ref.shape[0]
    count = gain_ref.shape[0]
    down_ref[...] = (wide_sum(*(ref[:half, :] for ref in in_refs)) * factor).astype(jnp.bfloat16)
    rows = wide_sum(*(ref[half:, :] for ref in in_refs))
    gain_ref[...] = (rows[:count] + rows[count : 2 * count]) * factor


def weight_sums(place, up_both, down_both, term, factor, n_seq, n_dp, seq):
    n_z, z = n_seq // CORES, seq // CORES
    up_keep, up_give = up_both
    down_keep, down_give = down_both
    up_mate = swap_seq(up_give, n_seq, 1)
    down_mate = swap_seq(down_give, n_seq, 1)
    other = swap_seq(term, n_seq, 1)

    def up_piece(index):
        return wide_sum(pick(up_keep, index), pick(up_mate, index))

    up_total = up_piece(z)
    for k in reversed(range(1, n_z)):
        block = swap_seq(up_piece(z ^ k).astype(jnp.bfloat16), n_seq, CORES * k)
        up_total = up_total + block.astype(jnp.float32)

    half, width = down_keep.shape[1:]
    planes = vmem_call(
        plane_kernel,
        jax.ShapeDtypeStruct((n_dp, half + PIECE, width), jnp.bfloat16),
        [pltpu.VMEM] * 4,
        1 << 20,
    )(down_keep, down_mate, term, other)
    planes = lax.all_to_all(planes, "dp", split_axis=0, concat_axis=0, tiled=True)
    piece = jax.ShapeDtypeStruct((half + PIECE, width), jnp.bfloat16)
    own, *sends = vmem_call(
        rise_kernel, (piece,) * n_z, [pltpu.SMEM, pltpu.VMEM], 1 << 20
    )(place, planes)
    got = [swap_seq(block, n_seq, CORES * (k + 1)) for k, block in enumerate(sends)]
    down_total, gain_total = vmem_call(
        lambda *refs: last_kernel(factor, *refs),
        (
            jax.ShapeDtypeStruct((half, width), jnp.bfloat16),
            jax.ShapeDtypeStruct((n_dp, width), jnp.float32),
        ),
        [pltpu.VMEM] * n_z,
        1 << 20,
    )(own, *got)
    return (up_total * factor).astype(jnp.bfloat16), down_total, gain_total.reshape(-1)


def per_device(
    queries,
    key_rows,
    value_rows,
    resid_in,
    llm_grad,
    vision_slot,
    window_mask,
    w_up,
    w_down,
    norm_gain,
):
    n_seq = lax.axis_size("seq")
    n_dp = lax.axis_size("dp")
    seq = lax.axis_index("seq")
    dp = lax.axis_index("dp")
    core = seq % CORES
    tokens, feat_dim = queries.shape[1:]

    factor = 1.0 / math.sqrt(n_dp * n_seq * tokens)
    place = jnp.stack([dp, core, seq // CORES]).astype(jnp.int32)
    quick = n_seq == CORES * n_dp

    if quick:
        mine = fetch_up(place, w_up, norm_gain, n_dp)
        mate = swap_seq(mine, n_seq, 1)
        gain_full = mine[:, -1, : norm_gain.shape[0]].reshape(-1)
    else:
        gain_full = gather_gain(norm_gain, n_dp, dp)
        own, mine, mate = fetch_pieces(w_up, n_dp, n_seq, dp, core)
    grad_rows = owner_rows(llm_grad[0], vision_slot, n_seq, tokens)

    attn_probs, attn_out, normal_unit, inverse = forward(
        window_mask[0], queries[0], key_rows[0], value_rows[0], resid_in[0]
    )
    normed = (normal_unit * gain_full.astype(jnp.float32)).astype(jnp.bfloat16)
    normed_blocks = [normed] + [swap_dp(normed, n_dp, k) for k in range(1, n_dp)]
    rows_all = gather_tokens(grad_rows, n_dp)
    if quick:
        up_cols, act_flip, slope, normed_flip, normed_all = assemble(
            place, mine, mate, normed_blocks
        )
        d_pre, *up_both = up_pieces(place, rows_all, w_down, slope, normed_flip, n_seq // CORES)
        down_both = down_pieces(place, act_flip, rows_all, n_dp)
        parts, term = normed_parts(place, d_pre, up_cols, normed_all, gain_full[None], n_dp)
        d_got = lax.all_to_all(parts, "dp", split_axis=0, concat_axis=0, tiled=True)
        grad_up, grad_down, grad_gain = weight_sums(
            place, up_both, down_both, term, factor, n_seq, n_dp, seq
        )
    else:
        normed_all = jnp.concatenate(normed_blocks, axis=0)
        up_cols = join_up(own, mine, mate, n_dp, dp, core)
        pre_act = contract(normed_all, up_cols, 1, 0)
        sig_gate = jax.nn.sigmoid(1.702 * pre_act)
        act_low = (pre_act * sig_gate).astype(jnp.bfloat16)
        d_act = contract(rows_all, w_down, 1, 1)
        d_pre = (d_act * (sig_gate + 1.702 * pre_act * sig_gate * (1.0 - sig_gate))).astype(
            jnp.bfloat16
        )
        d_part = contract(d_pre, up_cols, 1, 1)
        blocks = d_part.astype(jnp.bfloat16).reshape(n_dp, tokens, feat_dim)
        d_got = jnp.stack([blocks[0]] + [swap_dp(blocks[k], n_dp, k) for k in range(1, n_dp)])
        up_sum = scatter_up(contract(normed_all, d_pre, 0, 0), n_seq, seq)
        down_sum = scatter_down(contract(act_low, rows_all, 0, 0), n_seq, n_dp, seq)
        gain_part = jnp.sum(d_part * normed_all.astype(jnp.float32), axis=0)
        grad_gain = factor * sum_all(gain_part / gain_full.astype(jnp.float32), n_seq, n_dp)
        grad_up = (up_sum * factor).astype(jnp.bfloat16)
        grad_down = (down_sum * factor).astype(jnp.bfloat16)

    grad_query, grad_key, grad_value, grad_resid = backward(
        d_got,
        grad_rows,
        normal_unit,
        inverse,
        gain_full[None],
        attn_probs,
        attn_out,
        queries[0],
        key_rows[0],
        value_rows[0],
    )
    return (
        grad_query[None],
        grad_key[None],
        grad_value[None],
        grad_resid[None],
        grad_up,
        grad_down,
        grad_gain,
    )


def solution(mesh):
    in_specs = (
        P("dp", "seq", None),
        P("dp", "seq", None),
        P("dp", "seq", None),
        P("dp", "seq", None),
        P("dp", "seq", None),
        P("dp", "seq"),
        P("dp", "seq", None),
        P("dp", None),
        P("dp", None),
        P("dp"),
    )
    out_specs = (
        P("dp", "seq", None),
        P("dp", "seq", None),
        P("dp", "seq", None),
        P("dp", "seq", None),
        P("seq", "dp"),
        P("seq", "dp"),
        P(),
    )
    return jax.shard_map(
        per_device, mesh=mesh, in_specs=in_specs, out_specs=out_specs, check_vma=False
    )
```

```python
import math

import jax
import jax.numpy as jnp
from jax import lax
from jax.experimental import pallas as pl
from jax.experimental.pallas import tpu as pltpu
from jax.sharding import PartitionSpec as P

HEADS = 16
HDIM = 80
BLK = 64
PIECE = 16
CORES = 2
LANES = 128
VMEM_BYTES = 16 * 1024 * 1024


def vmem_call(body, out_shape, in_spaces, flops):
    def run(*operands):
        places = [i for i, space in enumerate(in_spaces) if space == pl.ANY]
        outs = len(jax.tree.leaves(out_shape))

        def kernel(*refs):
            refs = list(refs)
            ins, rest = refs[: len(in_spaces)], refs[len(in_spaces) :]
            held, sems = rest[outs : outs + len(places)], rest[outs + len(places) :]
            copies = [
                pltpu.make_async_copy(ins[i], held[n], sems[n]) for n, i in enumerate(places)
            ]
            for copy in copies:
                copy.start()
            for copy in copies:
                copy.wait()
            for n, i in enumerate(places):
                ins[i] = held[n]
            body(*ins, *rest[:outs])

        return pl.pallas_call(
            kernel if places else body,
            out_shape=out_shape,
            in_specs=[pl.BlockSpec(memory_space=space) for space in in_spaces],
            out_specs=jax.tree.map(lambda _: pl.BlockSpec(memory_space=pltpu.VMEM), out_shape),
            scratch_shapes=[pltpu.VMEM(operands[i].shape, operands[i].dtype) for i in places]
            + [pltpu.SemaphoreType.DMA for _ in places],
            compiler_params=pltpu.CompilerParams(vmem_limit_bytes=VMEM_BYTES),
            cost_estimate=pl.CostEstimate(
                flops=flops, bytes_accessed=4 << 20, transcendentals=0
            ),
        )(*operands)

    return run


def contract(left, right, left_dim, right_dim):
    return lax.dot_general(
        left, right, (((left_dim,), (right_dim,)), ((), ())), preferred_element_type=jnp.float32
    )


def pick(blocks, index):
    return lax.dynamic_index_in_dim(blocks, index, 0, keepdims=False)


def swap_dp(block, count, step):
    return lax.ppermute(block, "dp", [(i, i ^ step) for i in range(count)])


def swap_seq(block, count, step):
    return lax.ppermute(block, "seq", [(i, i ^ step) for i in range(count)])


def fetch_pieces(w_up, n_dp, n_seq, dp, core):
    rows, ff = w_up.shape
    cols, half = ff // n_dp, rows // CORES
    own = lax.dynamic_slice(w_up, (0, dp * cols), (rows, cols))
    got = []
    for k in range(1, n_dp):
        piece = lax.dynamic_slice(w_up, (core * half, (dp ^ k) * cols), (half, cols))
        got.append(swap_dp(piece, n_dp, k))
    mine = jnp.stack(got)
    return own, mine, swap_seq(mine, n_seq, 1)


def join_up(own, mine, mate, n_dp, dp, core):
    low = jnp.where(core == 0, mine, mate)
    high = jnp.where(core == 0, mate, mine)
    pairs = jnp.concatenate([low, high], axis=1)
    full = jnp.concatenate([own[None], pairs], axis=0)
    return full[dp ^ jnp.arange(n_dp)].reshape(-1, own.shape[1])


def gather_gain(norm_gain, n_dp, dp):
    parts = jnp.stack(
        [norm_gain] + [swap_dp(norm_gain, n_dp, k) for k in range(1, n_dp)]
    )
    return parts[dp ^ jnp.arange(n_dp)].reshape(-1)


def send_kernel(n_seq, capacity, per_owner, slot_ref, rows_ref, out_ref):
    length, feat = rows_ref.shape
    out_ref[...] = jnp.zeros(out_ref.shape, jnp.bfloat16)
    row = lax.broadcasted_iota(jnp.int32, (PIECE, LANES), 0)
    firsts = [slot_ref[0, t * PIECE] for t in range(length // PIECE)]
    owners = [jnp.where(f >= 0, f // (per_owner * PIECE), n_seq) for f in firsts]
    for t, first in enumerate(firsts):
        rank = jnp.int32(0)
        for earlier in range(t):
            rank = rank + jnp.where(owners[earlier] == owners[t], 1, 0)

        @pl.when(first >= 0)
        def _(t=t, first=first, rank=rank):
            place = pl.ds(pl.multiple_of(rank * PIECE, PIECE), PIECE)
            out_ref[owners[t], place, :feat] = rows_ref[t * PIECE : (t + 1) * PIECE, :]
            landing = first % (per_owner * PIECE) + row + 1
            out_ref[owners[t], place, feat:] = landing.astype(jnp.float32).astype(jnp.bfloat16)


def land_kernel(got_ref, out_ref):
    tokens, feat = out_ref.shape
    slots = got_ref.shape[0]
    marks = got_ref[:, feat:].astype(jnp.float32)
    goal = lax.broadcasted_iota(jnp.int32, (slots, LANES), 1) + 1
    rows = got_ref[:, :feat]
    for part in range(tokens // LANES):
        select = (marks == (goal + part * LANES).astype(jnp.float32)).astype(jnp.bfloat16)
        out_ref[part * LANES : (part + 1) * LANES, :] = contract(select, rows, 0, 0).astype(
            jnp.bfloat16
        )


def send_tiles(llm_rows, slot_ids, n_seq, tokens):
    per_owner = tokens // PIECE
    capacity = 1 + (per_owner + n_seq - 2) // n_seq
    return vmem_call(
        lambda *refs: send_kernel(n_seq, capacity, per_owner, *refs),
        jax.ShapeDtypeStruct(
            (n_seq, capacity * PIECE, llm_rows.shape[1] + LANES), jnp.bfloat16
        ),
        [pltpu.SMEM, pltpu.VMEM],
        1 << 20,
    )(slot_ids, llm_rows)


def land_tiles(got, tokens):
    return vmem_call(
        land_kernel,
        jax.ShapeDtypeStruct((tokens, got.shape[2] - LANES), jnp.bfloat16),
        [pltpu.VMEM],
        1 << 26,
    )(got.reshape(-1, got.shape[2]))


def head_lanes(head, rows, width, start):
    lane = lax.broadcasted_iota(jnp.int32, (rows, width), 1) + start
    return (lane >= head * HDIM) & (lane < (head + 1) * HDIM)


def span_of(head):
    start = head * HDIM // LANES * LANES
    stop = -(-(head + 1) * HDIM // LANES) * LANES
    return start, stop


def masked_head(ref, head):
    start, stop = span_of(head)
    block = ref[:, start:stop]
    return jnp.where(head_lanes(head, block.shape[0], stop - start, start), block, 0).astype(
        block.dtype
    )


def add_span(total, head, part):
    start, stop = span_of(head)
    for at in range(start, stop, LANES):
        piece = part[:, at - start : at - start + LANES]
        total[at] = total[at] + piece if at in total else piece


def forward_kernel(mask_ref, q_ref, k_ref, v_ref, resid_ref, out_ref, unit_ref, *saved_refs):
    tokens, feat = q_ref.shape
    scale = 1.0 / math.sqrt(HDIM)
    row = lax.broadcasted_iota(jnp.int32, (tokens, tokens), 0) // BLK
    col = lax.broadcasted_iota(jnp.int32, (tokens, tokens), 1) // BLK
    allowed = row == col
    for i in range(tokens // BLK):
        for j in range(tokens // BLK):
            if i != j:
                allowed = allowed | ((row == i) & (col == j) & (mask_ref[i, j] > 0))
    total = {}
    for head in range(HEADS):
        start, stop = span_of(head)
        scores = contract(q_ref[:, start:stop], masked_head(k_ref, head), 1, 1) * scale
        scores = jnp.where(allowed, scores, -jnp.inf)
        exp_terms = jnp.exp(scores - jnp.max(scores, axis=1, keepdims=True))
        probs = exp_terms / jnp.sum(exp_terms, axis=1, keepdims=True)
        if saved_refs:
            saved_refs[0][head] = probs
        add_span(total, head, contract(probs.astype(jnp.bfloat16), masked_head(v_ref, head), 1, 0))
    for at, value in total.items():
        out_ref[:, at : at + LANES] = value.astype(jnp.bfloat16)
    hidden = resid_ref[...].astype(jnp.float32) + out_ref[...].astype(jnp.float32)
    center = jnp.mean(hidden, axis=1, keepdims=True)
    hidden = hidden - center
    variance = jnp.mean(jnp.square(hidden), axis=1, keepdims=True)
    inverse = lax.rsqrt(variance + 1e-06)
    unit_ref[...] = (hidden * inverse).astype(unit_ref.dtype)
    if saved_refs:
        saved_refs[1][...] = jnp.broadcast_to(inverse, saved_refs[1].shape)


def forward(mask, query, key_block, value_block, resid, flops, saved):
    tokens, feat = query.shape
    rest = (
        jax.ShapeDtypeStruct((HEADS, tokens, tokens), jnp.float32),
        jax.ShapeDtypeStruct((tokens, LANES), jnp.float32),
    )
    return vmem_call(
        forward_kernel,
        (
            jax.ShapeDtypeStruct((tokens, feat), jnp.bfloat16),
            jax.ShapeDtypeStruct((tokens, feat), jnp.float32 if saved else jnp.bfloat16),
        )
        + (rest if saved else ()),
        [pltpu.SMEM] + [pltpu.VMEM] * 4,
        flops,
    )(mask, query, key_block, value_block, resid)


def backward_kernel(
    got_ref,
    rows_ref,
    unit_ref,
    inverse_ref,
    gain_ref,
    probs_ref,
    out_ref,
    q_ref,
    k_ref,
    v_ref,
    gq_ref,
    gk_ref,
    gv_ref,
    gr_ref,
):
    tokens, feat = q_ref.shape
    scale = 1.0 / math.sqrt(HDIM)
    d_normed = sum(got_ref[part].astype(jnp.float32) for part in range(got_ref.shape[0]))
    unit = unit_ref[...]
    d_unit = d_normed * gain_ref[...].astype(jnp.float32)
    d_hidden = inverse_ref[:, :1] * (
        d_unit
        - jnp.mean(d_unit, axis=1, keepdims=True)
        - unit * jnp.mean(d_unit * unit, axis=1, keepdims=True)
    )
    gr_ref[...] = (rows_ref[...].astype(jnp.float32) + d_hidden).astype(jnp.bfloat16)
    totals = ({}, {}, {})
    for head in range(HEADS):
        start, stop = span_of(head)
        probs = probs_ref[head]
        grad = masked_head(gr_ref, head)
        add_span(totals[0], head, contract(probs.astype(jnp.bfloat16), grad, 0, 0))
        d_probs = contract(grad, v_ref[:, start:stop], 1, 1)
        delta = jnp.sum(
            grad.astype(jnp.float32) * out_ref[:, start:stop].astype(jnp.float32),
            axis=1,
            keepdims=True,
        )
        d_scores = (probs * (d_probs - delta) * scale).astype(jnp.bfloat16)
        add_span(totals[1], head, contract(d_scores, masked_head(k_ref, head), 1, 0))
        add_span(totals[2], head, contract(d_scores, masked_head(q_ref, head), 0, 0))
    for ref, total in zip((gv_ref, gq_ref, gk_ref), totals):
        for at, value in total.items():
            ref[:, at : at + LANES] = value.astype(jnp.bfloat16)


def backward(*operands):
    tokens, feat = operands[1].shape
    return vmem_call(
        backward_kernel,
        tuple(jax.ShapeDtypeStruct((tokens, feat), jnp.bfloat16) for _ in range(4)),
        [pltpu.VMEM] * 10,
        1 << 32,
    )(*operands)


def scatter_up(term, n_seq, seq):
    n_z, core, z = n_seq // CORES, seq % CORES, seq // CORES
    rows, cols = term.shape
    pieces = term.reshape(n_z, CORES, rows // n_seq, cols)
    keep = lax.dynamic_index_in_dim(pieces, core, 1, keepdims=False)
    give = lax.dynamic_index_in_dim(pieces, 1 - core, 1, keepdims=False)
    both = (
        keep.astype(jnp.float32) + swap_seq(give.astype(jnp.bfloat16), n_seq, 1).astype(jnp.float32)
    ).astype(jnp.bfloat16)
    total = pick(both, z).astype(jnp.float32)
    for k in reversed(range(1, n_z)):
        total = total + swap_seq(pick(both, z ^ k), n_seq, CORES * k).astype(jnp.float32)
    return total


def scatter_down(term, n_seq, n_dp, seq):
    n_z, core, z = n_seq // CORES, seq % CORES, seq // CORES
    rows, cols = term.shape
    n_h, n_e = n_seq // n_dp, n_dp // CORES
    half = cols // CORES
    keep = lax.dynamic_slice(term, (0, core * half), (rows, half))
    give = lax.dynamic_slice(term, (0, (1 - core) * half), (rows, half))
    both = keep + swap_seq(give.astype(jnp.bfloat16), n_seq, 1).astype(jnp.float32)
    pieces = (
        both.reshape(n_h, rows // n_h, n_e, half // n_e)
        .transpose(0, 2, 1, 3)
        .reshape(n_z, rows // n_h, half // n_e)
        .astype(jnp.bfloat16)
    )
    total = 0.0
    for j in range(n_z):
        pairs = []
        for a in range(n_z):
            m = (a + j) % n_z
            for c in range(CORES):
                for d in range(n_dp):
                    source = (a * CORES + c) * n_dp + d
                    goal = (d * n_h + m // n_e) * n_dp + c * n_e + m % n_e
                    pairs.append((source, goal))
        block = lax.ppermute(pick(pieces, (z + j) % n_z), ("seq", "dp"), pairs)
        total = total + block.astype(jnp.float32)
    return total


def sum_all(term, n_seq, n_dp):
    total = term + swap_seq(term, n_seq, 1)
    term = total
    for k in range(1, n_seq // CORES):
        total = total + swap_seq(term, n_seq, CORES * k)
    term = total
    for k in range(1, n_dp):
        total = total + swap_dp(term, n_dp, k)
    return total


def fetch_kernel(place_ref, up_ref, gain_ref, *out_refs):
    rows, cols = out_refs[0].shape
    half = rows - PIECE
    own = pl.ds(pl.multiple_of(place_ref[1] * half, PIECE), half)
    gain = gain_ref[...].astype(jnp.float32)
    gain = jnp.concatenate([gain, jnp.zeros((1, cols - gain.shape[1]), jnp.float32)], axis=1)
    gain = jnp.broadcast_to(gain, (PIECE, cols)).astype(jnp.bfloat16)
    for k, ref in enumerate(out_refs):
        at = pl.multiple_of((place_ref[0] ^ k) * cols, LANES)
        ref[:half, :] = up_ref[own, pl.ds(at, cols)]
        ref[half:, :] = gain


def fetch_up(place, w_up, norm_gain, n_dp):
    rows, ff = w_up.shape
    piece = jax.ShapeDtypeStruct((rows // CORES + PIECE, ff // n_dp), jnp.bfloat16)
    return vmem_call(
        fetch_kernel, (piece,) * n_dp, [pltpu.SMEM, pltpu.VMEM, pltpu.VMEM], 1 << 20
    )(place, w_up, norm_gain[None])


def join_kernel(place_ref, mine_ref, mate_ref, up_ref, gain_ref):
    n_dp, half, cols = mine_ref.shape
    half = half - PIECE
    core = place_ref[1]
    for d in range(n_dp):
        for ref, which in ((mine_ref, core), (mate_ref, 1 - core)):
            base = ((place_ref[0] ^ d) * CORES + which) * half
            up_ref[pl.ds(pl.multiple_of(base, PIECE), half), :] = ref[d, :half, :]
    size = gain_ref.shape[1] // n_dp
    parts = [mine_ref[k, half:, :].astype(jnp.float32)[:1, :size] for k in range(n_dp)]
    row = []
    for d in range(n_dp):
        total = jnp.zeros((1, size), jnp.float32)
        for k, part in enumerate(parts):
            total = jnp.where((place_ref[0] ^ k) == d, part, total)
        row.append(total)
    gain_ref[...] = jnp.concatenate(row, axis=1)


def join_columns(place, mine, mate):
    n_dp, half, cols = mine.shape
    feat = n_dp * CORES * (half - PIECE)
    return vmem_call(
        join_kernel,
        (
            jax.ShapeDtypeStruct((feat, cols), jnp.bfloat16),
            jax.ShapeDtypeStruct((1, feat), jnp.float32),
        ),
        [pltpu.SMEM, pl.ANY, pl.ANY],
        1 << 20,
    )(place, mine, mate)


def mlp_kernel(up_ref, gain_ref, *refs):
    *unit_refs, act_ref, slope_ref, flip_ref, all_ref = refs
    tokens = unit_refs[0].shape[0]
    gain = gain_ref[...]
    for k, ref in enumerate(unit_refs):
        normed = (ref[...].astype(jnp.float32) * gain).astype(jnp.bfloat16)
        all_ref[k * tokens : (k + 1) * tokens, :] = normed
        flip_ref[:, k * tokens : (k + 1) * tokens] = normed.T
    pre_act = contract(all_ref[...], up_ref[...], 1, 0)
    sig_gate = jax.nn.sigmoid(1.702 * pre_act)
    act_ref[...] = (pre_act * sig_gate).astype(jnp.bfloat16).T
    slope_ref[...] = sig_gate + 1.702 * pre_act * sig_gate * (1.0 - sig_gate)


def mlp(up_cols, gain, unit_blocks):
    tokens, feat = unit_blocks[0].shape
    total = tokens * len(unit_blocks)
    cols = up_cols.shape[1]
    return vmem_call(
        mlp_kernel,
        (
            jax.ShapeDtypeStruct((cols, total), jnp.bfloat16),
            jax.ShapeDtypeStruct((total, cols), jnp.float32),
            jax.ShapeDtypeStruct((feat, total), jnp.bfloat16),
            jax.ShapeDtypeStruct((total, feat), jnp.bfloat16),
        ),
        [pltpu.VMEM] * (2 + len(unit_blocks)),
        2 * total * feat * cols,
    )(up_cols, gain, *unit_blocks)


def store_by_core(core, value, which, keep_ref, give_ref, index):
    @pl.when(core == which)
    def _():
        keep_ref[index] = value

    @pl.when(core != which)
    def _():
        give_ref[index] = value


def down_kernel(place_ref, act_ref, *refs):
    *rows_refs, all_ref, keep_ref, give_ref = refs
    n_dp, half, width = keep_ref.shape
    tokens = rows_refs[0].shape[0]
    for k, ref in enumerate(rows_refs):
        all_ref[k * tokens : (k + 1) * tokens, :] = ref[...]
    term = contract(act_ref[...], all_ref[...], 1, 0).astype(jnp.bfloat16)
    for which in range(CORES):
        for d in range(n_dp):
            piece = term[which * half : (which + 1) * half, d * width : (d + 1) * width]
            store_by_core(place_ref[1], piece, which, keep_ref, give_ref, d)


def down_pieces(place, act_flip, rows_blocks):
    n_dp = len(rows_blocks)
    tokens, feat = rows_blocks[0].shape
    cols = act_flip.shape[0]
    piece = jax.ShapeDtypeStruct((n_dp, cols // CORES, feat // n_dp), jnp.bfloat16)
    return vmem_call(
        down_kernel,
        (jax.ShapeDtypeStruct((n_dp * tokens, feat), jnp.bfloat16), piece, piece),
        [pltpu.SMEM] + [pltpu.VMEM] * (1 + n_dp),
        2 * n_dp * tokens * feat * cols,
    )(place, act_flip, *rows_blocks)


def up_kernel(place_ref, rows_ref, down_ref, slope_ref, flip_ref, pre_ref, keep_ref, give_ref):
    n_z, rows, cols = keep_ref.shape
    d_act = contract(rows_ref[...], down_ref[...], 1, 1)
    d_pre = (d_act * slope_ref[...]).astype(jnp.bfloat16)
    pre_ref[...] = d_pre
    term = contract(flip_ref[...], d_pre, 1, 0).astype(jnp.bfloat16)
    for z in range(n_z):
        for which in range(CORES):
            start = (z * CORES + which) * rows
            piece = term[start : start + rows]
            store_by_core(place_ref[1], piece, which, keep_ref, give_ref, z)


def up_pieces(place, rows_all, w_down, slope, normed_flip, n_z):
    total, cols = slope.shape
    feat = w_down.shape[1]
    piece = jax.ShapeDtypeStruct((n_z, feat // n_z // CORES, cols), jnp.bfloat16)
    return vmem_call(
        up_kernel,
        (jax.ShapeDtypeStruct((total, cols), jnp.bfloat16), piece, piece),
        [pltpu.SMEM] + [pl.ANY] * 4,
        4 * total * feat * cols,
    )(place, rows_all, w_down, slope, normed_flip)


def part_kernel(place_ref, pre_ref, up_ref, *refs):
    *unit_refs, parts_ref, term_ref = refs
    n_dp, tokens, _ = parts_ref.shape
    part = contract(pre_ref[...], up_ref[...], 1, 1)
    for k in range(n_dp):
        rows = part[k * tokens : (k + 1) * tokens]
        parts_ref[place_ref[0] ^ k] = rows.astype(jnp.bfloat16)
        term = jnp.sum(rows * unit_refs[k][...].astype(jnp.float32), axis=0, keepdims=True)
        term_ref[...] = term if k == 0 else term_ref[...] + term


def normed_parts(place, d_pre, up_cols, unit_blocks):
    tokens, feat = unit_blocks[0].shape
    n_dp = len(unit_blocks)
    return vmem_call(
        part_kernel,
        (
            jax.ShapeDtypeStruct((n_dp, tokens, feat), jnp.bfloat16),
            jax.ShapeDtypeStruct((1, feat), jnp.float32),
        ),
        [pltpu.SMEM] + [pl.ANY] * (2 + n_dp),
        2 * n_dp * tokens * feat * d_pre.shape[1],
    )(place, d_pre, up_cols, *unit_blocks)


def wide_sum(*terms):
    return sum(term.astype(jnp.float32) for term in terms)


def to_rows(vector, width):
    high = vector.astype(jnp.bfloat16).astype(jnp.float32)
    rows = [
        part[:, at : at + width]
        for part in (high, vector - high)
        for at in range(0, vector.shape[1], width)
    ]
    rows.append(jnp.zeros((PIECE - len(rows), width), jnp.float32))
    return jnp.concatenate(rows, axis=0).astype(jnp.bfloat16)


def side_kernel(place_ref, keep_ref, mate_ref, keep_out, give_out):
    z = place_ref[2]
    count = keep_out.shape[0]
    for i in range(count):
        for ref, at in ((keep_out, z ^ (2 * i)), (give_out, z ^ (2 * i + 1))):
            ref[i] = wide_sum(keep_ref[at], mate_ref[at]).astype(jnp.bfloat16)


def middle_kernel(keep_ref, got_ref, keep_out, give_out):
    keep_out[...] = wide_sum(keep_ref[0], got_ref[0]).astype(jnp.bfloat16)
    give_out[...] = wide_sum(keep_ref[1], got_ref[1]).astype(jnp.bfloat16)


def plane_kernel(place_ref, keep_ref, mate_ref, *out_refs):
    for k, ref in enumerate(out_refs):
        at = place_ref[0] ^ k
        ref[...] = wide_sum(keep_ref[at], mate_ref[at]).astype(jnp.bfloat16)


def rise_kernel(place_ref, term_ref, other_ref, *refs):
    count = len(refs) // 2
    got_refs, out_refs = refs[:count], refs[count:]
    half, width = got_refs[0].shape
    rows = to_rows(term_ref[...] + other_ref[...], width)
    for k, ref in enumerate(out_refs):
        for step, got_ref in enumerate(got_refs):

            @pl.when((place_ref[2] ^ k) == (place_ref[0] ^ step))
            def _(ref=ref, got_ref=got_ref):
                ref[:half, :] = got_ref[...]

        ref[half:, :] = rows


def total_kernel(factor, *refs):
    *in_refs, out_ref = refs
    out_ref[...] = (wide_sum(*(ref[...] for ref in in_refs)) * factor).astype(jnp.bfloat16)


def last_kernel(factor, *refs):
    *in_refs, down_ref, gain_ref = refs
    half = down_ref.shape[0]
    count = len(in_refs)
    down_ref[...] = (wide_sum(*(ref[:half, :] for ref in in_refs)) * factor).astype(jnp.bfloat16)
    rows = wide_sum(*(ref[half:, :] for ref in in_refs))
    rows = (rows[:count] + rows[count : 2 * count]) * factor
    gain_ref[...] = jnp.concatenate([rows[i : i + 1] for i in range(count)], axis=1)


def up_sides(place, keep, mate):
    pair = jax.ShapeDtypeStruct((keep.shape[0] // 2,) + keep.shape[1:], jnp.bfloat16)
    return vmem_call(side_kernel, (pair, pair), [pltpu.SMEM, pltpu.VMEM, pltpu.VMEM], 1 << 20)(
        place, keep, mate
    )


def up_middle(keep, got):
    piece = jax.ShapeDtypeStruct(keep.shape[1:], jnp.bfloat16)
    return vmem_call(middle_kernel, (piece, piece), [pltpu.VMEM] * 2, 1 << 20)(keep, got)


def up_total(keep, got, factor):
    piece = jax.ShapeDtypeStruct(keep.shape, jnp.bfloat16)
    return vmem_call(
        lambda *refs: total_kernel(factor, *refs), piece, [pltpu.VMEM] * 2, 1 << 20
    )(keep, got)


def down_planes(place, keep, mate):
    n_dp, half, width = keep.shape
    piece = jax.ShapeDtypeStruct((half, width), jnp.bfloat16)
    return vmem_call(
        plane_kernel, (piece,) * n_dp, [pltpu.SMEM] + [pltpu.VMEM] * 2, 1 << 20
    )(place, keep, mate)


def down_rise(place, term, other, planes):
    count = len(planes)
    half, width = planes[0].shape
    piece = jax.ShapeDtypeStruct((half + PIECE, width), jnp.bfloat16)
    return vmem_call(
        rise_kernel, (piece,) * count, [pltpu.SMEM] + [pltpu.VMEM] * (2 + count), 1 << 20
    )(place, term, other, *planes)


def down_total(pieces, factor):
    rows, width = pieces[0].shape
    down, gain = vmem_call(
        lambda *refs: last_kernel(factor, *refs),
        (
            jax.ShapeDtypeStruct((rows - PIECE, width), jnp.bfloat16),
            jax.ShapeDtypeStruct((1, width * len(pieces)), jnp.float32),
        ),
        [pltpu.VMEM] * len(pieces),
        1 << 20,
    )(*pieces)
    return down, gain[0]


def after(value, *others):
    return lax.optimization_barrier((value,) + others)[0]


def per_device(
    queries,
    key_rows,
    value_rows,
    resid_in,
    llm_grad,
    vision_slot,
    window_mask,
    w_up,
    w_down,
    norm_gain,
):
    n_seq = lax.axis_size("seq")
    n_dp = lax.axis_size("dp")
    seq = lax.axis_index("seq")
    dp = lax.axis_index("dp")
    core = seq % CORES
    tokens, feat_dim = queries.shape[1:]

    factor = 1.0 / math.sqrt(n_dp * n_seq * tokens)
    place = jnp.stack([dp, core, seq // CORES]).astype(jnp.int32)
    quick = n_seq == CORES * n_dp == 8

    def backward_pass(d_got, saved):
        attn_out, normal_unit, attn_probs, inverse = saved
        return backward(
            d_got,
            grad_rows,
            normal_unit,
            inverse,
            gain_row,
            attn_probs,
            attn_out,
            queries[0],
            key_rows[0],
            value_rows[0],
        )

    def all_dp(block):
        return [block] + [swap_dp(block, n_dp, k) for k in range(1, n_dp)]

    sent = send_tiles(llm_grad[0], vision_slot, n_seq, tokens)
    landing = lax.all_to_all(sent, "seq", split_axis=0, concat_axis=0, tiled=True)
    attention = (queries[0], key_rows[0], value_rows[0], resid_in[0])
    if quick:
        _, unit_low = forward(window_mask[0], *attention, 1 << 31, False)
        unit_blocks = all_dp(unit_low)
        own, *others = fetch_up(place, after(w_up, sent), norm_gain, n_dp)
        mine = jnp.stack([own] + [swap_dp(block, n_dp, k + 1) for k, block in enumerate(others)])
        up_cols, gain_row = join_columns(place, mine, swap_seq(mine, n_seq, 1))
        landing = after(landing, up_cols)
    else:
        gain_row = gather_gain(norm_gain, n_dp, dp).astype(jnp.float32)[None]
        own, mine, mate = fetch_pieces(w_up, n_dp, n_seq, dp, core)
        saved = forward(window_mask[0], *attention, 1 << 31, True)
        normed_blocks = all_dp((saved[1] * gain_row).astype(jnp.bfloat16))
    grad_rows = land_tiles(landing, tokens)
    rows_blocks = all_dp(grad_rows)
    if quick:
        act_flip, slope, normed_flip, normed_all = mlp(up_cols, gain_row, unit_blocks)
        rows_all, down_keep, down_give = down_pieces(place, act_flip, rows_blocks)
        down_mate = swap_seq(down_give, n_seq, 1)
        d_pre, up_keep, up_give = up_pieces(
            place, rows_all, w_down, slope, normed_flip, n_seq // CORES
        )
        up_mate = swap_seq(up_give, n_seq, 1)
        own, *sends = down_planes(place, after(down_keep, d_pre), down_mate)
        planes = [own] + [swap_dp(block, n_dp, k + 1) for k, block in enumerate(sends)]
        parts, term = normed_parts(place, after(d_pre, own), up_cols, unit_blocks)
        term = term + swap_seq(term, n_seq, 1)
        up_keep, up_give = up_sides(place, after(up_keep, own), up_mate)
        up_got = swap_seq(up_give, n_seq, CORES)
        term = term + swap_dp(term, n_dp, 1)
        own, *sends = down_rise(place, term, swap_dp(term, n_dp, 2), planes)
        pieces = [own] + [
            swap_seq(block, n_seq, CORES * (k + 1)) for k, block in enumerate(sends)
        ]
        up_keep, up_give = up_middle(up_keep, up_got)
        up_got = swap_seq(up_give, n_seq, 2 * CORES)
        d_got = lax.all_to_all(
            after(parts, own, up_give), "dp", split_axis=0, concat_axis=0, tiled=True
        )
        saved = forward(after(window_mask[0], own), *attention, 1 << 31, True)
        grads = backward_pass(after(d_got, up_got), saved)
        pieces[0] = after(pieces[0], grads[3])
        grad_up = up_total(up_keep, up_got, factor)
        grad_down, grad_gain = down_total(pieces, factor)
    else:
        normed_all = jnp.concatenate(normed_blocks, axis=0)
        rows_all = jnp.concatenate(rows_blocks, axis=0)
        up_cols = join_up(own, mine, mate, n_dp, dp, core)
        pre_act = contract(normed_all, up_cols, 1, 0)
        sig_gate = jax.nn.sigmoid(1.702 * pre_act)
        act_low = (pre_act * sig_gate).astype(jnp.bfloat16)
        d_act = contract(rows_all, w_down, 1, 1)
        d_pre = (d_act * (sig_gate + 1.702 * pre_act * sig_gate * (1.0 - sig_gate))).astype(
            jnp.bfloat16
        )
        d_part = contract(d_pre, up_cols, 1, 1)
        blocks = d_part.astype(jnp.bfloat16).reshape(n_dp, tokens, feat_dim)
        d_got = jnp.stack([blocks[0]] + [swap_dp(blocks[k], n_dp, k) for k in range(1, n_dp)])
        up_sum = scatter_up(contract(normed_all, d_pre, 0, 0), n_seq, seq)
        down_sum = scatter_down(contract(act_low, rows_all, 0, 0), n_seq, n_dp, seq)
        gain_part = jnp.sum(d_part * normed_all.astype(jnp.float32), axis=0)
        grad_gain = factor * sum_all(gain_part / gain_row[0], n_seq, n_dp)
        grad_up = (up_sum * factor).astype(jnp.bfloat16)
        grad_down = (down_sum * factor).astype(jnp.bfloat16)
        grads = backward_pass(d_got, saved)
    grad_query, grad_key, grad_value, grad_resid = grads

    return (
        grad_query[None],
        grad_key[None],
        grad_value[None],
        grad_resid[None],
        grad_up,
        grad_down,
        grad_gain,
    )


def solution(mesh):
    in_specs = (
        P("dp", "seq", None),
        P("dp", "seq", None),
        P("dp", "seq", None),
        P("dp", "seq", None),
        P("dp", "seq", None),
        P("dp", "seq"),
        P("dp", "seq", None),
        P("dp", None),
        P("dp", None),
        P("dp"),
    )
    out_specs = (
        P("dp", "seq", None),
        P("dp", "seq", None),
        P("dp", "seq", None),
        P("dp", "seq", None),
        P("seq", "dp"),
        P("seq", "dp"),
        P(),
    )
    return jax.shard_map(
        per_device, mesh=mesh, in_specs=in_specs, out_specs=out_specs, check_vma=False
    )
```

```python
import math

import jax
import jax.numpy as jnp
from jax import lax
from jax.experimental import pallas as pl
from jax.experimental.pallas import tpu as pltpu
from jax.sharding import PartitionSpec as P

HEADS = 16
HDIM = 80
BLK = 64
PIECE = 16
CORES = 2
LANES = 128
VMEM_BYTES = 16 * 1024 * 1024
MOST_BYTES = 60 * 1024 * 1024


def vmem_call(body, out_shape, in_spaces, flops, late=(), limit=VMEM_BYTES):
    def run(*operands):
        places = [i for i, space in enumerate(in_spaces) if space == pl.ANY]
        outs = len(jax.tree.leaves(out_shape))

        def kernel(*refs):
            refs = list(refs)
            ins, rest = refs[: len(in_spaces)], refs[len(in_spaces) :]
            held, sems = rest[outs : outs + len(places)], rest[outs + len(places) :]
            copies = [
                pltpu.make_async_copy(ins[i], held[n], sems[n]) for n, i in enumerate(places)
            ]
            for copy in copies:
                copy.start()
            for n, i in enumerate(places):
                ins[i] = held[n]
                if i not in late:
                    copies[n].wait()
            waits = [copies[places.index(i)].wait for i in late]
            body(*waits, *ins, *rest[:outs])

        return pl.pallas_call(
            kernel if places else body,
            out_shape=out_shape,
            in_specs=[pl.BlockSpec(memory_space=space) for space in in_spaces],
            out_specs=jax.tree.map(lambda _: pl.BlockSpec(memory_space=pltpu.VMEM), out_shape),
            scratch_shapes=[pltpu.VMEM(operands[i].shape, operands[i].dtype) for i in places]
            + [pltpu.SemaphoreType.DMA for _ in places],
            compiler_params=pltpu.CompilerParams(vmem_limit_bytes=limit),
            cost_estimate=pl.CostEstimate(
                flops=flops, bytes_accessed=4 << 20, transcendentals=0
            ),
        )(*operands)

    return run


def contract(left, right, left_dim, right_dim):
    return lax.dot_general(
        left, right, (((left_dim,), (right_dim,)), ((), ())), preferred_element_type=jnp.float32
    )


def pick(blocks, index):
    return lax.dynamic_index_in_dim(blocks, index, 0, keepdims=False)


def swap_dp(block, count, step):
    return lax.ppermute(block, "dp", [(i, i ^ step) for i in range(count)])


def swap_seq(block, count, step):
    return lax.ppermute(block, "seq", [(i, i ^ step) for i in range(count)])


def fetch_pieces(w_up, n_dp, n_seq, dp, core):
    rows, ff = w_up.shape
    cols, half = ff // n_dp, rows // CORES
    own = lax.dynamic_slice(w_up, (0, dp * cols), (rows, cols))
    got = []
    for k in range(1, n_dp):
        piece = lax.dynamic_slice(w_up, (core * half, (dp ^ k) * cols), (half, cols))
        got.append(swap_dp(piece, n_dp, k))
    mine = jnp.stack(got)
    return own, mine, swap_seq(mine, n_seq, 1)


def join_up(own, mine, mate, n_dp, dp, core):
    low = jnp.where(core == 0, mine, mate)
    high = jnp.where(core == 0, mate, mine)
    pairs = jnp.concatenate([low, high], axis=1)
    full = jnp.concatenate([own[None], pairs], axis=0)
    return full[dp ^ jnp.arange(n_dp)].reshape(-1, own.shape[1])


def gather_gain(norm_gain, n_dp, dp):
    parts = jnp.stack(
        [norm_gain] + [swap_dp(norm_gain, n_dp, k) for k in range(1, n_dp)]
    )
    return parts[dp ^ jnp.arange(n_dp)].reshape(-1)


def send_kernel(n_seq, capacity, per_owner, slot_ref, rows_ref, out_ref):
    length, feat = rows_ref.shape
    out_ref[...] = jnp.zeros(out_ref.shape, jnp.bfloat16)
    row = lax.broadcasted_iota(jnp.int32, (PIECE, LANES), 0)
    firsts = [slot_ref[0, t * PIECE] for t in range(length // PIECE)]
    owners = [jnp.where(f >= 0, f // (per_owner * PIECE), n_seq) for f in firsts]
    for t, first in enumerate(firsts):
        rank = jnp.int32(0)
        for earlier in range(t):
            rank = rank + jnp.where(owners[earlier] == owners[t], 1, 0)

        @pl.when(first >= 0)
        def _(t=t, first=first, rank=rank):
            place = pl.ds(pl.multiple_of(rank * PIECE, PIECE), PIECE)
            out_ref[owners[t], place, :feat] = rows_ref[t * PIECE : (t + 1) * PIECE, :]
            landing = first % (per_owner * PIECE) + row + 1
            out_ref[owners[t], place, feat:] = landing.astype(jnp.float32).astype(jnp.bfloat16)


def land_kernel(got_ref, out_ref):
    tokens, feat = out_ref.shape
    slots = got_ref.shape[0]
    marks = got_ref[:, feat:].astype(jnp.float32)
    goal = lax.broadcasted_iota(jnp.int32, (slots, LANES), 1) + 1
    rows = got_ref[:, :feat]
    for part in range(tokens // LANES):
        select = (marks == (goal + part * LANES).astype(jnp.float32)).astype(jnp.bfloat16)
        out_ref[part * LANES : (part + 1) * LANES, :] = contract(select, rows, 0, 0).astype(
            jnp.bfloat16
        )


def send_tiles(llm_rows, slot_ids, n_seq, tokens):
    per_owner = tokens // PIECE
    capacity = 1 + (per_owner + n_seq - 2) // n_seq
    return vmem_call(
        lambda *refs: send_kernel(n_seq, capacity, per_owner, *refs),
        jax.ShapeDtypeStruct(
            (n_seq, capacity * PIECE, llm_rows.shape[1] + LANES), jnp.bfloat16
        ),
        [pltpu.SMEM, pltpu.VMEM],
        1 << 20,
    )(slot_ids, llm_rows)


def land_tiles(got, tokens):
    return vmem_call(
        land_kernel,
        jax.ShapeDtypeStruct((tokens, got.shape[2] - LANES), jnp.bfloat16),
        [pltpu.VMEM],
        1 << 26,
    )(got.reshape(-1, got.shape[2]))


def head_lanes(head, rows, width, start):
    lane = lax.broadcasted_iota(jnp.int32, (rows, width), 1) + start
    return (lane >= head * HDIM) & (lane < (head + 1) * HDIM)


def span_of(head):
    start = head * HDIM // LANES * LANES
    stop = -(-(head + 1) * HDIM // LANES) * LANES
    return start, stop


def masked_head(ref, head):
    start, stop = span_of(head)
    block = ref[:, start:stop]
    return jnp.where(head_lanes(head, block.shape[0], stop - start, start), block, 0).astype(
        block.dtype
    )


def add_span(total, head, part):
    start, stop = span_of(head)
    for at in range(start, stop, LANES):
        piece = part[:, at - start : at - start + LANES]
        total[at] = total[at] + piece if at in total else piece


def forward_kernel(mask_ref, q_ref, k_ref, v_ref, resid_ref, out_ref, unit_ref, *saved_refs):
    tokens, feat = q_ref.shape
    scale = 1.0 / math.sqrt(HDIM)
    row = lax.broadcasted_iota(jnp.int32, (tokens, tokens), 0) // BLK
    col = lax.broadcasted_iota(jnp.int32, (tokens, tokens), 1) // BLK
    allowed = row == col
    for i in range(tokens // BLK):
        for j in range(tokens // BLK):
            if i != j:
                allowed = allowed | ((row == i) & (col == j) & (mask_ref[i, j] > 0))
    total = {}
    for head in range(HEADS):
        start, stop = span_of(head)
        scores = contract(q_ref[:, start:stop], masked_head(k_ref, head), 1, 1) * scale
        scores = jnp.where(allowed, scores, -jnp.inf)
        exp_terms = jnp.exp(scores - jnp.max(scores, axis=1, keepdims=True))
        probs = exp_terms / jnp.sum(exp_terms, axis=1, keepdims=True)
        if saved_refs:
            saved_refs[0][head] = probs
        add_span(total, head, contract(probs.astype(jnp.bfloat16), masked_head(v_ref, head), 1, 0))
    for at, value in total.items():
        out_ref[:, at : at + LANES] = value.astype(jnp.bfloat16)
    hidden = resid_ref[...].astype(jnp.float32) + out_ref[...].astype(jnp.float32)
    center = jnp.mean(hidden, axis=1, keepdims=True)
    hidden = hidden - center
    variance = jnp.mean(jnp.square(hidden), axis=1, keepdims=True)
    inverse = lax.rsqrt(variance + 1e-06)
    unit_ref[...] = (hidden * inverse).astype(unit_ref.dtype)
    if saved_refs:
        saved_refs[1][...] = jnp.broadcast_to(inverse, saved_refs[1].shape)


def forward(mask, query, key_block, value_block, resid, flops, saved):
    tokens, feat = query.shape
    rest = (
        jax.ShapeDtypeStruct((HEADS, tokens, tokens), jnp.float32),
        jax.ShapeDtypeStruct((tokens, LANES), jnp.float32),
    )
    return vmem_call(
        forward_kernel,
        (
            jax.ShapeDtypeStruct((tokens, feat), jnp.bfloat16),
            jax.ShapeDtypeStruct((tokens, feat), jnp.float32 if saved else jnp.bfloat16),
        )
        + (rest if saved else ()),
        [pltpu.SMEM] + [pltpu.VMEM] * 4,
        flops,
    )(mask, query, key_block, value_block, resid)


def backward_kernel(
    wait_probs,
    wait_out,
    wait_q,
    wait_k,
    wait_v,
    got_ref,
    rows_ref,
    unit_ref,
    inverse_ref,
    gain_ref,
    probs_ref,
    out_ref,
    q_ref,
    k_ref,
    v_ref,
    gq_ref,
    gk_ref,
    gv_ref,
    gr_ref,
):
    tokens, feat = q_ref.shape
    scale = 1.0 / math.sqrt(HDIM)
    d_normed = sum(got_ref[part].astype(jnp.float32) for part in range(got_ref.shape[0]))
    unit = unit_ref[...]
    d_unit = d_normed * gain_ref[...].astype(jnp.float32)
    d_hidden = inverse_ref[:, :1] * (
        d_unit
        - jnp.mean(d_unit, axis=1, keepdims=True)
        - unit * jnp.mean(d_unit * unit, axis=1, keepdims=True)
    )
    gr_ref[...] = (rows_ref[...].astype(jnp.float32) + d_hidden).astype(jnp.bfloat16)
    for wait in (wait_probs, wait_out, wait_q, wait_k, wait_v):
        wait()
    totals = ({}, {}, {})
    for head in range(HEADS):
        start, stop = span_of(head)
        probs = probs_ref[head]
        grad = masked_head(gr_ref, head)
        add_span(totals[0], head, contract(probs.astype(jnp.bfloat16), grad, 0, 0))
        d_probs = contract(grad, v_ref[:, start:stop], 1, 1)
        delta = jnp.sum(
            grad.astype(jnp.float32) * out_ref[:, start:stop].astype(jnp.float32),
            axis=1,
            keepdims=True,
        )
        d_scores = (probs * (d_probs - delta) * scale).astype(jnp.bfloat16)
        add_span(totals[1], head, contract(d_scores, masked_head(k_ref, head), 1, 0))
        add_span(totals[2], head, contract(d_scores, masked_head(q_ref, head), 0, 0))
    for ref, total in zip((gv_ref, gq_ref, gk_ref), totals):
        for at, value in total.items():
            ref[:, at : at + LANES] = value.astype(jnp.bfloat16)


def backward(*operands):
    tokens, feat = operands[1].shape
    return vmem_call(
        backward_kernel,
        tuple(jax.ShapeDtypeStruct((tokens, feat), jnp.bfloat16) for _ in range(4)),
        [pl.ANY] * 10,
        1 << 32,
        late=(5, 6, 7, 8, 9),
        limit=MOST_BYTES,
    )(*operands)


def scatter_up(term, n_seq, seq):
    n_z, core, z = n_seq // CORES, seq % CORES, seq // CORES
    rows, cols = term.shape
    pieces = term.reshape(n_z, CORES, rows // n_seq, cols)
    keep = lax.dynamic_index_in_dim(pieces, core, 1, keepdims=False)
    give = lax.dynamic_index_in_dim(pieces, 1 - core, 1, keepdims=False)
    both = (
        keep.astype(jnp.float32) + swap_seq(give.astype(jnp.bfloat16), n_seq, 1).astype(jnp.float32)
    ).astype(jnp.bfloat16)
    total = pick(both, z).astype(jnp.float32)
    for k in reversed(range(1, n_z)):
        total = total + swap_seq(pick(both, z ^ k), n_seq, CORES * k).astype(jnp.float32)
    return total


def scatter_down(term, n_seq, n_dp, seq):
    n_z, core, z = n_seq // CORES, seq % CORES, seq // CORES
    rows, cols = term.shape
    n_h, n_e = n_seq // n_dp, n_dp // CORES
    half = cols // CORES
    keep = lax.dynamic_slice(term, (0, core * half), (rows, half))
    give = lax.dynamic_slice(term, (0, (1 - core) * half), (rows, half))
    both = keep + swap_seq(give.astype(jnp.bfloat16), n_seq, 1).astype(jnp.float32)
    pieces = (
        both.reshape(n_h, rows // n_h, n_e, half // n_e)
        .transpose(0, 2, 1, 3)
        .reshape(n_z, rows // n_h, half // n_e)
        .astype(jnp.bfloat16)
    )
    total = 0.0
    for j in range(n_z):
        pairs = []
        for a in range(n_z):
            m = (a + j) % n_z
            for c in range(CORES):
                for d in range(n_dp):
                    source = (a * CORES + c) * n_dp + d
                    goal = (d * n_h + m // n_e) * n_dp + c * n_e + m % n_e
                    pairs.append((source, goal))
        block = lax.ppermute(pick(pieces, (z + j) % n_z), ("seq", "dp"), pairs)
        total = total + block.astype(jnp.float32)
    return total


def sum_all(term, n_seq, n_dp):
    total = term + swap_seq(term, n_seq, 1)
    term = total
    for k in range(1, n_seq // CORES):
        total = total + swap_seq(term, n_seq, CORES * k)
    term = total
    for k in range(1, n_dp):
        total = total + swap_dp(term, n_dp, k)
    return total


def fetch_kernel(place_ref, up_ref, gain_ref, *out_refs):
    rows, cols = out_refs[0].shape
    half = rows - PIECE
    own = pl.ds(pl.multiple_of(place_ref[1] * half, PIECE), half)
    gain = gain_ref[...].astype(jnp.float32)
    gain = jnp.concatenate([gain, jnp.zeros((1, cols - gain.shape[1]), jnp.float32)], axis=1)
    gain = jnp.broadcast_to(gain, (PIECE, cols)).astype(jnp.bfloat16)
    for k, ref in enumerate(out_refs):
        at = pl.multiple_of((place_ref[0] ^ k) * cols, LANES)
        ref[:half, :] = up_ref[own, pl.ds(at, cols)]
        ref[half:, :] = gain


def send_first(place, slot_ids, llm_rows, w_up, norm_gain, n_seq, n_dp, tokens):
    rows, ff = w_up.shape
    per_owner = tokens // PIECE
    capacity = 1 + (per_owner + n_seq - 2) // n_seq
    piece = jax.ShapeDtypeStruct((rows // CORES + PIECE, ff // n_dp), jnp.bfloat16)
    tiles = jax.ShapeDtypeStruct(
        (n_seq, capacity * PIECE, llm_rows.shape[1] + LANES), jnp.bfloat16
    )

    def body(wait_up, place_ref, slot_ref, gain_ref, rows_ref, up_ref, tiles_ref, *piece_refs):
        send_kernel(n_seq, capacity, per_owner, slot_ref, rows_ref, tiles_ref)
        wait_up()
        fetch_kernel(place_ref, up_ref, gain_ref, *piece_refs)

    return vmem_call(
        body,
        (tiles,) + (piece,) * n_dp,
        [pltpu.SMEM, pltpu.SMEM, pltpu.VMEM, pl.ANY, pl.ANY],
        1 << 20,
        late=(4,),
        limit=MOST_BYTES,
    )(place, slot_ids, norm_gain[None], llm_rows, w_up)


def join_kernel(place_ref, mine_ref, mate_ref, up_ref, gain_ref):
    n_dp, half, cols = mine_ref.shape
    half = half - PIECE
    core = place_ref[1]
    for d in range(n_dp):
        for ref, which in ((mine_ref, core), (mate_ref, 1 - core)):
            base = ((place_ref[0] ^ d) * CORES + which) * half
            up_ref[pl.ds(pl.multiple_of(base, PIECE), half), :] = ref[d, :half, :]
    size = gain_ref.shape[1] // n_dp
    parts = [mine_ref[k, half:, :].astype(jnp.float32)[:1, :size] for k in range(n_dp)]
    row = []
    for d in range(n_dp):
        total = jnp.zeros((1, size), jnp.float32)
        for k, part in enumerate(parts):
            total = jnp.where((place_ref[0] ^ k) == d, part, total)
        row.append(total)
    gain_ref[...] = jnp.concatenate(row, axis=1)


def join_columns(place, mine, mate):
    n_dp, half, cols = mine.shape
    feat = n_dp * CORES * (half - PIECE)
    return vmem_call(
        join_kernel,
        (
            jax.ShapeDtypeStruct((feat, cols), jnp.bfloat16),
            jax.ShapeDtypeStruct((1, feat), jnp.float32),
        ),
        [pltpu.SMEM, pl.ANY, pl.ANY],
        1 << 20,
    )(place, mine, mate)


def mlp_kernel(up_ref, gain_ref, *refs):
    *unit_refs, act_ref, slope_ref, flip_ref, all_ref = refs
    tokens = unit_refs[0].shape[0]
    gain = gain_ref[...]
    for k, ref in enumerate(unit_refs):
        normed = (ref[...].astype(jnp.float32) * gain).astype(jnp.bfloat16)
        all_ref[k * tokens : (k + 1) * tokens, :] = normed
        flip_ref[:, k * tokens : (k + 1) * tokens] = normed.T
    pre_act = contract(all_ref[...], up_ref[...], 1, 0)
    sig_gate = jax.nn.sigmoid(1.702 * pre_act)
    act_ref[...] = (pre_act * sig_gate).astype(jnp.bfloat16).T
    slope_ref[...] = sig_gate + 1.702 * pre_act * sig_gate * (1.0 - sig_gate)


def mlp(up_cols, gain, unit_blocks):
    tokens, feat = unit_blocks[0].shape
    total = tokens * len(unit_blocks)
    cols = up_cols.shape[1]
    return vmem_call(
        mlp_kernel,
        (
            jax.ShapeDtypeStruct((cols, total), jnp.bfloat16),
            jax.ShapeDtypeStruct((total, cols), jnp.float32),
            jax.ShapeDtypeStruct((feat, total), jnp.bfloat16),
            jax.ShapeDtypeStruct((total, feat), jnp.bfloat16),
        ),
        [pltpu.VMEM] * (2 + len(unit_blocks)),
        2 * total * feat * cols,
    )(up_cols, gain, *unit_blocks)


def store_by_core(core, value, which, keep_ref, give_ref, index):
    @pl.when(core == which)
    def _():
        keep_ref[index] = value

    @pl.when(core != which)
    def _():
        give_ref[index] = value


def down_kernel(place_ref, act_ref, *refs):
    *rows_refs, all_ref, keep_ref, give_ref = refs
    n_dp, half, width = keep_ref.shape
    tokens = rows_refs[0].shape[0]
    for k, ref in enumerate(rows_refs):
        all_ref[k * tokens : (k + 1) * tokens, :] = ref[...]
    term = contract(act_ref[...], all_ref[...], 1, 0).astype(jnp.bfloat16)
    for which in range(CORES):
        for d in range(n_dp):
            piece = term[which * half : (which + 1) * half, d * width : (d + 1) * width]
            store_by_core(place_ref[1], piece, which, keep_ref, give_ref, d)


def down_pieces(place, act_flip, rows_blocks):
    n_dp = len(rows_blocks)
    tokens, feat = rows_blocks[0].shape
    cols = act_flip.shape[0]
    piece = jax.ShapeDtypeStruct((n_dp, cols // CORES, feat // n_dp), jnp.bfloat16)
    return vmem_call(
        down_kernel,
        (jax.ShapeDtypeStruct((n_dp * tokens, feat), jnp.bfloat16), piece, piece),
        [pltpu.SMEM] + [pltpu.VMEM] * (1 + n_dp),
        2 * n_dp * tokens * feat * cols,
    )(place, act_flip, *rows_blocks)


def up_kernel(place_ref, rows_ref, down_ref, slope_ref, flip_ref, pre_ref, keep_ref, give_ref):
    n_z, rows, cols = keep_ref.shape
    d_act = contract(rows_ref[...], down_ref[...], 1, 1)
    d_pre = (d_act * slope_ref[...]).astype(jnp.bfloat16)
    pre_ref[...] = d_pre
    term = contract(flip_ref[...], d_pre, 1, 0).astype(jnp.bfloat16)
    for z in range(n_z):
        for which in range(CORES):
            start = (z * CORES + which) * rows
            piece = term[start : start + rows]
            store_by_core(place_ref[1], piece, which, keep_ref, give_ref, z)


def up_pieces(place, rows_all, w_down, slope, normed_flip, n_z):
    total, cols = slope.shape
    feat = w_down.shape[1]
    piece = jax.ShapeDtypeStruct((n_z, feat // n_z // CORES, cols), jnp.bfloat16)
    return vmem_call(
        up_kernel,
        (jax.ShapeDtypeStruct((total, cols), jnp.bfloat16), piece, piece),
        [pltpu.SMEM] + [pltpu.VMEM] * 4,
        4 * total * feat * cols,
    )(place, rows_all, w_down, slope, normed_flip)


def part_kernel(place_ref, pre_ref, up_ref, *refs):
    *unit_refs, parts_ref, term_ref = refs
    n_dp, tokens, _ = parts_ref.shape
    part = contract(pre_ref[...], up_ref[...], 1, 1)
    for k in range(n_dp):
        rows = part[k * tokens : (k + 1) * tokens]
        parts_ref[place_ref[0] ^ k] = rows.astype(jnp.bfloat16)
        term = jnp.sum(rows * unit_refs[k][...].astype(jnp.float32), axis=0, keepdims=True)
        term_ref[...] = term if k == 0 else term_ref[...] + term


def normed_parts(place, d_pre, up_cols, unit_blocks):
    tokens, feat = unit_blocks[0].shape
    n_dp = len(unit_blocks)
    return vmem_call(
        part_kernel,
        (
            jax.ShapeDtypeStruct((n_dp, tokens, feat), jnp.bfloat16),
            jax.ShapeDtypeStruct((1, feat), jnp.float32),
        ),
        [pltpu.SMEM] + [pltpu.VMEM] * (2 + n_dp),
        2 * n_dp * tokens * feat * d_pre.shape[1],
    )(place, d_pre, up_cols, *unit_blocks)


def copy_kernel(in_ref, out_ref):
    out_ref[...] = in_ref[...]


def again(value):
    shape = jax.ShapeDtypeStruct(value.shape, value.dtype)
    return vmem_call(copy_kernel, shape, [pltpu.VMEM], 1 << 20)(value)


def wide_sum(*terms):
    return sum(term.astype(jnp.float32) for term in terms)


def to_rows(vector, width):
    high = vector.astype(jnp.bfloat16).astype(jnp.float32)
    rows = [
        part[:, at : at + width]
        for part in (high, vector - high)
        for at in range(0, vector.shape[1], width)
    ]
    rows.append(jnp.zeros((PIECE - len(rows), width), jnp.float32))
    return jnp.concatenate(rows, axis=0).astype(jnp.bfloat16)


def side_kernel(place_ref, keep_ref, mate_ref, keep_out, give_out):
    z = place_ref[2]
    count = keep_out.shape[0]
    for i in range(count):
        for ref, at in ((keep_out, z ^ (2 * i)), (give_out, z ^ (2 * i + 1))):
            ref[i] = wide_sum(keep_ref[at], mate_ref[at]).astype(jnp.bfloat16)


def middle_kernel(keep_ref, got_ref, keep_out, give_out):
    keep_out[...] = wide_sum(keep_ref[0], got_ref[0]).astype(jnp.bfloat16)
    give_out[...] = wide_sum(keep_ref[1], got_ref[1]).astype(jnp.bfloat16)


def plane_kernel(place_ref, keep_ref, mate_ref, *out_refs):
    for k, ref in enumerate(out_refs):
        at = place_ref[0] ^ k
        ref[...] = wide_sum(keep_ref[at], mate_ref[at]).astype(jnp.bfloat16)


def rise_kernel(place_ref, term_ref, other_ref, *refs):
    *got_refs, keep_ref, give_ref, sum_ref = refs
    half, width = got_refs[0].shape
    for k in range(len(got_refs)):
        ref = (keep_ref, give_ref)[k % 2]
        at = k // 2 * half
        for step, got_ref in enumerate(got_refs):

            @pl.when((place_ref[2] ^ k) == (place_ref[0] ^ step))
            def _(ref=ref, at=at, got_ref=got_ref):
                ref[at : at + half, :] = got_ref[...]

    total = term_ref[...] + other_ref[...]
    sum_ref[...] = total
    give_ref[2 * half :, :] = to_rows(total, width)


def from_rows(rows, count):
    rows = rows.astype(jnp.float32)
    rows = rows[:count] + rows[count : 2 * count]
    return jnp.concatenate([rows[i : i + 1] for i in range(count)], axis=1)


def climb_kernel(keep_ref, got_ref, term_ref, own_ref, give_ref, sum_ref):
    half, width = own_ref.shape
    own_ref[...] = wide_sum(keep_ref[:half, :], got_ref[:half, :]).astype(jnp.bfloat16)
    give = wide_sum(keep_ref[half:, :], got_ref[half : 2 * half, :])
    give_ref[:half, :] = give.astype(jnp.bfloat16)
    total = term_ref[...] + from_rows(got_ref[2 * half :, :], term_ref.shape[1] // width)
    sum_ref[...] = total
    give_ref[half:, :] = to_rows(total, width)


def total_kernel(factor, *refs):
    *in_refs, out_ref = refs
    out_ref[...] = (wide_sum(*(ref[...] for ref in in_refs)) * factor).astype(jnp.bfloat16)


def last_kernel(factor, own_ref, got_ref, term_ref, down_ref, gain_ref):
    half, width = own_ref.shape
    down_ref[...] = (wide_sum(own_ref[...], got_ref[:half, :]) * factor).astype(jnp.bfloat16)
    rest = from_rows(got_ref[half:, :], term_ref.shape[1] // width)
    gain_ref[...] = (term_ref[...] + rest) * factor


def up_sides(place, keep, mate):
    pair = jax.ShapeDtypeStruct((keep.shape[0] // 2,) + keep.shape[1:], jnp.bfloat16)
    return vmem_call(side_kernel, (pair, pair), [pltpu.SMEM, pltpu.VMEM, pltpu.VMEM], 1 << 20)(
        place, keep, mate
    )


def up_middle(keep, got):
    piece = jax.ShapeDtypeStruct(keep.shape[1:], jnp.bfloat16)
    return vmem_call(middle_kernel, (piece, piece), [pltpu.VMEM] * 2, 1 << 37)(keep, got)


def up_total(keep, got, factor):
    piece = jax.ShapeDtypeStruct(keep.shape, jnp.bfloat16)
    return vmem_call(
        lambda *refs: total_kernel(factor, *refs), piece, [pltpu.VMEM] * 2, 1 << 20
    )(keep, got)


def down_planes(place, keep, mate):
    n_dp, half, width = keep.shape
    piece = jax.ShapeDtypeStruct((half, width), jnp.bfloat16)
    return vmem_call(
        plane_kernel, (piece,) * n_dp, [pltpu.SMEM] + [pltpu.VMEM] * 2, 1 << 20
    )(place, keep, mate)


def down_rise(place, term, other, planes):
    half, width = planes[0].shape
    return vmem_call(
        rise_kernel,
        (
            jax.ShapeDtypeStruct((2 * half, width), jnp.bfloat16),
            jax.ShapeDtypeStruct((2 * half + PIECE, width), jnp.bfloat16),
            jax.ShapeDtypeStruct(term.shape, jnp.float32),
        ),
        [pltpu.SMEM] + [pltpu.VMEM] * (2 + len(planes)),
        1 << 20,
    )(place, term, other, *planes)


def down_climb(keep, got, term):
    half, width = keep.shape[0] // 2, keep.shape[1]
    return vmem_call(
        climb_kernel,
        (
            jax.ShapeDtypeStruct((half, width), jnp.bfloat16),
            jax.ShapeDtypeStruct((half + PIECE, width), jnp.bfloat16),
            jax.ShapeDtypeStruct(term.shape, jnp.float32),
        ),
        [pltpu.VMEM] * 3,
        1 << 35,
    )(keep, got, term)


def down_total(own, got, term, factor):
    down, gain = vmem_call(
        lambda *refs: last_kernel(factor, *refs),
        (
            jax.ShapeDtypeStruct(own.shape, jnp.bfloat16),
            jax.ShapeDtypeStruct(term.shape, jnp.float32),
        ),
        [pltpu.VMEM] * 3,
        1 << 20,
    )(own, got, term)
    return down, gain.reshape(-1)


def after(value, *others):
    return lax.optimization_barrier((value,) + others)[0]


def per_device(
    queries,
    key_rows,
    value_rows,
    resid_in,
    llm_grad,
    vision_slot,
    window_mask,
    w_up,
    w_down,
    norm_gain,
):
    n_seq = lax.axis_size("seq")
    n_dp = lax.axis_size("dp")
    seq = lax.axis_index("seq")
    dp = lax.axis_index("dp")
    core = seq % CORES
    tokens, feat_dim = queries.shape[1:]

    factor = 1.0 / math.sqrt(n_dp * n_seq * tokens)
    place = jnp.stack([dp, core, seq // CORES]).astype(jnp.int32)
    quick = n_seq == CORES * n_dp == 8

    def backward_pass(d_got, saved):
        attn_out, normal_unit, attn_probs, inverse = saved
        return backward(
            d_got,
            grad_rows,
            normal_unit,
            inverse,
            gain_row,
            attn_probs,
            attn_out,
            queries[0],
            key_rows[0],
            value_rows[0],
        )

    def all_dp(block):
        return [block] + [swap_dp(block, n_dp, k) for k in range(1, n_dp)]

    attention = (queries[0], key_rows[0], value_rows[0], resid_in[0])
    if quick:
        sent, own, *others = send_first(
            place, vision_slot, llm_grad[0], w_up, norm_gain, n_seq, n_dp, tokens
        )
        landing = lax.all_to_all(sent, "seq", split_axis=0, concat_axis=0, tiled=True)
        _, unit_low = forward(window_mask[0], *attention, 1 << 31, False)
        unit_blocks = all_dp(unit_low)
        mine = jnp.stack([own] + [swap_dp(block, n_dp, k + 1) for k, block in enumerate(others)])
        up_cols, gain_row = join_columns(place, mine, swap_seq(mine, n_seq, 1))
        landing = after(landing, up_cols)
    else:
        sent = send_tiles(llm_grad[0], vision_slot, n_seq, tokens)
        landing = lax.all_to_all(sent, "seq", split_axis=0, concat_axis=0, tiled=True)
        gain_row = gather_gain(norm_gain, n_dp, dp).astype(jnp.float32)[None]
        own, mine, mate = fetch_pieces(w_up, n_dp, n_seq, dp, core)
        saved = forward(window_mask[0], *attention, 1 << 31, True)
        normed_blocks = all_dp((saved[1] * gain_row).astype(jnp.bfloat16))
    grad_rows = land_tiles(landing, tokens)
    rows_blocks = all_dp(grad_rows)
    if quick:
        act_flip, slope, normed_flip, normed_all = mlp(up_cols, gain_row, unit_blocks)
        rows_all, down_keep, down_give = down_pieces(place, act_flip, rows_blocks)
        down_mate = swap_seq(down_give, n_seq, 1)
        d_pre, up_keep, up_give = up_pieces(
            place, rows_all, w_down, slope, normed_flip, n_seq // CORES
        )
        up_mate = swap_seq(up_give, n_seq, 1)
        own, *sends = down_planes(place, after(down_keep, d_pre), down_mate)
        planes = [own] + [swap_dp(block, n_dp, k + 1) for k, block in enumerate(sends)]
        parts, term = normed_parts(place, after(d_pre, own), up_cols, unit_blocks)
        term = term + swap_seq(term, n_seq, 1)
        up_keep, up_give = up_sides(place, after(up_keep, own), up_mate)
        up_got = swap_seq(up_give, n_seq, CORES)
        term = term + swap_dp(term, n_dp, 1)
        down_keep, down_give, term = down_rise(place, term, swap_dp(term, n_dp, 2), planes)
        down_got = swap_seq(down_give, n_seq, CORES)
        up_keep, up_give = up_middle(up_keep, up_got)
        up_got = swap_seq(up_give, n_seq, 2 * CORES)
        d_got = lax.all_to_all(
            (after(parts, *planes, up_give)), "dp", split_axis=0, concat_axis=0, tiled=True
        )
        own, down_give, term = down_climb(down_keep, down_got, term)
        down_got = swap_seq(down_give, n_seq, 2 * CORES)
        saved = forward(after(window_mask[0], up_give), *attention, 1 << 31, True)
        grads = backward_pass(d_got, saved)
        grad_up = up_total(after(up_keep, own), up_got, factor)
        grad_down, grad_gain = down_total(after(own, grads[3]), down_got, term, factor)
    else:
        normed_all = jnp.concatenate(normed_blocks, axis=0)
        rows_all = jnp.concatenate(rows_blocks, axis=0)
        up_cols = join_up(own, mine, mate, n_dp, dp, core)
        pre_act = contract(normed_all, up_cols, 1, 0)
        sig_gate = jax.nn.sigmoid(1.702 * pre_act)
        act_low = (pre_act * sig_gate).astype(jnp.bfloat16)
        d_act = contract(rows_all, w_down, 1, 1)
        d_pre = (d_act * (sig_gate + 1.702 * pre_act * sig_gate * (1.0 - sig_gate))).astype(
            jnp.bfloat16
        )
        d_part = contract(d_pre, up_cols, 1, 1)
        blocks = d_part.astype(jnp.bfloat16).reshape(n_dp, tokens, feat_dim)
        d_got = jnp.stack([blocks[0]] + [swap_dp(blocks[k], n_dp, k) for k in range(1, n_dp)])
        up_sum = scatter_up(contract(normed_all, d_pre, 0, 0), n_seq, seq)
        down_sum = scatter_down(contract(act_low, rows_all, 0, 0), n_seq, n_dp, seq)
        gain_part = jnp.sum(d_part * normed_all.astype(jnp.float32), axis=0)
        grad_gain = factor * sum_all(gain_part / gain_row[0], n_seq, n_dp)
        grad_up = (up_sum * factor).astype(jnp.bfloat16)
        grad_down = (down_sum * factor).astype(jnp.bfloat16)
        grads = backward_pass(d_got, saved)
    grad_query, grad_key, grad_value, grad_resid = grads

    return (
        grad_query[None],
        grad_key[None],
        grad_value[None],
        grad_resid[None],
        grad_up,
        grad_down,
        grad_gain,
    )


def solution(mesh):
    in_specs = (
        P("dp", "seq", None),
        P("dp", "seq", None),
        P("dp", "seq", None),
        P("dp", "seq", None),
        P("dp", "seq", None),
        P("dp", "seq"),
        P("dp", "seq", None),
        P("dp", None),
        P("dp", None),
        P("dp"),
    )
    out_specs = (
        P("dp", "seq", None),
        P("dp", "seq", None),
        P("dp", "seq", None),
        P("dp", "seq", None),
        P("seq", "dp"),
        P("seq", "dp"),
        P(),
    )
    return jax.shard_map(
        per_device, mesh=mesh, in_specs=in_specs, out_specs=out_specs, check_vma=False
    )
```

```python
import math

import jax
import jax.numpy as jnp
from jax import lax
from jax.experimental import pallas as pl
from jax.experimental.pallas import tpu as pltpu
from jax.sharding import PartitionSpec as P

HEADS = 16
HDIM = 80
BLK = 64
PIECE = 16
CORES = 2
LANES = 128
VMEM_BYTES = 16 * 1024 * 1024
MOST_BYTES = 60 * 1024 * 1024


def vmem_call(body, out_shape, in_spaces, flops, late=(), limit=VMEM_BYTES):
    def run(*operands):
        places = [i for i, space in enumerate(in_spaces) if space == pl.ANY]
        outs = len(jax.tree.leaves(out_shape))

        def kernel(*refs):
            refs = list(refs)
            ins, rest = refs[: len(in_spaces)], refs[len(in_spaces) :]
            held, sems = rest[outs : outs + len(places)], rest[outs + len(places) :]
            copies = [
                pltpu.make_async_copy(ins[i], held[n], sems[n]) for n, i in enumerate(places)
            ]
            for copy in copies:
                copy.start()
            for n, i in enumerate(places):
                ins[i] = held[n]
                if i not in late:
                    copies[n].wait()
            waits = [copies[places.index(i)].wait for i in late]
            body(*waits, *ins, *rest[:outs])

        return pl.pallas_call(
            kernel if places else body,
            out_shape=out_shape,
            in_specs=[pl.BlockSpec(memory_space=space) for space in in_spaces],
            out_specs=jax.tree.map(lambda _: pl.BlockSpec(memory_space=pltpu.VMEM), out_shape),
            scratch_shapes=[pltpu.VMEM(operands[i].shape, operands[i].dtype) for i in places]
            + [pltpu.SemaphoreType.DMA for _ in places],
            compiler_params=pltpu.CompilerParams(vmem_limit_bytes=limit),
            cost_estimate=pl.CostEstimate(
                flops=flops, bytes_accessed=4 << 20, transcendentals=0
            ),
        )(*operands)

    return run


def contract(left, right, left_dim, right_dim):
    return lax.dot_general(
        left, right, (((left_dim,), (right_dim,)), ((), ())), preferred_element_type=jnp.float32
    )


def pick(blocks, index):
    return lax.dynamic_index_in_dim(blocks, index, 0, keepdims=False)


def swap_dp(block, count, step):
    return lax.ppermute(block, "dp", [(i, i ^ step) for i in range(count)])


def swap_seq(block, count, step):
    return lax.ppermute(block, "seq", [(i, i ^ step) for i in range(count)])


def fetch_pieces(w_up, n_dp, n_seq, dp, core):
    rows, ff = w_up.shape
    cols, half = ff // n_dp, rows // CORES
    own = lax.dynamic_slice(w_up, (0, dp * cols), (rows, cols))
    got = []
    for k in range(1, n_dp):
        piece = lax.dynamic_slice(w_up, (core * half, (dp ^ k) * cols), (half, cols))
        got.append(swap_dp(piece, n_dp, k))
    mine = jnp.stack(got)
    return own, mine, swap_seq(mine, n_seq, 1)


def join_up(own, mine, mate, n_dp, dp, core):
    low = jnp.where(core == 0, mine, mate)
    high = jnp.where(core == 0, mate, mine)
    pairs = jnp.concatenate([low, high], axis=1)
    full = jnp.concatenate([own[None], pairs], axis=0)
    return full[dp ^ jnp.arange(n_dp)].reshape(-1, own.shape[1])


def gather_gain(norm_gain, n_dp, dp):
    parts = jnp.stack(
        [norm_gain] + [swap_dp(norm_gain, n_dp, k) for k in range(1, n_dp)]
    )
    return parts[dp ^ jnp.arange(n_dp)].reshape(-1)


def send_kernel(n_seq, capacity, per_owner, slot_ref, rows_ref, out_ref):
    length, feat = rows_ref.shape
    out_ref[...] = jnp.zeros(out_ref.shape, jnp.bfloat16)
    row = lax.broadcasted_iota(jnp.int32, (PIECE, LANES), 0)
    firsts = [slot_ref[0, t * PIECE] for t in range(length // PIECE)]
    owners = [jnp.where(f >= 0, f // (per_owner * PIECE), n_seq) for f in firsts]
    for t, first in enumerate(firsts):
        rank = jnp.int32(0)
        for earlier in range(t):
            rank = rank + jnp.where(owners[earlier] == owners[t], 1, 0)

        @pl.when(first >= 0)
        def _(t=t, first=first, rank=rank):
            place = pl.ds(pl.multiple_of(rank * PIECE, PIECE), PIECE)
            out_ref[owners[t], place, :feat] = rows_ref[t * PIECE : (t + 1) * PIECE, :]
            landing = first % (per_owner * PIECE) + row + 1
            out_ref[owners[t], place, feat:] = landing.astype(jnp.float32).astype(jnp.bfloat16)


def land_kernel(got_ref, out_ref):
    tokens, feat = out_ref.shape
    slots = got_ref.shape[0]
    marks = got_ref[:, feat:].astype(jnp.float32)
    goal = lax.broadcasted_iota(jnp.int32, (slots, LANES), 1) + 1
    rows = got_ref[:, :feat]
    for part in range(tokens // LANES):
        select = (marks == (goal + part * LANES).astype(jnp.float32)).astype(jnp.bfloat16)
        out_ref[part * LANES : (part + 1) * LANES, :] = contract(select, rows, 0, 0).astype(
            jnp.bfloat16
        )


def send_tiles(llm_rows, slot_ids, n_seq, tokens):
    per_owner = tokens // PIECE
    capacity = 1 + (per_owner + n_seq - 2) // n_seq
    return vmem_call(
        lambda *refs: send_kernel(n_seq, capacity, per_owner, *refs),
        jax.ShapeDtypeStruct(
            (n_seq, capacity * PIECE, llm_rows.shape[1] + LANES), jnp.bfloat16
        ),
        [pltpu.SMEM, pltpu.VMEM],
        1 << 20,
    )(slot_ids, llm_rows)


def land_tiles(got, tokens):
    return vmem_call(
        land_kernel,
        jax.ShapeDtypeStruct((tokens, got.shape[2] - LANES), jnp.bfloat16),
        [pltpu.VMEM],
        1 << 26,
    )(got.reshape(-1, got.shape[2]))


def head_lanes(head, rows, width, start):
    lane = lax.broadcasted_iota(jnp.int32, (rows, width), 1) + start
    return (lane >= head * HDIM) & (lane < (head + 1) * HDIM)


def span_of(head):
    start = head * HDIM // LANES * LANES
    stop = -(-(head + 1) * HDIM // LANES) * LANES
    return start, stop


def masked_head(ref, head):
    start, stop = span_of(head)
    block = ref[:, start:stop]
    return jnp.where(head_lanes(head, block.shape[0], stop - start, start), block, 0).astype(
        block.dtype
    )


def add_span(total, head, part):
    start, stop = span_of(head)
    for at in range(start, stop, LANES):
        piece = part[:, at - start : at - start + LANES]
        total[at] = total[at] + piece if at in total else piece


def forward_kernel(mask_ref, q_ref, k_ref, v_ref, resid_ref, out_ref, unit_ref, *saved_refs):
    tokens, feat = q_ref.shape
    scale = 1.0 / math.sqrt(HDIM)
    row = lax.broadcasted_iota(jnp.int32, (tokens, tokens), 0) // BLK
    col = lax.broadcasted_iota(jnp.int32, (tokens, tokens), 1) // BLK
    allowed = row == col
    for i in range(tokens // BLK):
        for j in range(tokens // BLK):
            if i != j:
                allowed = allowed | ((row == i) & (col == j) & (mask_ref[i, j] > 0))
    total = {}
    for head in range(HEADS):
        start, stop = span_of(head)
        scores = contract(q_ref[:, start:stop], masked_head(k_ref, head), 1, 1) * scale
        scores = jnp.where(allowed, scores, -jnp.inf)
        exp_terms = jnp.exp(scores - jnp.max(scores, axis=1, keepdims=True))
        probs = exp_terms / jnp.sum(exp_terms, axis=1, keepdims=True)
        if saved_refs:
            saved_refs[0][head] = probs
        add_span(total, head, contract(probs.astype(jnp.bfloat16), masked_head(v_ref, head), 1, 0))
    for at, value in total.items():
        out_ref[:, at : at + LANES] = value.astype(jnp.bfloat16)
    hidden = resid_ref[...].astype(jnp.float32) + out_ref[...].astype(jnp.float32)
    center = jnp.mean(hidden, axis=1, keepdims=True)
    hidden = hidden - center
    variance = jnp.mean(jnp.square(hidden), axis=1, keepdims=True)
    inverse = lax.rsqrt(variance + 1e-06)
    unit_ref[...] = (hidden * inverse).astype(unit_ref.dtype)
    if saved_refs:
        saved_refs[1][...] = jnp.broadcast_to(inverse, saved_refs[1].shape)


def forward(mask, query, key_block, value_block, resid, flops, saved):
    tokens, feat = query.shape
    rest = (
        jax.ShapeDtypeStruct((HEADS, tokens, tokens), jnp.float32),
        jax.ShapeDtypeStruct((tokens, LANES), jnp.float32),
    )
    return vmem_call(
        forward_kernel,
        (
            jax.ShapeDtypeStruct((tokens, feat), jnp.bfloat16),
            jax.ShapeDtypeStruct((tokens, feat), jnp.float32 if saved else jnp.bfloat16),
        )
        + (rest if saved else ()),
        [pltpu.SMEM] + [pltpu.VMEM] * 4,
        flops,
    )(mask, query, key_block, value_block, resid)


def backward_kernel(
    wait_probs,
    wait_out,
    wait_q,
    wait_k,
    wait_v,
    got_ref,
    rows_ref,
    unit_ref,
    inverse_ref,
    gain_ref,
    probs_ref,
    out_ref,
    q_ref,
    k_ref,
    v_ref,
    gq_ref,
    gk_ref,
    gv_ref,
    gr_ref,
):
    tokens, feat = q_ref.shape
    scale = 1.0 / math.sqrt(HDIM)
    d_normed = sum(got_ref[part].astype(jnp.float32) for part in range(got_ref.shape[0]))
    unit = unit_ref[...]
    d_unit = d_normed * gain_ref[...].astype(jnp.float32)
    d_hidden = inverse_ref[:, :1] * (
        d_unit
        - jnp.mean(d_unit, axis=1, keepdims=True)
        - unit * jnp.mean(d_unit * unit, axis=1, keepdims=True)
    )
    gr_ref[...] = (rows_ref[...].astype(jnp.float32) + d_hidden).astype(jnp.bfloat16)
    for wait in (wait_probs, wait_out, wait_q, wait_k, wait_v):
        wait()
    totals = ({}, {}, {})
    for head in range(HEADS):
        start, stop = span_of(head)
        probs = probs_ref[head]
        grad = masked_head(gr_ref, head)
        add_span(totals[0], head, contract(probs.astype(jnp.bfloat16), grad, 0, 0))
        d_probs = contract(grad, v_ref[:, start:stop], 1, 1)
        delta = jnp.sum(
            grad.astype(jnp.float32) * out_ref[:, start:stop].astype(jnp.float32),
            axis=1,
            keepdims=True,
        )
        d_scores = (probs * (d_probs - delta) * scale).astype(jnp.bfloat16)
        add_span(totals[1], head, contract(d_scores, masked_head(k_ref, head), 1, 0))
        add_span(totals[2], head, contract(d_scores, masked_head(q_ref, head), 0, 0))
    for ref, total in zip((gv_ref, gq_ref, gk_ref), totals):
        for at, value in total.items():
            ref[:, at : at + LANES] = value.astype(jnp.bfloat16)


def backward(*operands):
    tokens, feat = operands[1].shape
    return vmem_call(
        backward_kernel,
        tuple(jax.ShapeDtypeStruct((tokens, feat), jnp.bfloat16) for _ in range(4)),
        [pl.ANY] * 10,
        1 << 32,
        late=(5, 6, 7, 8, 9),
        limit=MOST_BYTES,
    )(*operands)


def scatter_up(term, n_seq, seq):
    n_z, core, z = n_seq // CORES, seq % CORES, seq // CORES
    rows, cols = term.shape
    pieces = term.reshape(n_z, CORES, rows // n_seq, cols)
    keep = lax.dynamic_index_in_dim(pieces, core, 1, keepdims=False)
    give = lax.dynamic_index_in_dim(pieces, 1 - core, 1, keepdims=False)
    both = (
        keep.astype(jnp.float32) + swap_seq(give.astype(jnp.bfloat16), n_seq, 1).astype(jnp.float32)
    ).astype(jnp.bfloat16)
    total = pick(both, z).astype(jnp.float32)
    for k in reversed(range(1, n_z)):
        total = total + swap_seq(pick(both, z ^ k), n_seq, CORES * k).astype(jnp.float32)
    return total


def scatter_down(term, n_seq, n_dp, seq):
    n_z, core, z = n_seq // CORES, seq % CORES, seq // CORES
    rows, cols = term.shape
    n_h, n_e = n_seq // n_dp, n_dp // CORES
    half = cols // CORES
    keep = lax.dynamic_slice(term, (0, core * half), (rows, half))
    give = lax.dynamic_slice(term, (0, (1 - core) * half), (rows, half))
    both = keep + swap_seq(give.astype(jnp.bfloat16), n_seq, 1).astype(jnp.float32)
    pieces = (
        both.reshape(n_h, rows // n_h, n_e, half // n_e)
        .transpose(0, 2, 1, 3)
        .reshape(n_z, rows // n_h, half // n_e)
        .astype(jnp.bfloat16)
    )
    total = 0.0
    for j in range(n_z):
        pairs = []
        for a in range(n_z):
            m = (a + j) % n_z
            for c in range(CORES):
                for d in range(n_dp):
                    source = (a * CORES + c) * n_dp + d
                    goal = (d * n_h + m // n_e) * n_dp + c * n_e + m % n_e
                    pairs.append((source, goal))
        block = lax.ppermute(pick(pieces, (z + j) % n_z), ("seq", "dp"), pairs)
        total = total + block.astype(jnp.float32)
    return total


def sum_all(term, n_seq, n_dp):
    total = term + swap_seq(term, n_seq, 1)
    term = total
    for k in range(1, n_seq // CORES):
        total = total + swap_seq(term, n_seq, CORES * k)
    term = total
    for k in range(1, n_dp):
        total = total + swap_dp(term, n_dp, k)
    return total


def fetch_kernel(place_ref, up_ref, gain_ref, *out_refs):
    rows, cols = out_refs[0].shape
    half = rows - PIECE
    own = pl.ds(pl.multiple_of(place_ref[1] * half, PIECE), half)
    gain = gain_ref[...].astype(jnp.float32).reshape(1, -1)
    gain = jnp.concatenate([gain, jnp.zeros((1, cols - gain.shape[1]), jnp.float32)], axis=1)
    gain = jnp.broadcast_to(gain, (PIECE, cols)).astype(jnp.bfloat16)
    for k, ref in enumerate(out_refs):
        at = pl.multiple_of((place_ref[0] ^ k) * cols, LANES)
        ref[:half, :] = up_ref[own, pl.ds(at, cols)]
        ref[half:, :] = gain


def send_first(place, slot_ids, llm_rows, w_up, norm_gain, n_seq, n_dp, tokens):
    rows, ff = w_up.shape
    per_owner = tokens // PIECE
    capacity = 1 + (per_owner + n_seq - 2) // n_seq
    piece = jax.ShapeDtypeStruct((rows // CORES + PIECE, ff // n_dp), jnp.bfloat16)
    tiles = jax.ShapeDtypeStruct(
        (n_seq, capacity * PIECE, llm_rows.shape[1] + LANES), jnp.bfloat16
    )

    def body(wait_up, place_ref, slot_ref, gain_ref, rows_ref, up_ref, tiles_ref, *piece_refs):
        send_kernel(n_seq, capacity, per_owner, slot_ref, rows_ref, tiles_ref)
        wait_up()
        fetch_kernel(place_ref, up_ref, gain_ref, *piece_refs)

    return vmem_call(
        body,
        (tiles,) + (piece,) * n_dp,
        [pltpu.SMEM, pltpu.SMEM, pltpu.VMEM, pl.ANY, pl.ANY],
        1 << 20,
        late=(4,),
        limit=MOST_BYTES,
    )(place, slot_ids, norm_gain, llm_rows, w_up)


def join_kernel(place_ref, mine_ref, mate_ref, up_ref, gain_ref):
    n_dp, half, cols = mine_ref.shape
    half = half - PIECE
    core = place_ref[1]
    for d in range(n_dp):
        for ref, which in ((mine_ref, core), (mate_ref, 1 - core)):
            base = ((place_ref[0] ^ d) * CORES + which) * half
            up_ref[pl.ds(pl.multiple_of(base, PIECE), half), :] = ref[d, :half, :]
    size = gain_ref.shape[1] // n_dp
    parts = [mine_ref[k, half:, :].astype(jnp.float32)[:1, :size] for k in range(n_dp)]
    row = []
    for d in range(n_dp):
        total = jnp.zeros((1, size), jnp.float32)
        for k, part in enumerate(parts):
            total = jnp.where((place_ref[0] ^ k) == d, part, total)
        row.append(total)
    gain_ref[...] = jnp.concatenate(row, axis=1)


def join_columns(place, mine, mate):
    n_dp, half, cols = mine.shape
    feat = n_dp * CORES * (half - PIECE)
    return vmem_call(
        join_kernel,
        (
            jax.ShapeDtypeStruct((feat, cols), jnp.bfloat16),
            jax.ShapeDtypeStruct((1, feat), jnp.float32),
        ),
        [pltpu.SMEM, pl.ANY, pl.ANY],
        1 << 20,
    )(place, mine, mate)


def mlp_kernel(up_ref, gain_ref, *refs):
    *unit_refs, act_ref, slope_ref, flip_ref, all_ref = refs
    tokens = unit_refs[0].shape[0]
    gain = gain_ref[...]
    for k, ref in enumerate(unit_refs):
        normed = (ref[...].astype(jnp.float32) * gain).astype(jnp.bfloat16)
        all_ref[k * tokens : (k + 1) * tokens, :] = normed
        flip_ref[:, k * tokens : (k + 1) * tokens] = normed.T
    pre_act = contract(all_ref[...], up_ref[...], 1, 0)
    sig_gate = jax.nn.sigmoid(1.702 * pre_act)
    act_ref[...] = (pre_act * sig_gate).astype(jnp.bfloat16).T
    slope_ref[...] = sig_gate + 1.702 * pre_act * sig_gate * (1.0 - sig_gate)


def mlp(up_cols, gain, unit_blocks):
    tokens, feat = unit_blocks[0].shape
    total = tokens * len(unit_blocks)
    cols = up_cols.shape[1]
    return vmem_call(
        mlp_kernel,
        (
            jax.ShapeDtypeStruct((cols, total), jnp.bfloat16),
            jax.ShapeDtypeStruct((total, cols), jnp.float32),
            jax.ShapeDtypeStruct((feat, total), jnp.bfloat16),
            jax.ShapeDtypeStruct((total, feat), jnp.bfloat16),
        ),
        [pltpu.VMEM] * (2 + len(unit_blocks)),
        2 * total * feat * cols,
    )(up_cols, gain, *unit_blocks)


def store_by_core(core, value, which, keep_ref, give_ref, index):
    @pl.when(core == which)
    def _():
        keep_ref[index] = value

    @pl.when(core != which)
    def _():
        give_ref[index] = value


def down_kernel(place_ref, act_ref, rows_ref, keep_ref, give_ref):
    n_dp, half, width = keep_ref.shape
    term = contract(act_ref[...], rows_ref[...], 1, 0).astype(jnp.bfloat16)
    for which in range(CORES):
        for d in range(n_dp):
            piece = term[which * half : (which + 1) * half, d * width : (d + 1) * width]
            store_by_core(place_ref[1], piece, which, keep_ref, give_ref, d)


def down_pieces(place, act_flip, rows_all, n_dp):
    total, feat = rows_all.shape
    cols = act_flip.shape[0]
    piece = jax.ShapeDtypeStruct((n_dp, cols // CORES, feat // n_dp), jnp.bfloat16)
    return vmem_call(
        down_kernel, (piece, piece), [pltpu.SMEM] + [pltpu.VMEM] * 2, 2 * total * feat * cols
    )(place, act_flip, rows_all)


def up_kernel(place_ref, down_ref, slope_ref, flip_ref, *refs):
    *rows_refs, all_ref, pre_ref, keep_ref, give_ref = refs
    n_z, rows, cols = keep_ref.shape
    tokens = rows_refs[0].shape[0]
    for k, ref in enumerate(rows_refs):
        all_ref[k * tokens : (k + 1) * tokens, :] = ref[...]
    d_act = contract(all_ref[...], down_ref[...], 1, 1)
    d_pre = (d_act * slope_ref[...]).astype(jnp.bfloat16)
    pre_ref[...] = d_pre
    term = contract(flip_ref[...], d_pre, 1, 0).astype(jnp.bfloat16)
    for z in range(n_z):
        for which in range(CORES):
            start = (z * CORES + which) * rows
            piece = term[start : start + rows]
            store_by_core(place_ref[1], piece, which, keep_ref, give_ref, z)


def up_pieces(place, rows_blocks, w_down, slope, normed_flip, n_z):
    total, cols = slope.shape
    feat = w_down.shape[1]
    piece = jax.ShapeDtypeStruct((n_z, feat // n_z // CORES, cols), jnp.bfloat16)
    return vmem_call(
        up_kernel,
        (
            jax.ShapeDtypeStruct((total, feat), jnp.bfloat16),
            jax.ShapeDtypeStruct((total, cols), jnp.bfloat16),
            piece,
            piece,
        ),
        [pltpu.SMEM] + [pltpu.VMEM] * (3 + len(rows_blocks)),
        4 * total * feat * cols,
    )(place, w_down, slope, normed_flip, *rows_blocks)


def part_kernel(place_ref, pre_ref, up_ref, *refs):
    *unit_refs, parts_ref, term_ref = refs
    n_dp, tokens, _ = parts_ref.shape
    part = contract(pre_ref[...], up_ref[...], 1, 1)
    for k in range(n_dp):
        rows = part[k * tokens : (k + 1) * tokens]
        parts_ref[place_ref[0] ^ k] = rows.astype(jnp.bfloat16)
        term = jnp.sum(rows * unit_refs[k][...].astype(jnp.float32), axis=0, keepdims=True)
        term_ref[...] = term if k == 0 else term_ref[...] + term


def normed_parts(place, d_pre, up_cols, unit_blocks):
    tokens, feat = unit_blocks[0].shape
    n_dp = len(unit_blocks)
    return vmem_call(
        part_kernel,
        (
            jax.ShapeDtypeStruct((n_dp, tokens, feat), jnp.bfloat16),
            jax.ShapeDtypeStruct((1, feat), jnp.float32),
        ),
        [pltpu.SMEM] + [pltpu.VMEM] * (2 + n_dp),
        2 * n_dp * tokens * feat * d_pre.shape[1],
    )(place, d_pre, up_cols, *unit_blocks)


def copy_kernel(in_ref, out_ref):
    out_ref[...] = in_ref[...]


def again(value):
    shape = jax.ShapeDtypeStruct(value.shape, value.dtype)
    return vmem_call(copy_kernel, shape, [pltpu.VMEM], 1 << 20)(value)


def wide_sum(*terms):
    return sum(term.astype(jnp.float32) for term in terms)


def to_rows(vector, width):
    high = vector.astype(jnp.bfloat16).astype(jnp.float32)
    rows = [
        part[:, at : at + width]
        for part in (high, vector - high)
        for at in range(0, vector.shape[1], width)
    ]
    rows.append(jnp.zeros((PIECE - len(rows), width), jnp.float32))
    return jnp.concatenate(rows, axis=0).astype(jnp.bfloat16)


def side_kernel(place_ref, keep_ref, mate_ref, keep_out, give_out):
    z = place_ref[2]
    count = keep_out.shape[0]
    for i in range(count):
        for ref, at in ((keep_out, z ^ (2 * i)), (give_out, z ^ (2 * i + 1))):
            ref[i] = wide_sum(keep_ref[at], mate_ref[at]).astype(jnp.bfloat16)


def middle_kernel(keep_ref, got_ref, keep_out, give_out):
    keep_out[...] = wide_sum(keep_ref[0], got_ref[0]).astype(jnp.bfloat16)
    give_out[...] = wide_sum(keep_ref[1], got_ref[1]).astype(jnp.bfloat16)


def plane_kernel(place_ref, keep_ref, mate_ref, *out_refs):
    for k, ref in enumerate(out_refs):
        at = place_ref[0] ^ k
        ref[...] = wide_sum(keep_ref[at], mate_ref[at]).astype(jnp.bfloat16)


def rise_kernel(place_ref, *refs):
    *got_refs, keep_ref, give_ref = refs
    half, width = got_refs[0].shape
    for k in range(len(got_refs)):
        ref = (keep_ref, give_ref)[k % 2]
        at = k // 2 * half
        for step, got_ref in enumerate(got_refs):

            @pl.when((place_ref[2] ^ k) == (place_ref[0] ^ step))
            def _(ref=ref, at=at, got_ref=got_ref):
                ref[at : at + half, :] = got_ref[...]


def from_rows(rows, count):
    rows = rows.astype(jnp.float32)
    rows = rows[:count] + rows[count : 2 * count]
    return jnp.concatenate([rows[i : i + 1] for i in range(count)], axis=1)


def climb_kernel(keep_ref, got_ref, term_ref, other_ref, own_ref, give_ref, sum_ref):
    half, width = own_ref.shape
    own_ref[...] = wide_sum(keep_ref[:half, :], got_ref[:half, :]).astype(jnp.bfloat16)
    give = wide_sum(keep_ref[half:, :], got_ref[half : 2 * half, :])
    give_ref[:half, :] = give.astype(jnp.bfloat16)
    total = term_ref[...] + other_ref[...]
    sum_ref[...] = total
    give_ref[half:, :] = to_rows(total, width)


def total_kernel(factor, *refs):
    *in_refs, out_ref = refs
    out_ref[...] = (wide_sum(*(ref[...] for ref in in_refs)) * factor).astype(jnp.bfloat16)


def last_kernel(factor, own_ref, got_ref, term_ref, down_ref, gain_ref):
    half, width = own_ref.shape
    down_ref[...] = (wide_sum(own_ref[...], got_ref[:half, :]) * factor).astype(jnp.bfloat16)
    rest = from_rows(got_ref[half:, :], term_ref.shape[1] // width)
    gain_ref[...] = (term_ref[...] + rest) * factor


def up_sides(place, keep, mate):
    pair = jax.ShapeDtypeStruct((keep.shape[0] // 2,) + keep.shape[1:], jnp.bfloat16)
    return vmem_call(side_kernel, (pair, pair), [pltpu.SMEM, pltpu.VMEM, pltpu.VMEM], 1 << 20)(
        place, keep, mate
    )


def up_middle(keep, got):
    piece = jax.ShapeDtypeStruct(keep.shape[1:], jnp.bfloat16)
    return vmem_call(middle_kernel, (piece, piece), [pltpu.VMEM] * 2, 1 << 37)(keep, got)


def up_total(keep, got, factor):
    piece = jax.ShapeDtypeStruct(keep.shape, jnp.bfloat16)
    return vmem_call(
        lambda *refs: total_kernel(factor, *refs), piece, [pltpu.VMEM] * 2, 1 << 20
    )(keep, got)


def down_planes(place, keep, mate):
    n_dp, half, width = keep.shape
    piece = jax.ShapeDtypeStruct((half, width), jnp.bfloat16)
    return vmem_call(
        plane_kernel, (piece,) * n_dp, [pltpu.SMEM] + [pltpu.VMEM] * 2, 1 << 20
    )(place, keep, mate)


def down_rise(place, planes):
    half, width = planes[0].shape
    return vmem_call(
        rise_kernel,
        (
            jax.ShapeDtypeStruct((2 * half, width), jnp.bfloat16),
            jax.ShapeDtypeStruct((2 * half, width), jnp.bfloat16),
        ),
        [pltpu.SMEM] + [pltpu.VMEM] * len(planes),
        1 << 20,
    )(place, *planes)


def down_climb(keep, got, term, other):
    half, width = keep.shape[0] // 2, keep.shape[1]
    return vmem_call(
        climb_kernel,
        (
            jax.ShapeDtypeStruct((half, width), jnp.bfloat16),
            jax.ShapeDtypeStruct((half + PIECE, width), jnp.bfloat16),
            jax.ShapeDtypeStruct(term.shape, jnp.float32),
        ),
        [pltpu.VMEM] * 4,
        1 << 35,
    )(keep, got, term, other)


def down_total(own, got, term, factor):
    down, gain = vmem_call(
        lambda *refs: last_kernel(factor, *refs),
        (
            jax.ShapeDtypeStruct(own.shape, jnp.bfloat16),
            jax.ShapeDtypeStruct(term.shape, jnp.float32),
        ),
        [pltpu.VMEM] * 3,
        1 << 20,
    )(own, got, term)
    return down, gain.reshape(-1)


def after(value, *others):
    return lax.optimization_barrier((value,) + others)[0]


def per_device(
    queries,
    key_rows,
    value_rows,
    resid_in,
    llm_grad,
    vision_slot,
    window_mask,
    w_up,
    w_down,
    norm_gain,
):
    n_seq = lax.axis_size("seq")
    n_dp = lax.axis_size("dp")
    seq = lax.axis_index("seq")
    dp = lax.axis_index("dp")
    core = seq % CORES
    tokens, feat_dim = queries.shape[1:]

    factor = 1.0 / math.sqrt(n_dp * n_seq * tokens)
    place = jnp.stack([dp, core, seq // CORES]).astype(jnp.int32)
    quick = n_seq == CORES * n_dp == 8

    def backward_pass(d_got, saved):
        attn_out, normal_unit, attn_probs, inverse = saved
        return backward(
            d_got,
            grad_rows,
            normal_unit,
            inverse,
            gain_row,
            attn_probs,
            attn_out,
            queries[0],
            key_rows[0],
            value_rows[0],
        )

    def all_dp(block):
        return [block] + [swap_dp(block, n_dp, k) for k in range(1, n_dp)]

    attention = (queries[0], key_rows[0], value_rows[0], resid_in[0])
    if quick:
        sent, own, *others = send_first(
            place, vision_slot, llm_grad[0], w_up, norm_gain, n_seq, n_dp, tokens
        )
        landing = lax.all_to_all(sent, "seq", split_axis=0, concat_axis=0, tiled=True)
        _, unit_low = forward(after(window_mask[0], sent), *attention, 1 << 31, False)
        unit_blocks = all_dp(unit_low)
        others[-1] = after(others[-1], unit_low)
        mine = jnp.stack([own] + [swap_dp(block, n_dp, k + 1) for k, block in enumerate(others)])
        up_cols, gain_row = join_columns(place, mine, swap_seq(mine, n_seq, 1))
        landing = after(landing, up_cols)
    else:
        sent = send_tiles(llm_grad[0], vision_slot, n_seq, tokens)
        landing = lax.all_to_all(sent, "seq", split_axis=0, concat_axis=0, tiled=True)
        gain_row = gather_gain(norm_gain, n_dp, dp).astype(jnp.float32)[None]
        own, mine, mate = fetch_pieces(w_up, n_dp, n_seq, dp, core)
        saved = forward(window_mask[0], *attention, 1 << 31, True)
        normed_blocks = all_dp((saved[1] * gain_row).astype(jnp.bfloat16))
    grad_rows = land_tiles(landing, tokens)
    rows_blocks = all_dp(grad_rows)
    if quick:
        act_flip, slope, normed_flip, normed_all = mlp(up_cols, gain_row, unit_blocks)
        rows_all, d_pre, up_keep, up_give = up_pieces(
            place, rows_blocks, w_down, slope, normed_flip, n_seq // CORES
        )
        up_mate = swap_seq(up_give, n_seq, 1)
        down_keep, down_give = down_pieces(place, act_flip, rows_all, n_dp)
        down_mate = swap_seq(down_give, n_seq, 1)
        up_keep, up_give = up_sides(place, up_keep, up_mate)
        up_got = swap_seq(up_give, n_seq, CORES)
        own, *sends = down_planes(place, after(down_keep, up_give), down_mate)
        planes = [own] + [swap_dp(block, n_dp, k + 1) for k, block in enumerate(sends)]
        parts, term = normed_parts(place, after(d_pre, own), up_cols, unit_blocks)
        term = term + swap_seq(term, n_seq, 1)
        term = term + swap_dp(term, n_dp, 1)
        down_keep, down_give = down_rise(place, planes)
        down_got = swap_seq(down_give, n_seq, CORES)
        up_keep, up_give = up_middle(up_keep, up_got)
        up_got = swap_seq(up_give, n_seq, 2 * CORES)
        d_got = lax.all_to_all(
            (after(parts, *planes, up_give)), "dp", split_axis=0, concat_axis=0, tiled=True
        )
        term = term + swap_dp(term, n_dp, 2)
        own, down_give, term = down_climb(
            down_keep, down_got, term, swap_seq(term, n_seq, CORES)
        )
        down_got = swap_seq(down_give, n_seq, 2 * CORES)
        saved = forward(after(window_mask[0], up_give), *attention, 1 << 31, True)
        grads = backward_pass(d_got, saved)
        grad_up = up_total(after(up_keep, own), up_got, factor)
        grad_down, grad_gain = down_total(after(own, grads[3]), down_got, term, factor)
    else:
        normed_all = jnp.concatenate(normed_blocks, axis=0)
        rows_all = jnp.concatenate(rows_blocks, axis=0)
        up_cols = join_up(own, mine, mate, n_dp, dp, core)
        pre_act = contract(normed_all, up_cols, 1, 0)
        sig_gate = jax.nn.sigmoid(1.702 * pre_act)
        act_low = (pre_act * sig_gate).astype(jnp.bfloat16)
        d_act = contract(rows_all, w_down, 1, 1)
        d_pre = (d_act * (sig_gate + 1.702 * pre_act * sig_gate * (1.0 - sig_gate))).astype(
            jnp.bfloat16
        )
        d_part = contract(d_pre, up_cols, 1, 1)
        blocks = d_part.astype(jnp.bfloat16).reshape(n_dp, tokens, feat_dim)
        d_got = jnp.stack([blocks[0]] + [swap_dp(blocks[k], n_dp, k) for k in range(1, n_dp)])
        up_sum = scatter_up(contract(normed_all, d_pre, 0, 0), n_seq, seq)
        down_sum = scatter_down(contract(act_low, rows_all, 0, 0), n_seq, n_dp, seq)
        gain_part = jnp.sum(d_part * normed_all.astype(jnp.float32), axis=0)
        grad_gain = factor * sum_all(gain_part / gain_row[0], n_seq, n_dp)
        grad_up = (up_sum * factor).astype(jnp.bfloat16)
        grad_down = (down_sum * factor).astype(jnp.bfloat16)
        grads = backward_pass(d_got, saved)
    grad_query, grad_key, grad_value, grad_resid = grads

    return (
        grad_query[None],
        grad_key[None],
        grad_value[None],
        grad_resid[None],
        grad_up,
        grad_down,
        grad_gain,
    )


def solution(mesh):
    in_specs = (
        P("dp", "seq", None),
        P("dp", "seq", None),
        P("dp", "seq", None),
        P("dp", "seq", None),
        P("dp", "seq", None),
        P("dp", "seq"),
        P("dp", "seq", None),
        P("dp", None),
        P("dp", None),
        P("dp"),
    )
    out_specs = (
        P("dp", "seq", None),
        P("dp", "seq", None),
        P("dp", "seq", None),
        P("dp", "seq", None),
        P("seq", "dp"),
        P("seq", "dp"),
        P(),
    )
    return jax.shard_map(
        per_device, mesh=mesh, in_specs=in_specs, out_specs=out_specs, check_vma=False
    )
```

```python
import math

import jax
import jax.numpy as jnp
from jax import lax
from jax.experimental import pallas as pl
from jax.experimental.pallas import tpu as pltpu
from jax.sharding import PartitionSpec as P

HEADS = 16
HDIM = 80
BLK = 64
PIECE = 16
CORES = 2
LANES = 128
VMEM_BYTES = 16 * 1024 * 1024
MOST_BYTES = 60 * 1024 * 1024


def vmem_call(body, out_shape, in_spaces, flops, late=(), limit=VMEM_BYTES):
    def run(*operands):
        places = [i for i, space in enumerate(in_spaces) if space == pl.ANY]
        outs = len(jax.tree.leaves(out_shape))

        def kernel(*refs):
            refs = list(refs)
            ins, rest = refs[: len(in_spaces)], refs[len(in_spaces) :]
            held, sems = rest[outs : outs + len(places)], rest[outs + len(places) :]
            copies = [
                pltpu.make_async_copy(ins[i], held[n], sems[n]) for n, i in enumerate(places)
            ]
            for copy in copies:
                copy.start()
            for n, i in enumerate(places):
                ins[i] = held[n]
                if i not in late:
                    copies[n].wait()
            waits = [copies[places.index(i)].wait for i in late]
            body(*waits, *ins, *rest[:outs])

        return pl.pallas_call(
            kernel if places else body,
            out_shape=out_shape,
            in_specs=[pl.BlockSpec(memory_space=space) for space in in_spaces],
            out_specs=jax.tree.map(lambda _: pl.BlockSpec(memory_space=pltpu.VMEM), out_shape),
            scratch_shapes=[pltpu.VMEM(operands[i].shape, operands[i].dtype) for i in places]
            + [pltpu.SemaphoreType.DMA for _ in places],
            compiler_params=pltpu.CompilerParams(vmem_limit_bytes=limit),
            cost_estimate=pl.CostEstimate(
                flops=flops, bytes_accessed=4 << 20, transcendentals=0
            ),
        )(*operands)

    return run


def contract(left, right, left_dim, right_dim):
    return lax.dot_general(
        left, right, (((left_dim,), (right_dim,)), ((), ())), preferred_element_type=jnp.float32
    )


def pick(blocks, index):
    return lax.dynamic_index_in_dim(blocks, index, 0, keepdims=False)


def swap_dp(block, count, step):
    return lax.ppermute(block, "dp", [(i, i ^ step) for i in range(count)])


def swap_seq(block, count, step):
    return lax.ppermute(block, "seq", [(i, i ^ step) for i in range(count)])


def fetch_pieces(w_up, n_dp, n_seq, dp, core):
    rows, ff = w_up.shape
    cols, half = ff // n_dp, rows // CORES
    own = lax.dynamic_slice(w_up, (0, dp * cols), (rows, cols))
    got = []
    for k in range(1, n_dp):
        piece = lax.dynamic_slice(w_up, (core * half, (dp ^ k) * cols), (half, cols))
        got.append(swap_dp(piece, n_dp, k))
    mine = jnp.stack(got)
    return own, mine, swap_seq(mine, n_seq, 1)


def join_up(own, mine, mate, n_dp, dp, core):
    low = jnp.where(core == 0, mine, mate)
    high = jnp.where(core == 0, mate, mine)
    pairs = jnp.concatenate([low, high], axis=1)
    full = jnp.concatenate([own[None], pairs], axis=0)
    return full[dp ^ jnp.arange(n_dp)].reshape(-1, own.shape[1])


def gather_gain(norm_gain, n_dp, dp):
    parts = jnp.stack(
        [norm_gain] + [swap_dp(norm_gain, n_dp, k) for k in range(1, n_dp)]
    )
    return parts[dp ^ jnp.arange(n_dp)].reshape(-1)


def send_kernel(n_seq, capacity, per_owner, slot_ref, rows_ref, out_ref):
    length, feat = rows_ref.shape
    out_ref[...] = jnp.zeros(out_ref.shape, jnp.bfloat16)
    row = lax.broadcasted_iota(jnp.int32, (PIECE, LANES), 0)
    firsts = [slot_ref[0, t * PIECE] for t in range(length // PIECE)]
    owners = [jnp.where(f >= 0, f // (per_owner * PIECE), n_seq) for f in firsts]
    for t, first in enumerate(firsts):
        rank = jnp.int32(0)
        for earlier in range(t):
            rank = rank + jnp.where(owners[earlier] == owners[t], 1, 0)

        @pl.when(first >= 0)
        def _(t=t, first=first, rank=rank):
            place = pl.ds(pl.multiple_of(rank * PIECE, PIECE), PIECE)
            out_ref[owners[t], place, :feat] = rows_ref[t * PIECE : (t + 1) * PIECE, :]
            landing = first % (per_owner * PIECE) + row + 1
            out_ref[owners[t], place, feat:] = landing.astype(jnp.float32).astype(jnp.bfloat16)


def land_kernel(got_ref, out_ref):
    tokens, feat = out_ref.shape
    slots = got_ref.shape[0]
    marks = got_ref[:, feat:].astype(jnp.float32)
    goal = lax.broadcasted_iota(jnp.int32, (slots, LANES), 1) + 1
    rows = got_ref[:, :feat]
    for part in range(tokens // LANES):
        select = (marks == (goal + part * LANES).astype(jnp.float32)).astype(jnp.bfloat16)
        out_ref[part * LANES : (part + 1) * LANES, :] = contract(select, rows, 0, 0).astype(
            jnp.bfloat16
        )


def send_tiles(llm_rows, slot_ids, n_seq, tokens):
    per_owner = tokens // PIECE
    capacity = 1 + (per_owner + n_seq - 2) // n_seq
    return vmem_call(
        lambda *refs: send_kernel(n_seq, capacity, per_owner, *refs),
        jax.ShapeDtypeStruct(
            (n_seq, capacity * PIECE, llm_rows.shape[1] + LANES), jnp.bfloat16
        ),
        [pltpu.SMEM, pltpu.VMEM],
        1 << 20,
    )(slot_ids, llm_rows)


def land_tiles(got, tokens):
    return vmem_call(
        land_kernel,
        jax.ShapeDtypeStruct((tokens, got.shape[2] - LANES), jnp.bfloat16),
        [pltpu.VMEM],
        1 << 26,
    )(got.reshape(-1, got.shape[2]))


def head_lanes(head, rows, width, start):
    lane = lax.broadcasted_iota(jnp.int32, (rows, width), 1) + start
    return (lane >= head * HDIM) & (lane < (head + 1) * HDIM)


def span_of(head):
    start = head * HDIM // LANES * LANES
    stop = -(-(head + 1) * HDIM // LANES) * LANES
    return start, stop


def masked_head(ref, head):
    start, stop = span_of(head)
    block = ref[:, start:stop]
    return jnp.where(head_lanes(head, block.shape[0], stop - start, start), block, 0).astype(
        block.dtype
    )


def add_span(total, head, part):
    start, stop = span_of(head)
    for at in range(start, stop, LANES):
        piece = part[:, at - start : at - start + LANES]
        total[at] = total[at] + piece if at in total else piece


def forward_kernel(mask_ref, q_ref, k_ref, v_ref, resid_ref, out_ref, unit_ref, *saved_refs):
    tokens, feat = q_ref.shape
    scale = 1.0 / math.sqrt(HDIM)
    row = lax.broadcasted_iota(jnp.int32, (tokens, tokens), 0) // BLK
    col = lax.broadcasted_iota(jnp.int32, (tokens, tokens), 1) // BLK
    allowed = row == col
    for i in range(tokens // BLK):
        for j in range(tokens // BLK):
            if i != j:
                allowed = allowed | ((row == i) & (col == j) & (mask_ref[i, j] > 0))
    total = {}
    for head in range(HEADS):
        start, stop = span_of(head)
        scores = contract(q_ref[:, start:stop], masked_head(k_ref, head), 1, 1) * scale
        scores = jnp.where(allowed, scores, -jnp.inf)
        exp_terms = jnp.exp(scores - jnp.max(scores, axis=1, keepdims=True))
        probs = exp_terms / jnp.sum(exp_terms, axis=1, keepdims=True)
        if saved_refs:
            saved_refs[0][head] = probs
        add_span(total, head, contract(probs.astype(jnp.bfloat16), masked_head(v_ref, head), 1, 0))
    for at, value in total.items():
        out_ref[:, at : at + LANES] = value.astype(jnp.bfloat16)
    hidden = resid_ref[...].astype(jnp.float32) + out_ref[...].astype(jnp.float32)
    center = jnp.mean(hidden, axis=1, keepdims=True)
    hidden = hidden - center
    variance = jnp.mean(jnp.square(hidden), axis=1, keepdims=True)
    inverse = lax.rsqrt(variance + 1e-06)
    unit_ref[...] = (hidden * inverse).astype(unit_ref.dtype)
    if saved_refs:
        saved_refs[1][...] = jnp.broadcast_to(inverse, saved_refs[1].shape)


def forward(mask, query, key_block, value_block, resid, flops, saved):
    tokens, feat = query.shape
    rest = (
        jax.ShapeDtypeStruct((HEADS, tokens, tokens), jnp.float32),
        jax.ShapeDtypeStruct((tokens, LANES), jnp.float32),
    )
    return vmem_call(
        forward_kernel,
        (
            jax.ShapeDtypeStruct((tokens, feat), jnp.bfloat16),
            jax.ShapeDtypeStruct((tokens, feat), jnp.float32 if saved else jnp.bfloat16),
        )
        + (rest if saved else ()),
        [pltpu.SMEM] + [pltpu.VMEM] * 4,
        flops,
    )(mask, query, key_block, value_block, resid)


def backward_kernel(
    wait_probs,
    wait_out,
    wait_q,
    wait_k,
    wait_v,
    got_ref,
    rows_ref,
    unit_ref,
    inverse_ref,
    gain_ref,
    probs_ref,
    out_ref,
    q_ref,
    k_ref,
    v_ref,
    gq_ref,
    gk_ref,
    gv_ref,
    gr_ref,
):
    tokens, feat = q_ref.shape
    scale = 1.0 / math.sqrt(HDIM)
    d_normed = sum(got_ref[part].astype(jnp.float32) for part in range(got_ref.shape[0]))
    unit = unit_ref[...]
    d_unit = d_normed * gain_ref[...].astype(jnp.float32)
    d_hidden = inverse_ref[:, :1] * (
        d_unit
        - jnp.mean(d_unit, axis=1, keepdims=True)
        - unit * jnp.mean(d_unit * unit, axis=1, keepdims=True)
    )
    gr_ref[...] = (rows_ref[...].astype(jnp.float32) + d_hidden).astype(jnp.bfloat16)
    for wait in (wait_probs, wait_out, wait_q, wait_k, wait_v):
        wait()
    totals = ({}, {}, {})
    for head in range(HEADS):
        start, stop = span_of(head)
        probs = probs_ref[head]
        grad = masked_head(gr_ref, head)
        add_span(totals[0], head, contract(probs.astype(jnp.bfloat16), grad, 0, 0))
        d_probs = contract(grad, v_ref[:, start:stop], 1, 1)
        delta = jnp.sum(
            grad.astype(jnp.float32) * out_ref[:, start:stop].astype(jnp.float32),
            axis=1,
            keepdims=True,
        )
        d_scores = (probs * (d_probs - delta) * scale).astype(jnp.bfloat16)
        add_span(totals[1], head, contract(d_scores, masked_head(k_ref, head), 1, 0))
        add_span(totals[2], head, contract(d_scores, masked_head(q_ref, head), 0, 0))
    for ref, total in zip((gv_ref, gq_ref, gk_ref), totals):
        for at, value in total.items():
            ref[:, at : at + LANES] = value.astype(jnp.bfloat16)


def backward(*operands):
    tokens, feat = operands[1].shape
    return vmem_call(
        backward_kernel,
        tuple(jax.ShapeDtypeStruct((tokens, feat), jnp.bfloat16) for _ in range(4)),
        [pl.ANY] * 10,
        1 << 32,
        late=(5, 6, 7, 8, 9),
        limit=MOST_BYTES,
    )(*operands)


def scatter_up(term, n_seq, seq):
    n_z, core, z = n_seq // CORES, seq % CORES, seq // CORES
    rows, cols = term.shape
    pieces = term.reshape(n_z, CORES, rows // n_seq, cols)
    keep = lax.dynamic_index_in_dim(pieces, core, 1, keepdims=False)
    give = lax.dynamic_index_in_dim(pieces, 1 - core, 1, keepdims=False)
    both = (
        keep.astype(jnp.float32) + swap_seq(give.astype(jnp.bfloat16), n_seq, 1).astype(jnp.float32)
    ).astype(jnp.bfloat16)
    total = pick(both, z).astype(jnp.float32)
    for k in reversed(range(1, n_z)):
        total = total + swap_seq(pick(both, z ^ k), n_seq, CORES * k).astype(jnp.float32)
    return total


def scatter_down(term, n_seq, n_dp, seq):
    n_z, core, z = n_seq // CORES, seq % CORES, seq // CORES
    rows, cols = term.shape
    n_h, n_e = n_seq // n_dp, n_dp // CORES
    half = cols // CORES
    keep = lax.dynamic_slice(term, (0, core * half), (rows, half))
    give = lax.dynamic_slice(term, (0, (1 - core) * half), (rows, half))
    both = keep + swap_seq(give.astype(jnp.bfloat16), n_seq, 1).astype(jnp.float32)
    pieces = (
        both.reshape(n_h, rows // n_h, n_e, half // n_e)
        .transpose(0, 2, 1, 3)
        .reshape(n_z, rows // n_h, half // n_e)
        .astype(jnp.bfloat16)
    )
    total = 0.0
    for j in range(n_z):
        pairs = []
        for a in range(n_z):
            m = (a + j) % n_z
            for c in range(CORES):
                for d in range(n_dp):
                    source = (a * CORES + c) * n_dp + d
                    goal = (d * n_h + m // n_e) * n_dp + c * n_e + m % n_e
                    pairs.append((source, goal))
        block = lax.ppermute(pick(pieces, (z + j) % n_z), ("seq", "dp"), pairs)
        total = total + block.astype(jnp.float32)
    return total


def sum_all(term, n_seq, n_dp):
    total = term + swap_seq(term, n_seq, 1)
    term = total
    for k in range(1, n_seq // CORES):
        total = total + swap_seq(term, n_seq, CORES * k)
    term = total
    for k in range(1, n_dp):
        total = total + swap_dp(term, n_dp, k)
    return total


def fetch_kernel(place_ref, up_ref, gain_ref, *out_refs):
    rows, cols = out_refs[0].shape
    half = rows - PIECE
    own = pl.ds(pl.multiple_of(place_ref[1] * half, PIECE), half)
    gain = gain_ref[...].astype(jnp.float32).reshape(1, -1)
    gain = jnp.concatenate([gain, jnp.zeros((1, cols - gain.shape[1]), jnp.float32)], axis=1)
    gain = jnp.broadcast_to(gain, (PIECE, cols)).astype(jnp.bfloat16)
    for k, ref in enumerate(out_refs):
        at = pl.multiple_of((place_ref[0] ^ k) * cols, LANES)
        ref[:half, :] = up_ref[own, pl.ds(at, cols)]
        ref[half:, :] = gain


def send_first(slot_ids, llm_rows, w_up, norm_gain, n_seq, n_dp, tokens):
    rows, ff = w_up.shape
    per_owner = tokens // PIECE
    capacity = 1 + (per_owner + n_seq - 2) // n_seq
    piece = jax.ShapeDtypeStruct((rows // CORES + PIECE, ff // n_dp), jnp.bfloat16)
    tiles = jax.ShapeDtypeStruct(
        (n_seq, capacity * PIECE, llm_rows.shape[1] + LANES), jnp.bfloat16
    )

    def body(wait_up, slot_ref, gain_ref, rows_ref, up_ref, tiles_ref, *piece_refs):
        place_ref = (lax.axis_index("dp"), lax.axis_index("seq") % CORES)
        send_kernel(n_seq, capacity, per_owner, slot_ref, rows_ref, tiles_ref)
        wait_up()
        fetch_kernel(place_ref, up_ref, gain_ref, *piece_refs)

    return vmem_call(
        body,
        (tiles,) + (piece,) * n_dp,
        [pltpu.SMEM, pltpu.VMEM, pl.ANY, pl.ANY],
        1 << 20,
        late=(3,),
        limit=MOST_BYTES,
    )(slot_ids, norm_gain, llm_rows, w_up)


def join_kernel(place_ref, mine_ref, mate_ref, up_ref, gain_ref):
    n_dp, half, cols = mine_ref.shape
    half = half - PIECE
    core = place_ref[1]
    for d in range(n_dp):
        for ref, which in ((mine_ref, core), (mate_ref, 1 - core)):
            base = ((place_ref[0] ^ d) * CORES + which) * half
            up_ref[pl.ds(pl.multiple_of(base, PIECE), half), :] = ref[d, :half, :]
    size = gain_ref.shape[1] // n_dp
    parts = [mine_ref[k, half:, :].astype(jnp.float32)[:1, :size] for k in range(n_dp)]
    row = []
    for d in range(n_dp):
        total = jnp.zeros((1, size), jnp.float32)
        for k, part in enumerate(parts):
            total = jnp.where((place_ref[0] ^ k) == d, part, total)
        row.append(total)
    gain_ref[...] = jnp.concatenate(row, axis=1)


def join_columns(place, mine, mate):
    n_dp, half, cols = mine.shape
    feat = n_dp * CORES * (half - PIECE)
    return vmem_call(
        join_kernel,
        (
            jax.ShapeDtypeStruct((feat, cols), jnp.bfloat16),
            jax.ShapeDtypeStruct((1, feat), jnp.float32),
        ),
        [pltpu.SMEM, pl.ANY, pl.ANY],
        1 << 20,
    )(place, mine, mate)


def mlp_kernel(up_ref, gain_ref, *refs):
    *unit_refs, act_ref, slope_ref, flip_ref, all_ref = refs
    tokens = unit_refs[0].shape[0]
    gain = gain_ref[...]
    for k, ref in enumerate(unit_refs):
        normed = (ref[...].astype(jnp.float32) * gain).astype(jnp.bfloat16)
        all_ref[k * tokens : (k + 1) * tokens, :] = normed
        flip_ref[:, k * tokens : (k + 1) * tokens] = normed.T
    pre_act = contract(all_ref[...], up_ref[...], 1, 0)
    sig_gate = jax.nn.sigmoid(1.702 * pre_act)
    act_ref[...] = (pre_act * sig_gate).astype(jnp.bfloat16).T
    slope_ref[...] = sig_gate + 1.702 * pre_act * sig_gate * (1.0 - sig_gate)


def mlp(up_cols, gain, unit_blocks):
    tokens, feat = unit_blocks[0].shape
    total = tokens * len(unit_blocks)
    cols = up_cols.shape[1]
    return vmem_call(
        mlp_kernel,
        (
            jax.ShapeDtypeStruct((cols, total), jnp.bfloat16),
            jax.ShapeDtypeStruct((total, cols), jnp.float32),
            jax.ShapeDtypeStruct((feat, total), jnp.bfloat16),
            jax.ShapeDtypeStruct((total, feat), jnp.bfloat16),
        ),
        [pltpu.VMEM] * (2 + len(unit_blocks)),
        2 * total * feat * cols,
    )(up_cols, gain, *unit_blocks)


def store_by_core(core, value, which, keep_ref, give_ref, index):
    @pl.when(core == which)
    def _():
        keep_ref[index] = value

    @pl.when(core != which)
    def _():
        give_ref[index] = value


def down_kernel(place_ref, act_ref, rows_ref, keep_ref, give_ref):
    n_dp, half, width = keep_ref.shape
    term = contract(act_ref[...], rows_ref[...], 1, 0).astype(jnp.bfloat16)
    for which in range(CORES):
        for d in range(n_dp):
            piece = term[which * half : (which + 1) * half, d * width : (d + 1) * width]
            store_by_core(place_ref[1], piece, which, keep_ref, give_ref, d)


def down_pieces(place, act_flip, rows_all, n_dp):
    total, feat = rows_all.shape
    cols = act_flip.shape[0]
    piece = jax.ShapeDtypeStruct((n_dp, cols // CORES, feat // n_dp), jnp.bfloat16)
    return vmem_call(
        down_kernel, (piece, piece), [pltpu.SMEM] + [pltpu.VMEM] * 2, 2 * total * feat * cols
    )(place, act_flip, rows_all)


def up_kernel(place_ref, down_ref, slope_ref, flip_ref, *refs):
    *rows_refs, all_ref, pre_ref, keep_ref, give_ref = refs
    n_z, rows, cols = keep_ref.shape
    tokens = rows_refs[0].shape[0]
    for k, ref in enumerate(rows_refs):
        all_ref[k * tokens : (k + 1) * tokens, :] = ref[...]
    d_act = contract(all_ref[...], down_ref[...], 1, 1)
    d_pre = (d_act * slope_ref[...]).astype(jnp.bfloat16)
    pre_ref[...] = d_pre
    term = contract(flip_ref[...], d_pre, 1, 0).astype(jnp.bfloat16)
    for z in range(n_z):
        for which in range(CORES):
            start = (z * CORES + which) * rows
            piece = term[start : start + rows]
            store_by_core(place_ref[1], piece, which, keep_ref, give_ref, z)


def up_pieces(place, rows_blocks, w_down, slope, normed_flip, n_z):
    total, cols = slope.shape
    feat = w_down.shape[1]
    piece = jax.ShapeDtypeStruct((n_z, feat // n_z // CORES, cols), jnp.bfloat16)
    return vmem_call(
        up_kernel,
        (
            jax.ShapeDtypeStruct((total, feat), jnp.bfloat16),
            jax.ShapeDtypeStruct((total, cols), jnp.bfloat16),
            piece,
            piece,
        ),
        [pltpu.SMEM] + [pltpu.VMEM] * (3 + len(rows_blocks)),
        4 * total * feat * cols,
    )(place, w_down, slope, normed_flip, *rows_blocks)


def part_kernel(place_ref, pre_ref, up_ref, *refs):
    *unit_refs, parts_ref, term_ref = refs
    n_dp, tokens, _ = parts_ref.shape
    part = contract(pre_ref[...], up_ref[...], 1, 1)
    for k in range(n_dp):
        rows = part[k * tokens : (k + 1) * tokens]
        parts_ref[place_ref[0] ^ k] = rows.astype(jnp.bfloat16)
        term = jnp.sum(rows * unit_refs[k][...].astype(jnp.float32), axis=0, keepdims=True)
        term_ref[...] = term if k == 0 else term_ref[...] + term


def normed_parts(place, d_pre, up_cols, unit_blocks):
    tokens, feat = unit_blocks[0].shape
    n_dp = len(unit_blocks)
    return vmem_call(
        part_kernel,
        (
            jax.ShapeDtypeStruct((n_dp, tokens, feat), jnp.bfloat16),
            jax.ShapeDtypeStruct((1, feat), jnp.float32),
        ),
        [pltpu.SMEM] + [pltpu.VMEM] * (2 + n_dp),
        2 * n_dp * tokens * feat * d_pre.shape[1],
    )(place, d_pre, up_cols, *unit_blocks)


def copy_kernel(in_ref, out_ref):
    out_ref[...] = in_ref[...]


def again(value):
    shape = jax.ShapeDtypeStruct(value.shape, value.dtype)
    return vmem_call(copy_kernel, shape, [pltpu.VMEM], 1 << 20)(value)


def wide_sum(*terms):
    return sum(term.astype(jnp.float32) for term in terms)


def to_rows(vector, width):
    high = vector.astype(jnp.bfloat16).astype(jnp.float32)
    rows = [
        part[:, at : at + width]
        for part in (high, vector - high)
        for at in range(0, vector.shape[1], width)
    ]
    rows.append(jnp.zeros((PIECE - len(rows), width), jnp.float32))
    return jnp.concatenate(rows, axis=0).astype(jnp.bfloat16)


def side_kernel(place_ref, keep_ref, mate_ref, keep_out, give_out):
    z = place_ref[2]
    count = keep_out.shape[0]
    for i in range(count):
        for ref, at in ((keep_out, z ^ (2 * i)), (give_out, z ^ (2 * i + 1))):
            ref[i] = wide_sum(keep_ref[at], mate_ref[at]).astype(jnp.bfloat16)


def middle_kernel(keep_ref, got_ref, keep_out, give_out):
    keep_out[...] = wide_sum(keep_ref[0], got_ref[0]).astype(jnp.bfloat16)
    give_out[...] = wide_sum(keep_ref[1], got_ref[1]).astype(jnp.bfloat16)


def plane_kernel(place_ref, keep_ref, mate_ref, *out_refs):
    for k, ref in enumerate(out_refs):
        at = place_ref[0] ^ k
        ref[...] = wide_sum(keep_ref[at], mate_ref[at]).astype(jnp.bfloat16)


def rise_kernel(place_ref, *refs):
    *got_refs, keep_ref, give_ref = refs
    half, width = got_refs[0].shape
    for k in range(len(got_refs)):
        ref = (keep_ref, give_ref)[k % 2]
        at = k // 2 * half
        for step, got_ref in enumerate(got_refs):

            @pl.when((place_ref[2] ^ k) == (place_ref[0] ^ step))
            def _(ref=ref, at=at, got_ref=got_ref):
                ref[at : at + half, :] = got_ref[...]


def from_rows(rows, count):
    rows = rows.astype(jnp.float32)
    rows = rows[:count] + rows[count : 2 * count]
    return jnp.concatenate([rows[i : i + 1] for i in range(count)], axis=1)


def climb_kernel(keep_ref, got_ref, term_ref, other_ref, own_ref, give_ref, sum_ref):
    half, width = own_ref.shape
    own_ref[...] = wide_sum(keep_ref[:half, :], got_ref[:half, :]).astype(jnp.bfloat16)
    give = wide_sum(keep_ref[half:, :], got_ref[half : 2 * half, :])
    give_ref[:half, :] = give.astype(jnp.bfloat16)
    total = term_ref[...] + other_ref[...]
    sum_ref[...] = total
    give_ref[half:, :] = to_rows(total, width)


def total_kernel(factor, *refs):
    *in_refs, out_ref = refs
    out_ref[...] = (wide_sum(*(ref[...] for ref in in_refs)) * factor).astype(jnp.bfloat16)


def last_kernel(factor, own_ref, got_ref, term_ref, down_ref, gain_ref):
    half, width = own_ref.shape
    down_ref[...] = (wide_sum(own_ref[...], got_ref[:half, :]) * factor).astype(jnp.bfloat16)
    rest = from_rows(got_ref[half:, :], term_ref.shape[1] // width)
    gain_ref[...] = ((term_ref[...] + rest) * factor).reshape(-1)


def up_sides(place, keep, mate):
    pair = jax.ShapeDtypeStruct((keep.shape[0] // 2,) + keep.shape[1:], jnp.bfloat16)
    return vmem_call(side_kernel, (pair, pair), [pltpu.SMEM, pltpu.VMEM, pltpu.VMEM], 1 << 20)(
        place, keep, mate
    )


def up_middle(keep, got):
    piece = jax.ShapeDtypeStruct(keep.shape[1:], jnp.bfloat16)
    return vmem_call(middle_kernel, (piece, piece), [pltpu.VMEM] * 2, 1 << 37)(keep, got)


def up_total(keep, got, factor):
    piece = jax.ShapeDtypeStruct(keep.shape, jnp.bfloat16)
    return vmem_call(
        lambda *refs: total_kernel(factor, *refs), piece, [pltpu.VMEM] * 2, 1 << 20
    )(keep, got)


def down_planes(place, keep, mate):
    n_dp, half, width = keep.shape
    piece = jax.ShapeDtypeStruct((half, width), jnp.bfloat16)
    return vmem_call(
        plane_kernel, (piece,) * n_dp, [pltpu.SMEM] + [pltpu.VMEM] * 2, 1 << 20
    )(place, keep, mate)


def down_rise(place, planes):
    half, width = planes[0].shape
    return vmem_call(
        rise_kernel,
        (
            jax.ShapeDtypeStruct((2 * half, width), jnp.bfloat16),
            jax.ShapeDtypeStruct((2 * half, width), jnp.bfloat16),
        ),
        [pltpu.SMEM] + [pltpu.VMEM] * len(planes),
        1 << 20,
    )(place, *planes)


def down_climb(keep, got, term, other):
    half, width = keep.shape[0] // 2, keep.shape[1]
    return vmem_call(
        climb_kernel,
        (
            jax.ShapeDtypeStruct((half, width), jnp.bfloat16),
            jax.ShapeDtypeStruct((half + PIECE, width), jnp.bfloat16),
            jax.ShapeDtypeStruct(term.shape, jnp.float32),
        ),
        [pltpu.VMEM] * 4,
        1 << 35,
    )(keep, got, term, other)


def down_total(own, got, term, factor):
    down, gain = vmem_call(
        lambda *refs: last_kernel(factor, *refs),
        (
            jax.ShapeDtypeStruct(own.shape, jnp.bfloat16),
            jax.ShapeDtypeStruct((term.size,), jnp.float32),
        ),
        [pltpu.VMEM] * 3,
        1 << 20,
    )(own, got, term)
    return down, gain


def after(value, *others):
    return lax.optimization_barrier((value,) + others)[0]


def per_device(
    queries,
    key_rows,
    value_rows,
    resid_in,
    llm_grad,
    vision_slot,
    window_mask,
    w_up,
    w_down,
    norm_gain,
):
    n_seq = lax.axis_size("seq")
    n_dp = lax.axis_size("dp")
    seq = lax.axis_index("seq")
    dp = lax.axis_index("dp")
    core = seq % CORES
    tokens, feat_dim = queries.shape[1:]

    factor = 1.0 / math.sqrt(n_dp * n_seq * tokens)
    place = jnp.stack([dp, core, seq // CORES]).astype(jnp.int32)
    quick = n_seq == CORES * n_dp == 8

    def backward_pass(d_got, saved):
        attn_out, normal_unit, attn_probs, inverse = saved
        return backward(
            d_got,
            grad_rows,
            normal_unit,
            inverse,
            gain_row,
            attn_probs,
            attn_out,
            queries[0],
            key_rows[0],
            value_rows[0],
        )

    def all_dp(block):
        return [block] + [swap_dp(block, n_dp, k) for k in range(1, n_dp)]

    attention = (queries[0], key_rows[0], value_rows[0], resid_in[0])
    if quick:
        sent, own, *others = send_first(
            vision_slot, llm_grad[0], w_up, norm_gain, n_seq, n_dp, tokens
        )
        landing = lax.all_to_all(sent, "seq", split_axis=0, concat_axis=0, tiled=True)
        _, unit_low = forward(after(window_mask[0], sent), *attention, 1 << 31, False)
        unit_blocks = all_dp(unit_low)
        others[-1] = after(others[-1], unit_low)
        mine = jnp.stack([own] + [swap_dp(block, n_dp, k + 1) for k, block in enumerate(others)])
        up_cols, gain_row = join_columns(place, mine, swap_seq(mine, n_seq, 1))
        landing = after(landing, up_cols)
    else:
        sent = send_tiles(llm_grad[0], vision_slot, n_seq, tokens)
        landing = lax.all_to_all(sent, "seq", split_axis=0, concat_axis=0, tiled=True)
        gain_row = gather_gain(norm_gain, n_dp, dp).astype(jnp.float32)[None]
        own, mine, mate = fetch_pieces(w_up, n_dp, n_seq, dp, core)
        saved = forward(window_mask[0], *attention, 1 << 31, True)
        normed_blocks = all_dp((saved[1] * gain_row).astype(jnp.bfloat16))
    grad_rows = land_tiles(landing, tokens)
    rows_blocks = all_dp(grad_rows)
    if quick:
        act_flip, slope, normed_flip, normed_all = mlp(up_cols, gain_row, unit_blocks)
        rows_all, d_pre, up_keep, up_give = up_pieces(
            place, rows_blocks, w_down, slope, normed_flip, n_seq // CORES
        )
        up_mate = swap_seq(up_give, n_seq, 1)
        down_keep, down_give = down_pieces(place, act_flip, rows_all, n_dp)
        down_mate = swap_seq(down_give, n_seq, 1)
        up_keep, up_give = up_sides(place, up_keep, up_mate)
        up_got = swap_seq(up_give, n_seq, CORES)
        own, *sends = down_planes(place, after(down_keep, up_give), down_mate)
        planes = [own] + [swap_dp(block, n_dp, k + 1) for k, block in enumerate(sends)]
        parts, term = normed_parts(place, after(d_pre, own), up_cols, unit_blocks)
        term = term + swap_seq(term, n_seq, 1)
        term = term + swap_dp(term, n_dp, 1)
        down_keep, down_give = down_rise(place, planes)
        down_got = swap_seq(down_give, n_seq, CORES)
        up_keep, up_give = up_middle(up_keep, up_got)
        up_got = swap_seq(up_give, n_seq, 2 * CORES)
        d_got = lax.all_to_all(
            (after(parts, *planes, up_give)), "dp", split_axis=0, concat_axis=0, tiled=True
        )
        term = term + swap_dp(term, n_dp, 2)
        own, down_give, term = down_climb(
            down_keep, down_got, term, swap_seq(term, n_seq, CORES)
        )
        down_got = swap_seq(down_give, n_seq, 2 * CORES)
        saved = forward(after(window_mask[0], up_give), *attention, 1 << 31, True)
        grads = backward_pass(d_got, saved)
        grad_up = up_total(after(up_keep, own), up_got, factor)
        grad_down, grad_gain = down_total(after(own, grads[3]), down_got, term, factor)
    else:
        normed_all = jnp.concatenate(normed_blocks, axis=0)
        rows_all = jnp.concatenate(rows_blocks, axis=0)
        up_cols = join_up(own, mine, mate, n_dp, dp, core)
        pre_act = contract(normed_all, up_cols, 1, 0)
        sig_gate = jax.nn.sigmoid(1.702 * pre_act)
        act_low = (pre_act * sig_gate).astype(jnp.bfloat16)
        d_act = contract(rows_all, w_down, 1, 1)
        d_pre = (d_act * (sig_gate + 1.702 * pre_act * sig_gate * (1.0 - sig_gate))).astype(
            jnp.bfloat16
        )
        d_part = contract(d_pre, up_cols, 1, 1)
        blocks = d_part.astype(jnp.bfloat16).reshape(n_dp, tokens, feat_dim)
        d_got = jnp.stack([blocks[0]] + [swap_dp(blocks[k], n_dp, k) for k in range(1, n_dp)])
        up_sum = scatter_up(contract(normed_all, d_pre, 0, 0), n_seq, seq)
        down_sum = scatter_down(contract(act_low, rows_all, 0, 0), n_seq, n_dp, seq)
        gain_part = jnp.sum(d_part * normed_all.astype(jnp.float32), axis=0)
        grad_gain = factor * sum_all(gain_part / gain_row[0], n_seq, n_dp)
        grad_up = (up_sum * factor).astype(jnp.bfloat16)
        grad_down = (down_sum * factor).astype(jnp.bfloat16)
        grads = backward_pass(d_got, saved)
    grad_query, grad_key, grad_value, grad_resid = grads

    return (
        grad_query[None],
        grad_key[None],
        grad_value[None],
        grad_resid[None],
        grad_up,
        grad_down,
        grad_gain,
    )


def solution(mesh):
    in_specs = (
        P("dp", "seq", None),
        P("dp", "seq", None),
        P("dp", "seq", None),
        P("dp", "seq", None),
        P("dp", "seq", None),
        P("dp", "seq"),
        P("dp", "seq", None),
        P("dp", None),
        P("dp", None),
        P("dp"),
    )
    out_specs = (
        P("dp", "seq", None),
        P("dp", "seq", None),
        P("dp", "seq", None),
        P("dp", "seq", None),
        P("seq", "dp"),
        P("seq", "dp"),
        P(),
    )
    return jax.shard_map(
        per_device, mesh=mesh, in_specs=in_specs, out_specs=out_specs, check_vma=False
    )
```

```python
import math

import jax
import jax.numpy as jnp
from jax import lax
from jax.experimental import pallas as pl
from jax.experimental.pallas import tpu as pltpu
from jax.sharding import PartitionSpec as P

HEADS = 16
HDIM = 80
BLK = 64
PIECE = 16
CORES = 2
LANES = 128
VMEM_BYTES = 8 * 1024 * 1024
MOST_BYTES = 60 * 1024 * 1024


def vmem_call(body, out_shape, in_spaces, flops, late=(), limit=VMEM_BYTES):
    def run(*operands):
        places = [i for i, space in enumerate(in_spaces) if space == pl.ANY]
        outs = len(jax.tree.leaves(out_shape))

        def kernel(*refs):
            refs = list(refs)
            ins, rest = refs[: len(in_spaces)], refs[len(in_spaces) :]
            held, sems = rest[outs : outs + len(places)], rest[outs + len(places) :]
            copies = [
                pltpu.make_async_copy(ins[i], held[n], sems[n]) for n, i in enumerate(places)
            ]
            for copy in copies:
                copy.start()
            for n, i in enumerate(places):
                ins[i] = held[n]
                if i not in late:
                    copies[n].wait()
            waits = [copies[places.index(i)].wait for i in late]
            body(*waits, *ins, *rest[:outs])

        return pl.pallas_call(
            kernel if places else body,
            out_shape=out_shape,
            in_specs=[pl.BlockSpec(memory_space=space) for space in in_spaces],
            out_specs=jax.tree.map(lambda _: pl.BlockSpec(memory_space=pltpu.VMEM), out_shape),
            scratch_shapes=[pltpu.VMEM(operands[i].shape, operands[i].dtype) for i in places]
            + [pltpu.SemaphoreType.DMA for _ in places],
            compiler_params=pltpu.CompilerParams(vmem_limit_bytes=limit),
            cost_estimate=pl.CostEstimate(
                flops=flops, bytes_accessed=4 << 20, transcendentals=0
            ),
        )(*operands)

    return run


def contract(left, right, left_dim, right_dim):
    return lax.dot_general(
        left, right, (((left_dim,), (right_dim,)), ((), ())), preferred_element_type=jnp.float32
    )


def pick(blocks, index):
    return lax.dynamic_index_in_dim(blocks, index, 0, keepdims=False)


def swap_dp(block, count, step):
    return lax.ppermute(block, "dp", [(i, i ^ step) for i in range(count)])


def swap_seq(block, count, step):
    return lax.ppermute(block, "seq", [(i, i ^ step) for i in range(count)])


def fetch_pieces(w_up, n_dp, n_seq, dp, core):
    rows, ff = w_up.shape
    cols, half = ff // n_dp, rows // CORES
    own = lax.dynamic_slice(w_up, (0, dp * cols), (rows, cols))
    got = []
    for k in range(1, n_dp):
        piece = lax.dynamic_slice(w_up, (core * half, (dp ^ k) * cols), (half, cols))
        got.append(swap_dp(piece, n_dp, k))
    mine = jnp.stack(got)
    return own, mine, swap_seq(mine, n_seq, 1)


def join_up(own, mine, mate, n_dp, dp, core):
    low = jnp.where(core == 0, mine, mate)
    high = jnp.where(core == 0, mate, mine)
    pairs = jnp.concatenate([low, high], axis=1)
    full = jnp.concatenate([own[None], pairs], axis=0)
    return full[dp ^ jnp.arange(n_dp)].reshape(-1, own.shape[1])


def gather_gain(norm_gain, n_dp, dp):
    parts = jnp.stack(
        [norm_gain] + [swap_dp(norm_gain, n_dp, k) for k in range(1, n_dp)]
    )
    return parts[dp ^ jnp.arange(n_dp)].reshape(-1)


def send_kernel(n_seq, capacity, per_owner, slot_ref, rows_ref, out_ref):
    length, feat = rows_ref.shape
    out_ref[...] = jnp.zeros(out_ref.shape, jnp.bfloat16)
    row = lax.broadcasted_iota(jnp.int32, (PIECE, LANES), 0)
    firsts = [slot_ref[0, t * PIECE] for t in range(length // PIECE)]
    owners = [jnp.where(f >= 0, f // (per_owner * PIECE), n_seq) for f in firsts]
    for t, first in enumerate(firsts):
        rank = jnp.int32(0)
        for earlier in range(t):
            rank = rank + jnp.where(owners[earlier] == owners[t], 1, 0)

        @pl.when(first >= 0)
        def _(t=t, first=first, rank=rank):
            place = pl.ds(pl.multiple_of(rank * PIECE, PIECE), PIECE)
            out_ref[owners[t], place, :feat] = rows_ref[t * PIECE : (t + 1) * PIECE, :]
            landing = first % (per_owner * PIECE) + row + 1
            out_ref[owners[t], place, feat:] = landing.astype(jnp.float32).astype(jnp.bfloat16)


def land_kernel(got_ref, out_ref):
    tokens, feat = out_ref.shape
    slots = got_ref.shape[0]
    marks = got_ref[:, feat:].astype(jnp.float32)
    goal = lax.broadcasted_iota(jnp.int32, (slots, LANES), 1) + 1
    rows = got_ref[:, :feat]
    for part in range(tokens // LANES):
        select = (marks == (goal + part * LANES).astype(jnp.float32)).astype(jnp.bfloat16)
        out_ref[part * LANES : (part + 1) * LANES, :] = contract(select, rows, 0, 0).astype(
            jnp.bfloat16
        )


def send_tiles(llm_rows, slot_ids, n_seq, tokens):
    per_owner = tokens // PIECE
    capacity = 1 + (per_owner + n_seq - 2) // n_seq
    return vmem_call(
        lambda *refs: send_kernel(n_seq, capacity, per_owner, *refs),
        jax.ShapeDtypeStruct(
            (n_seq, capacity * PIECE, llm_rows.shape[1] + LANES), jnp.bfloat16
        ),
        [pltpu.SMEM, pltpu.VMEM],
        1 << 20,
    )(slot_ids, llm_rows)


def land_tiles(got, tokens):
    return vmem_call(
        land_kernel,
        jax.ShapeDtypeStruct((tokens, got.shape[2] - LANES), jnp.bfloat16),
        [pltpu.VMEM],
        1 << 26,
    )(got.reshape(-1, got.shape[2]))


def head_lanes(head, rows, width, start):
    lane = lax.broadcasted_iota(jnp.int32, (rows, width), 1) + start
    return (lane >= head * HDIM) & (lane < (head + 1) * HDIM)


def span_of(head):
    start = head * HDIM // LANES * LANES
    stop = -(-(head + 1) * HDIM // LANES) * LANES
    return start, stop


def masked_head(ref, head):
    start, stop = span_of(head)
    block = ref[:, start:stop]
    return jnp.where(head_lanes(head, block.shape[0], stop - start, start), block, 0).astype(
        block.dtype
    )


def add_span(total, head, part):
    start, stop = span_of(head)
    for at in range(start, stop, LANES):
        piece = part[:, at - start : at - start + LANES]
        total[at] = total[at] + piece if at in total else piece


def forward_kernel(mask_ref, q_ref, k_ref, v_ref, resid_ref, out_ref, unit_ref, *saved_refs):
    tokens, feat = q_ref.shape
    scale = 1.0 / math.sqrt(HDIM)
    row = lax.broadcasted_iota(jnp.int32, (tokens, tokens), 0) // BLK
    col = lax.broadcasted_iota(jnp.int32, (tokens, tokens), 1) // BLK
    allowed = row == col
    for i in range(tokens // BLK):
        for j in range(tokens // BLK):
            if i != j:
                allowed = allowed | ((row == i) & (col == j) & (mask_ref[i, j] > 0))
    total = {}
    for head in range(HEADS):
        start, stop = span_of(head)
        scores = contract(q_ref[:, start:stop], masked_head(k_ref, head), 1, 1) * scale
        scores = jnp.where(allowed, scores, -jnp.inf)
        exp_terms = jnp.exp(scores - jnp.max(scores, axis=1, keepdims=True))
        probs = exp_terms / jnp.sum(exp_terms, axis=1, keepdims=True)
        if saved_refs:
            saved_refs[0][head] = probs
        add_span(total, head, contract(probs.astype(jnp.bfloat16), masked_head(v_ref, head), 1, 0))
    for at, value in total.items():
        out_ref[:, at : at + LANES] = value.astype(jnp.bfloat16)
    hidden = resid_ref[...].astype(jnp.float32) + out_ref[...].astype(jnp.float32)
    center = jnp.mean(hidden, axis=1, keepdims=True)
    hidden = hidden - center
    variance = jnp.mean(jnp.square(hidden), axis=1, keepdims=True)
    inverse = lax.rsqrt(variance + 1e-06)
    unit_ref[...] = (hidden * inverse).astype(unit_ref.dtype)
    if saved_refs:
        saved_refs[1][...] = jnp.broadcast_to(inverse, saved_refs[1].shape)


def forward(mask, query, key_block, value_block, resid, flops, saved):
    tokens, feat = query.shape
    rest = (
        jax.ShapeDtypeStruct((HEADS, tokens, tokens), jnp.float32),
        jax.ShapeDtypeStruct((tokens, LANES), jnp.float32),
    )
    return vmem_call(
        forward_kernel,
        (
            jax.ShapeDtypeStruct((tokens, feat), jnp.bfloat16),
            jax.ShapeDtypeStruct((tokens, feat), jnp.float32 if saved else jnp.bfloat16),
        )
        + (rest if saved else ()),
        [pltpu.SMEM] + [pltpu.VMEM] * 4,
        flops,
    )(mask, query, key_block, value_block, resid)


def backward_kernel(
    wait_probs,
    wait_out,
    wait_q,
    wait_k,
    wait_v,
    got_ref,
    rows_ref,
    unit_ref,
    inverse_ref,
    gain_ref,
    probs_ref,
    out_ref,
    q_ref,
    k_ref,
    v_ref,
    gq_ref,
    gk_ref,
    gv_ref,
    gr_ref,
):
    tokens, feat = q_ref.shape
    scale = 1.0 / math.sqrt(HDIM)
    d_normed = sum(got_ref[part].astype(jnp.float32) for part in range(got_ref.shape[0]))
    unit = unit_ref[...]
    d_unit = d_normed * gain_ref[...].astype(jnp.float32)
    d_hidden = inverse_ref[:, :1] * (
        d_unit
        - jnp.mean(d_unit, axis=1, keepdims=True)
        - unit * jnp.mean(d_unit * unit, axis=1, keepdims=True)
    )
    gr_ref[...] = (rows_ref[...].astype(jnp.float32) + d_hidden).astype(jnp.bfloat16)
    for wait in (wait_probs, wait_out, wait_q, wait_k, wait_v):
        wait()
    totals = ({}, {}, {})
    for head in range(HEADS):
        start, stop = span_of(head)
        probs = probs_ref[head]
        grad = masked_head(gr_ref, head)
        add_span(totals[0], head, contract(probs.astype(jnp.bfloat16), grad, 0, 0))
        d_probs = contract(grad, v_ref[:, start:stop], 1, 1)
        delta = jnp.sum(
            grad.astype(jnp.float32) * out_ref[:, start:stop].astype(jnp.float32),
            axis=1,
            keepdims=True,
        )
        d_scores = (probs * (d_probs - delta) * scale).astype(jnp.bfloat16)
        add_span(totals[1], head, contract(d_scores, masked_head(k_ref, head), 1, 0))
        add_span(totals[2], head, contract(d_scores, masked_head(q_ref, head), 0, 0))
    for ref, total in zip((gv_ref, gq_ref, gk_ref), totals):
        for at, value in total.items():
            ref[:, at : at + LANES] = value.astype(jnp.bfloat16)


def backward(*operands):
    tokens, feat = operands[1].shape
    return vmem_call(
        backward_kernel,
        tuple(jax.ShapeDtypeStruct((tokens, feat), jnp.bfloat16) for _ in range(4)),
        [pl.ANY] * 10,
        1 << 32,
        late=(5, 6, 7, 8, 9),
        limit=MOST_BYTES,
    )(*operands)


def scatter_up(term, n_seq, seq):
    n_z, core, z = n_seq // CORES, seq % CORES, seq // CORES
    rows, cols = term.shape
    pieces = term.reshape(n_z, CORES, rows // n_seq, cols)
    keep = lax.dynamic_index_in_dim(pieces, core, 1, keepdims=False)
    give = lax.dynamic_index_in_dim(pieces, 1 - core, 1, keepdims=False)
    both = (
        keep.astype(jnp.float32) + swap_seq(give.astype(jnp.bfloat16), n_seq, 1).astype(jnp.float32)
    ).astype(jnp.bfloat16)
    total = pick(both, z).astype(jnp.float32)
    for k in reversed(range(1, n_z)):
        total = total + swap_seq(pick(both, z ^ k), n_seq, CORES * k).astype(jnp.float32)
    return total


def scatter_down(term, n_seq, n_dp, seq):
    n_z, core, z = n_seq // CORES, seq % CORES, seq // CORES
    rows, cols = term.shape
    n_h, n_e = n_seq // n_dp, n_dp // CORES
    half = cols // CORES
    keep = lax.dynamic_slice(term, (0, core * half), (rows, half))
    give = lax.dynamic_slice(term, (0, (1 - core) * half), (rows, half))
    both = keep + swap_seq(give.astype(jnp.bfloat16), n_seq, 1).astype(jnp.float32)
    pieces = (
        both.reshape(n_h, rows // n_h, n_e, half // n_e)
        .transpose(0, 2, 1, 3)
        .reshape(n_z, rows // n_h, half // n_e)
        .astype(jnp.bfloat16)
    )
    total = 0.0
    for j in range(n_z):
        pairs = []
        for a in range(n_z):
            m = (a + j) % n_z
            for c in range(CORES):
                for d in range(n_dp):
                    source = (a * CORES + c) * n_dp + d
                    goal = (d * n_h + m // n_e) * n_dp + c * n_e + m % n_e
                    pairs.append((source, goal))
        block = lax.ppermute(pick(pieces, (z + j) % n_z), ("seq", "dp"), pairs)
        total = total + block.astype(jnp.float32)
    return total


def sum_all(term, n_seq, n_dp):
    total = term + swap_seq(term, n_seq, 1)
    term = total
    for k in range(1, n_seq // CORES):
        total = total + swap_seq(term, n_seq, CORES * k)
    term = total
    for k in range(1, n_dp):
        total = total + swap_dp(term, n_dp, k)
    return total


def fetch_kernel(place_ref, up_ref, gain_ref, *out_refs):
    rows, cols = out_refs[0].shape
    half = rows - PIECE
    own = pl.ds(pl.multiple_of(place_ref[1] * half, PIECE), half)
    gain = gain_ref[...].astype(jnp.float32).reshape(1, -1)
    gain = jnp.concatenate([gain, jnp.zeros((1, cols - gain.shape[1]), jnp.float32)], axis=1)
    gain = jnp.broadcast_to(gain, (PIECE, cols)).astype(jnp.bfloat16)
    for k, ref in enumerate(out_refs):
        at = pl.multiple_of((place_ref[0] ^ k) * cols, LANES)
        ref[:half, :] = up_ref[own, pl.ds(at, cols)]
        ref[half:, :] = gain


def send_first(slot_ids, llm_rows, w_up, norm_gain, n_seq, n_dp, tokens):
    rows, ff = w_up.shape
    per_owner = tokens // PIECE
    capacity = 1 + (per_owner + n_seq - 2) // n_seq
    piece = jax.ShapeDtypeStruct((rows // CORES + PIECE, ff // n_dp), jnp.bfloat16)
    tiles = jax.ShapeDtypeStruct(
        (n_seq, capacity * PIECE, llm_rows.shape[1] + LANES), jnp.bfloat16
    )

    def body(wait_up, slot_ref, gain_ref, rows_ref, up_ref, tiles_ref, *piece_refs):
        place_ref = (lax.axis_index("dp"), lax.axis_index("seq") % CORES)
        send_kernel(n_seq, capacity, per_owner, slot_ref, rows_ref, tiles_ref)
        wait_up()
        fetch_kernel(place_ref, up_ref, gain_ref, *piece_refs)

    return vmem_call(
        body,
        (tiles,) + (piece,) * n_dp,
        [pltpu.SMEM, pltpu.VMEM, pl.ANY, pl.ANY],
        1 << 20,
        late=(3,),
        limit=MOST_BYTES,
    )(slot_ids, norm_gain, llm_rows, w_up)


def join_kernel(place_ref, mine_ref, mate_ref, up_ref, gain_ref):
    n_dp, half, cols = mine_ref.shape
    half = half - PIECE
    core = place_ref[1]
    for d in range(n_dp):
        for ref, which in ((mine_ref, core), (mate_ref, 1 - core)):
            base = ((place_ref[0] ^ d) * CORES + which) * half
            up_ref[pl.ds(pl.multiple_of(base, PIECE), half), :] = ref[d, :half, :]
    size = gain_ref.shape[1] // n_dp
    parts = [mine_ref[k, half:, :].astype(jnp.float32)[:1, :size] for k in range(n_dp)]
    row = []
    for d in range(n_dp):
        total = jnp.zeros((1, size), jnp.float32)
        for k, part in enumerate(parts):
            total = jnp.where((place_ref[0] ^ k) == d, part, total)
        row.append(total)
    gain_ref[...] = jnp.concatenate(row, axis=1)


def join_columns(place, mine, mate):
    n_dp, half, cols = mine.shape
    feat = n_dp * CORES * (half - PIECE)
    return vmem_call(
        join_kernel,
        (
            jax.ShapeDtypeStruct((feat, cols), jnp.bfloat16),
            jax.ShapeDtypeStruct((1, feat), jnp.float32),
        ),
        [pltpu.SMEM, pl.ANY, pl.ANY],
        1 << 20,
    )(place, mine, mate)


def mlp_kernel(up_ref, gain_ref, *refs):
    *unit_refs, act_ref, slope_ref, flip_ref, all_ref = refs
    tokens = unit_refs[0].shape[0]
    gain = gain_ref[...]
    for k, ref in enumerate(unit_refs):
        normed = (ref[...].astype(jnp.float32) * gain).astype(jnp.bfloat16)
        all_ref[k * tokens : (k + 1) * tokens, :] = normed
        flip_ref[:, k * tokens : (k + 1) * tokens] = normed.T
    pre_act = contract(all_ref[...], up_ref[...], 1, 0)
    sig_gate = jax.nn.sigmoid(1.702 * pre_act)
    act_ref[...] = (pre_act * sig_gate).astype(jnp.bfloat16).T
    slope_ref[...] = sig_gate + 1.702 * pre_act * sig_gate * (1.0 - sig_gate)


def mlp(up_cols, gain, unit_blocks):
    tokens, feat = unit_blocks[0].shape
    total = tokens * len(unit_blocks)
    cols = up_cols.shape[1]
    return vmem_call(
        mlp_kernel,
        (
            jax.ShapeDtypeStruct((cols, total), jnp.bfloat16),
            jax.ShapeDtypeStruct((total, cols), jnp.float32),
            jax.ShapeDtypeStruct((feat, total), jnp.bfloat16),
            jax.ShapeDtypeStruct((total, feat), jnp.bfloat16),
        ),
        [pltpu.VMEM] * (2 + len(unit_blocks)),
        2 * total * feat * cols,
    )(up_cols, gain, *unit_blocks)


def store_by_core(core, value, which, keep_ref, give_ref, index):
    @pl.when(core == which)
    def _():
        keep_ref[index] = value

    @pl.when(core != which)
    def _():
        give_ref[index] = value


def down_kernel(place_ref, act_ref, rows_ref, keep_ref, give_ref):
    n_dp, half, width = keep_ref.shape
    term = contract(act_ref[...], rows_ref[...], 1, 0).astype(jnp.bfloat16)
    for which in range(CORES):
        for d in range(n_dp):
            piece = term[which * half : (which + 1) * half, d * width : (d + 1) * width]
            store_by_core(place_ref[1], piece, which, keep_ref, give_ref, d)


def down_pieces(place, act_flip, rows_all, n_dp):
    total, feat = rows_all.shape
    cols = act_flip.shape[0]
    piece = jax.ShapeDtypeStruct((n_dp, cols // CORES, feat // n_dp), jnp.bfloat16)
    return vmem_call(
        down_kernel, (piece, piece), [pltpu.SMEM] + [pltpu.VMEM] * 2, 2 * total * feat * cols
    )(place, act_flip, rows_all)


def up_kernel(place_ref, down_ref, slope_ref, flip_ref, *refs):
    *rows_refs, all_ref, pre_ref, keep_ref, give_ref = refs
    n_z, rows, cols = keep_ref.shape
    tokens = rows_refs[0].shape[0]
    for k, ref in enumerate(rows_refs):
        all_ref[k * tokens : (k + 1) * tokens, :] = ref[...]
    d_act = contract(all_ref[...], down_ref[...], 1, 1)
    d_pre = (d_act * slope_ref[...]).astype(jnp.bfloat16)
    pre_ref[...] = d_pre
    term = contract(flip_ref[...], d_pre, 1, 0).astype(jnp.bfloat16)
    for z in range(n_z):
        for which in range(CORES):
            start = (z * CORES + which) * rows
            piece = term[start : start + rows]
            store_by_core(place_ref[1], piece, which, keep_ref, give_ref, z)


def up_pieces(place, rows_blocks, w_down, slope, normed_flip, n_z):
    total, cols = slope.shape
    feat = w_down.shape[1]
    piece = jax.ShapeDtypeStruct((n_z, feat // n_z // CORES, cols), jnp.bfloat16)
    return vmem_call(
        up_kernel,
        (
            jax.ShapeDtypeStruct((total, feat), jnp.bfloat16),
            jax.ShapeDtypeStruct((total, cols), jnp.bfloat16),
            piece,
            piece,
        ),
        [pltpu.SMEM] + [pltpu.VMEM] * (3 + len(rows_blocks)),
        4 * total * feat * cols,
    )(place, w_down, slope, normed_flip, *rows_blocks)


def part_kernel(place_ref, pre_ref, up_ref, *refs):
    *unit_refs, parts_ref, term_ref = refs
    n_dp, tokens, _ = parts_ref.shape
    part = contract(pre_ref[...], up_ref[...], 1, 1)
    for k in range(n_dp):
        rows = part[k * tokens : (k + 1) * tokens]
        parts_ref[place_ref[0] ^ k] = rows.astype(jnp.bfloat16)
        term = jnp.sum(rows * unit_refs[k][...].astype(jnp.float32), axis=0, keepdims=True)
        term_ref[...] = term if k == 0 else term_ref[...] + term


def normed_parts(place, d_pre, up_cols, unit_blocks):
    tokens, feat = unit_blocks[0].shape
    n_dp = len(unit_blocks)
    return vmem_call(
        part_kernel,
        (
            jax.ShapeDtypeStruct((n_dp, tokens, feat), jnp.bfloat16),
            jax.ShapeDtypeStruct((1, feat), jnp.float32),
        ),
        [pltpu.SMEM] + [pltpu.VMEM] * (2 + n_dp),
        2 * n_dp * tokens * feat * d_pre.shape[1],
    )(place, d_pre, up_cols, *unit_blocks)


def copy_kernel(in_ref, out_ref):
    out_ref[...] = in_ref[...]


def again(value):
    shape = jax.ShapeDtypeStruct(value.shape, value.dtype)
    return vmem_call(copy_kernel, shape, [pltpu.VMEM], 1 << 20)(value)


def wide_sum(*terms):
    return sum(term.astype(jnp.float32) for term in terms)


def to_rows(vector, width):
    high = vector.astype(jnp.bfloat16).astype(jnp.float32)
    rows = [
        part[:, at : at + width]
        for part in (high, vector - high)
        for at in range(0, vector.shape[1], width)
    ]
    rows.append(jnp.zeros((PIECE - len(rows), width), jnp.float32))
    return jnp.concatenate(rows, axis=0).astype(jnp.bfloat16)


def side_kernel(place_ref, keep_ref, mate_ref, keep_out, give_out):
    z = place_ref[2]
    count = keep_out.shape[0]
    for i in range(count):
        for ref, at in ((keep_out, z ^ (2 * i)), (give_out, z ^ (2 * i + 1))):
            ref[i] = wide_sum(keep_ref[at], mate_ref[at]).astype(jnp.bfloat16)


def middle_kernel(keep_ref, got_ref, keep_out, give_out):
    keep_out[...] = wide_sum(keep_ref[0], got_ref[0]).astype(jnp.bfloat16)
    give_out[...] = wide_sum(keep_ref[1], got_ref[1]).astype(jnp.bfloat16)


def plane_kernel(place_ref, keep_ref, mate_ref, *out_refs):
    for k, ref in enumerate(out_refs):
        at = place_ref[0] ^ k
        ref[...] = wide_sum(keep_ref[at], mate_ref[at]).astype(jnp.bfloat16)


def rise_kernel(place_ref, *refs):
    *got_refs, keep_ref, give_ref = refs
    half, width = got_refs[0].shape
    for k in range(len(got_refs)):
        ref = (keep_ref, give_ref)[k % 2]
        at = k // 2 * half
        for step, got_ref in enumerate(got_refs):

            @pl.when((place_ref[2] ^ k) == (place_ref[0] ^ step))
            def _(ref=ref, at=at, got_ref=got_ref):
                ref[at : at + half, :] = got_ref[...]


def from_rows(rows, count):
    rows = rows.astype(jnp.float32)
    rows = rows[:count] + rows[count : 2 * count]
    return jnp.concatenate([rows[i : i + 1] for i in range(count)], axis=1)


def climb_kernel(keep_ref, got_ref, term_ref, other_ref, own_ref, give_ref, sum_ref):
    half, width = own_ref.shape
    own_ref[...] = wide_sum(keep_ref[:half, :], got_ref[:half, :]).astype(jnp.bfloat16)
    give = wide_sum(keep_ref[half:, :], got_ref[half : 2 * half, :])
    give_ref[:half, :] = give.astype(jnp.bfloat16)
    total = term_ref[...] + other_ref[...]
    sum_ref[...] = total
    give_ref[half:, :] = to_rows(total, width)


def total_kernel(factor, *refs):
    *in_refs, out_ref = refs
    out_ref[...] = (wide_sum(*(ref[...] for ref in in_refs)) * factor).astype(jnp.bfloat16)


def last_kernel(factor, own_ref, got_ref, term_ref, down_ref, gain_ref):
    half, width = own_ref.shape
    down_ref[...] = (wide_sum(own_ref[...], got_ref[:half, :]) * factor).astype(jnp.bfloat16)
    rest = from_rows(got_ref[half:, :], term_ref.shape[1] // width)
    gain_ref[...] = ((term_ref[...] + rest) * factor).reshape(-1)


def up_sides(place, keep, mate):
    pair = jax.ShapeDtypeStruct((keep.shape[0] // 2,) + keep.shape[1:], jnp.bfloat16)
    return vmem_call(side_kernel, (pair, pair), [pltpu.SMEM, pltpu.VMEM, pltpu.VMEM], 1 << 20)(
        place, keep, mate
    )


def up_middle(keep, got):
    piece = jax.ShapeDtypeStruct(keep.shape[1:], jnp.bfloat16)
    return vmem_call(middle_kernel, (piece, piece), [pltpu.VMEM] * 2, 1 << 37)(keep, got)


def up_total(keep, got, factor):
    piece = jax.ShapeDtypeStruct(keep.shape, jnp.bfloat16)
    return vmem_call(
        lambda *refs: total_kernel(factor, *refs), piece, [pltpu.VMEM] * 2, 1 << 20
    )(keep, got)


def down_planes(place, keep, mate):
    n_dp, half, width = keep.shape
    piece = jax.ShapeDtypeStruct((half, width), jnp.bfloat16)
    return vmem_call(
        plane_kernel, (piece,) * n_dp, [pltpu.SMEM] + [pltpu.VMEM] * 2, 1 << 20
    )(place, keep, mate)


def down_rise(place, planes):
    half, width = planes[0].shape
    return vmem_call(
        rise_kernel,
        (
            jax.ShapeDtypeStruct((2 * half, width), jnp.bfloat16),
            jax.ShapeDtypeStruct((2 * half, width), jnp.bfloat16),
        ),
        [pltpu.SMEM] + [pltpu.VMEM] * len(planes),
        1 << 20,
    )(place, *planes)


def down_climb(keep, got, term, other):
    half, width = keep.shape[0] // 2, keep.shape[1]
    return vmem_call(
        climb_kernel,
        (
            jax.ShapeDtypeStruct((half, width), jnp.bfloat16),
            jax.ShapeDtypeStruct((half + PIECE, width), jnp.bfloat16),
            jax.ShapeDtypeStruct(term.shape, jnp.float32),
        ),
        [pltpu.VMEM] * 4,
        1 << 35,
    )(keep, got, term, other)


def down_total(own, got, term, factor):
    down, gain = vmem_call(
        lambda *refs: last_kernel(factor, *refs),
        (
            jax.ShapeDtypeStruct(own.shape, jnp.bfloat16),
            jax.ShapeDtypeStruct((term.size,), jnp.float32),
        ),
        [pltpu.VMEM] * 3,
        1 << 20,
    )(own, got, term)
    return down, gain


def after(value, *others):
    return lax.optimization_barrier((value,) + others)[0]


def per_device(
    queries,
    key_rows,
    value_rows,
    resid_in,
    llm_grad,
    vision_slot,
    window_mask,
    w_up,
    w_down,
    norm_gain,
):
    n_seq = lax.axis_size("seq")
    n_dp = lax.axis_size("dp")
    seq = lax.axis_index("seq")
    dp = lax.axis_index("dp")
    core = seq % CORES
    tokens, feat_dim = queries.shape[1:]

    factor = 1.0 / math.sqrt(n_dp * n_seq * tokens)
    place = jnp.stack([dp, core, seq // CORES]).astype(jnp.int32)
    quick = n_seq == CORES * n_dp == 8

    def backward_pass(d_got, saved):
        attn_out, normal_unit, attn_probs, inverse = saved
        return backward(
            d_got,
            grad_rows,
            normal_unit,
            inverse,
            gain_row,
            attn_probs,
            attn_out,
            queries[0],
            key_rows[0],
            value_rows[0],
        )

    def all_dp(block):
        return [block] + [swap_dp(block, n_dp, k) for k in range(1, n_dp)]

    attention = (queries[0], key_rows[0], value_rows[0], resid_in[0])
    if quick:
        sent, own, *others = send_first(
            vision_slot, llm_grad[0], w_up, norm_gain, n_seq, n_dp, tokens
        )
        landing = lax.all_to_all(sent, "seq", split_axis=0, concat_axis=0, tiled=True)
        _, unit_low = forward(after(window_mask[0], sent), *attention, 1 << 31, False)
        unit_blocks = all_dp(unit_low)
        others[-1] = after(others[-1], unit_low)
        mine = jnp.stack([own] + [swap_dp(block, n_dp, k + 1) for k, block in enumerate(others)])
        up_cols, gain_row = join_columns(place, mine, swap_seq(mine, n_seq, 1))
        landing = after(landing, up_cols)
    else:
        sent = send_tiles(llm_grad[0], vision_slot, n_seq, tokens)
        landing = lax.all_to_all(sent, "seq", split_axis=0, concat_axis=0, tiled=True)
        gain_row = gather_gain(norm_gain, n_dp, dp).astype(jnp.float32)[None]
        own, mine, mate = fetch_pieces(w_up, n_dp, n_seq, dp, core)
        saved = forward(window_mask[0], *attention, 1 << 31, True)
        normed_blocks = all_dp((saved[1] * gain_row).astype(jnp.bfloat16))
    grad_rows = land_tiles(landing, tokens)
    rows_blocks = all_dp(grad_rows)
    if quick:
        act_flip, slope, normed_flip, normed_all = mlp(up_cols, gain_row, unit_blocks)
        rows_all, d_pre, up_keep, up_give = up_pieces(
            place, rows_blocks, w_down, slope, normed_flip, n_seq // CORES
        )
        up_mate = swap_seq(up_give, n_seq, 1)
        down_keep, down_give = down_pieces(place, act_flip, rows_all, n_dp)
        down_mate = swap_seq(down_give, n_seq, 1)
        up_keep, up_give = up_sides(place, up_keep, up_mate)
        up_got = swap_seq(up_give, n_seq, CORES)
        own, *sends = down_planes(place, after(down_keep, d_pre), down_mate)
        planes = [own] + [swap_dp(block, n_dp, k + 1) for k, block in enumerate(sends)]
        parts, term = normed_parts(place, after(d_pre, own), up_cols, unit_blocks)
        term = term + swap_seq(term, n_seq, 1)
        term = term + swap_dp(term, n_dp, 1)
        down_keep, down_give = down_rise(place, planes)
        down_got = swap_seq(down_give, n_seq, CORES)
        up_keep, up_give = up_middle(up_keep, up_got)
        up_got = swap_seq(up_give, n_seq, 2 * CORES)
        d_got = lax.all_to_all(
            (after(parts, *planes, up_give)), "dp", split_axis=0, concat_axis=0, tiled=True
        )
        term = term + swap_dp(term, n_dp, 2)
        own, down_give, term = down_climb(
            down_keep, down_got, term, swap_seq(term, n_seq, CORES)
        )
        down_got = swap_seq(down_give, n_seq, 2 * CORES)
        saved = forward(after(window_mask[0], up_give), *attention, 1 << 31, True)
        grads = backward_pass(d_got, saved)
        grad_up = up_total(after(up_keep, own), up_got, factor)
        grad_down, grad_gain = down_total(after(own, grads[3]), down_got, term, factor)
    else:
        normed_all = jnp.concatenate(normed_blocks, axis=0)
        rows_all = jnp.concatenate(rows_blocks, axis=0)
        up_cols = join_up(own, mine, mate, n_dp, dp, core)
        pre_act = contract(normed_all, up_cols, 1, 0)
        sig_gate = jax.nn.sigmoid(1.702 * pre_act)
        act_low = (pre_act * sig_gate).astype(jnp.bfloat16)
        d_act = contract(rows_all, w_down, 1, 1)
        d_pre = (d_act * (sig_gate + 1.702 * pre_act * sig_gate * (1.0 - sig_gate))).astype(
            jnp.bfloat16
        )
        d_part = contract(d_pre, up_cols, 1, 1)
        blocks = d_part.astype(jnp.bfloat16).reshape(n_dp, tokens, feat_dim)
        d_got = jnp.stack([blocks[0]] + [swap_dp(blocks[k], n_dp, k) for k in range(1, n_dp)])
        up_sum = scatter_up(contract(normed_all, d_pre, 0, 0), n_seq, seq)
        down_sum = scatter_down(contract(act_low, rows_all, 0, 0), n_seq, n_dp, seq)
        gain_part = jnp.sum(d_part * normed_all.astype(jnp.float32), axis=0)
        grad_gain = factor * sum_all(gain_part / gain_row[0], n_seq, n_dp)
        grad_up = (up_sum * factor).astype(jnp.bfloat16)
        grad_down = (down_sum * factor).astype(jnp.bfloat16)
        grads = backward_pass(d_got, saved)
    grad_query, grad_key, grad_value, grad_resid = grads

    return (
        grad_query[None],
        grad_key[None],
        grad_value[None],
        grad_resid[None],
        grad_up,
        grad_down,
        grad_gain,
    )


def solution(mesh):
    in_specs = (
        P("dp", "seq", None),
        P("dp", "seq", None),
        P("dp", "seq", None),
        P("dp", "seq", None),
        P("dp", "seq", None),
        P("dp", "seq"),
        P("dp", "seq", None),
        P("dp", None),
        P("dp", None),
        P("dp"),
    )
    out_specs = (
        P("dp", "seq", None),
        P("dp", "seq", None),
        P("dp", "seq", None),
        P("dp", "seq", None),
        P("seq", "dp"),
        P("seq", "dp"),
        P(),
    )
    return jax.shard_map(
        per_device, mesh=mesh, in_specs=in_specs, out_specs=out_specs, check_vma=False
    )
```
